32 devices in a mesh: dp: 4 (over z), feat: 8 (over y, x, core).
Axes of the slice: x: 2, y: 2, z: 4, core: 2. Of those that a mesh axis runs over, the one named last changes fastest.
Arguments:
- earlier: bfloat16 [3, 16384, 2560], P(None, 'feat', 'dp'), may hold values from -6 to 6
- mix_weights: float32 [3], replicated, may hold values from 0.3 to 1
- destinations: int32 [2560], replicated, may hold values from -1 to 2047, as said below
- cotangent: bfloat16 [16384, 2048], P('feat', 'dp'), may hold values from -6 to 6
- right_gate: bfloat16 [128, 128, 128], P('feat'), may hold values from -0.5 to 0.5
- left_gate: bfloat16 [128, 128, 128], P('feat'), may hold values from -0.5 to 0.5
- right_up: bfloat16 [128, 128, 128], P('feat'), may hold values from -0.5 to 0.5
- left_up: bfloat16 [128, 128, 128], P('feat'), may hold values from -0.5 to 0.5
- right_down: bfloat16 [128, 128, 128], P('feat'), may hold values from -0.5 to 0.5
- left_down: bfloat16 [128, 128, 128], P('feat'), may hold values from -0.5 to 0.5
Outputs:
- output: bfloat16 [16384, 2048], P('feat', 'dp')
- mixed_grad: bfloat16 [16384, 2560], P('feat', 'dp')
- grad_right_gate: float32 [128, 128, 128], P('feat', 'dp')
- grad_left_gate: float32 [128, 128, 128], P('feat', 'dp')
- grad_right_up: float32 [128, 128, 128], P('feat', 'dp')
- grad_left_up: float32 [128, 128, 128], P('feat', 'dp')
- grad_right_down: float32 [128, 128, 128], P('feat', 'dp')
- grad_left_down: float32 [128, 128, 128], P('feat', 'dp')
The draws below stay inside these ranges and needn't reach their ends.
Inputs may be any that keep to these rules, and one draw needn't show every extreme that they name: `destinations`: every packed row 0 to 2047 is named by exactly one slot; other slots hold -1. Among the 640 slots of one index of dp, at most 160 name rows of any one index of dp (packed rows of index g are g * 512 to (g + 1) * 512 - 1). In every draw one index of dp fills all its 640 slots, sending exactly 160 rows to every index.
All inputs are finite; a program needn't handle non-finite values.
Results may differ from the reference program's by a relative error of at most 0.0092.
Values may be sent and summed in bfloat16 or wider, within the bound.
No kernel may reach another device: no remote copies, remote signals or barrier semaphores. Data moves between devices by JAX's collectives and lax.ppermute only.
A program may use at most 128 MiB of HBM per device.

```python
import jax
import jax.numpy as jnp
from jax import lax

B = 128
D = 16384
DEPTH = 3
TOK_DEV = 512
TOKENS = 2048
ROWS_ALL = 2560
N_DP = 4


def draw_destinations(key, part):
    groups = N_DP
    tok_rows = TOK_DEV
    cap_rows = 5 * TOK_DEV // (4 * N_DP)
    slot_count = 5 * TOK_DEV // 4
    others = groups - 1
    key_list = jax.random.split(key, 5)
    full_source = jax.random.randint(key_list[0], (), 0, groups)
    remainder = tok_rows - cap_rows
    base_count = remainder // others
    extra_count = remainder % others
    reach_limit = min(base_count - 1, cap_rows - base_count - 1)
    position = jnp.arange(others)
    drawn_counts = base_count + (position < extra_count).astype(jnp.int32)
    pair_count = others // 2
    moves = jax.random.randint(key_list[1], (groups, pair_count), 0, reach_limit + 1)
    pair_index = jnp.minimum(position // 2, pair_count - 1)
    signs = jnp.where(position % 2 == 0, 1, -1)
    paired = position // 2 < pair_count
    counts = drawn_counts[None, :] + jnp.where(paired[None, :], signs[None, :] * moves[:, pair_index], 0)
    shuffles = jax.vmap(lambda sub: jax.random.permutation(sub, others))(jax.random.split(key_list[2], groups))
    sources = (full_source + 1 + shuffles) % groups
    columns = jnp.broadcast_to(jnp.arange(groups)[:, None], (groups, others))
    matrix = jnp.zeros((groups, groups), jnp.int32).at[sources, columns].set(counts.astype(jnp.int32))
    matrix = matrix.at[full_source, :].set(cap_rows)
    live_rows = jnp.sum(matrix, axis=1)
    upper = jnp.cumsum(matrix, axis=1)
    lower = upper - matrix
    earlier_in = jnp.cumsum(matrix, axis=0) - matrix
    scores = jax.random.randint(key_list[3], (groups, slot_count), 0, 1 << 20) * slot_count + jnp.arange(slot_count)[None, :]
    ranks = jnp.argsort(jnp.argsort(scores, axis=1, stable=True), axis=1, stable=True).astype(jnp.int32)
    slot_orders = jax.vmap(lambda sub: jax.random.permutation(sub, tok_rows))(jax.random.split(key_list[4], groups)).astype(jnp.int32)

    def one_source(row_ranks, row_upper, row_lower, row_before, live_count):
        target = jnp.minimum(jnp.sum((row_ranks[:, None] >= row_upper[None, :]).astype(jnp.int32), axis=1), groups - 1)
        local_index = row_ranks - row_lower[target]
        ahead = jnp.clip(row_before[target] + local_index, 0, tok_rows - 1)
        chosen = slot_orders[target, ahead]
        return jnp.where(row_ranks < live_count, target * tok_rows + chosen, -1)
    table = jax.vmap(one_source)(ranks, upper, lower, earlier_in, live_rows)
    return table.reshape(-1).astype(jnp.int32)


def block_scale(rng, dims, cuts, low, high):
    def one(axis_at, shards_of):
        steps = jax.random.uniform(jax.random.fold_in(jax.random.fold_in(rng, 6), axis_at), (shards_of,), jnp.float32, low / len(cuts), high / len(cuts))
        return jnp.repeat(jnp.exp(steps), dims[axis_at] // shards_of).reshape((-1,) + (1,) * (len(dims) - axis_at - 1))

    loudness = one(*cuts[0])
    for cut in cuts[1:]:
        loudness = loudness * one(*cut)
    return loudness


def centred(key, dims, deviation, most, pieces=(), kind=jnp.bfloat16):
    entries = deviation * jax.random.normal(key, dims, jnp.float32)
    if pieces:
        entries = entries * block_scale(key, dims, pieces, -0.22, 0.18)
    return jnp.clip(entries, -most, most).astype(kind)


def setup_inputs(seed: int = 0) -> dict:
    key_of = jax.random.split(jax.random.key(seed), 11)
    return {
        "earlier": centred(key_of[0], (DEPTH, D, ROWS_ALL), 1.0, 6.0, ((1, 8), (2, 4))),
        "mix_weights": jnp.clip(jax.random.uniform(key_of[1], (DEPTH,), jnp.float32, 0.3, 1.0), 0.3, 1.0),
        "destinations": draw_destinations(jax.random.fold_in(key_of[10], 71), 0),
        "cotangent": centred(key_of[3], (D, TOKENS), 1.0, 6.0, ((0, 8), (1, 4))),
        "right_gate": centred(key_of[4], (B, B, B), B ** -0.5, 0.5, ((0, 8),)),
        "left_gate": centred(key_of[5], (B, B, B), B ** -0.5, 0.5, ((0, 8),)),
        "right_up": centred(key_of[6], (B, B, B), B ** -0.5, 0.5, ((0, 8),)),
        "left_up": centred(key_of[7], (B, B, B), B ** -0.5, 0.5, ((0, 8),)),
        "right_down": centred(key_of[8], (B, B, B), B ** -0.5, 0.5, ((0, 8),)),
        "left_down": centred(key_of[9], (B, B, B), B ** -0.5, 0.5, ((0, 8),)),
    }


def right_apply(values, right_factor):
    return jnp.einsum('ijt,ijo->iot', values.astype(jnp.float32), right_factor.astype(jnp.float32)).astype(jnp.bfloat16)

def left_apply(spread, left_factor):
    return jnp.einsum('iot,oip->pot', spread.astype(jnp.float32), left_factor.astype(jnp.float32)).astype(jnp.bfloat16)

def left_back(out_grad, left_factor):
    return jnp.einsum('pot,oip->iot', out_grad.astype(jnp.float32), left_factor.astype(jnp.float32)).astype(jnp.bfloat16)

def right_back(spread_grad, right_factor):
    return jnp.einsum('iot,ijo->ijt', spread_grad.astype(jnp.float32), right_factor.astype(jnp.float32))

def left_grad(spread, out_grad):
    return jnp.einsum('iot,pot->oip', spread.astype(jnp.float32), out_grad.astype(jnp.float32))

def right_grad(values, spread_grad):
    return jnp.einsum('ijt,iot->ijo', values.astype(jnp.float32), spread_grad.astype(jnp.float32))

def gelu_slope(values):
    return jax.vjp(jax.nn.gelu, values)[1](jnp.ones_like(values))[0]

def mixer_block(inputs, out_grads, factors):
    right_gate, left_gate, right_up, left_up, right_down, left_down = factors
    gate_spread = right_apply(inputs, right_gate)
    up_spread = right_apply(inputs, right_up)
    gate_out = left_apply(gate_spread, left_gate)
    up_out = left_apply(up_spread, left_up)
    gate_f = gate_out.astype(jnp.float32)
    up_f = up_out.astype(jnp.float32)
    hidden = (jax.nn.gelu(gate_f) * up_f).astype(jnp.bfloat16)
    down_spread = right_apply(hidden, right_down)
    output = left_apply(down_spread, left_down)
    down_spread_grad = left_back(out_grads, left_down)
    grad_left_down = left_grad(down_spread, out_grads)
    hidden_grad = right_back(down_spread_grad, right_down)
    grad_right_down = right_grad(hidden, down_spread_grad)
    gate_grad = (hidden_grad * up_f * gelu_slope(gate_f)).astype(jnp.bfloat16)
    up_grad = (hidden_grad * jax.nn.gelu(gate_f)).astype(jnp.bfloat16)
    gate_spread_grad = left_back(gate_grad, left_gate)
    up_spread_grad = left_back(up_grad, left_up)
    grad_left_gate = left_grad(gate_spread, gate_grad)
    grad_left_up = left_grad(up_spread, up_grad)
    input_grad = (right_back(gate_spread_grad, right_gate) + right_back(up_spread_grad, right_up)).astype(jnp.bfloat16)
    grad_right_gate = right_grad(inputs, gate_spread_grad)
    grad_right_up = right_grad(inputs, up_spread_grad)
    grads = (grad_right_gate, grad_left_gate, grad_right_up, grad_left_up, grad_right_down, grad_left_down)
    return (output, input_grad, grads)

def reference(earlier, mix_weights, destinations, cotangent, right_gate, left_gate, right_up, left_up, right_down, left_down):
    factors = (right_gate, left_gate, right_up, left_up, right_down, left_down)
    live = destinations >= 0
    source_of = jnp.zeros((TOKENS,), jnp.int32).at[jnp.where(live, destinations, TOKENS).astype(jnp.int32)].set(jnp.arange(ROWS_ALL, dtype=jnp.int32), mode='drop')

    def step(sums_carry, group):
        start = (group * TOK_DEV).astype(jnp.int32)
        picks = lax.dynamic_slice_in_dim(source_of, start, TOK_DEV)
        columns = jnp.take(earlier, picks, axis=2).astype(jnp.float32)
        averaged = jnp.zeros((D, TOK_DEV), jnp.float32)
        for depth_index in range(DEPTH):
            averaged = averaged + mix_weights[depth_index] * columns[depth_index]
        inputs = averaged.astype(jnp.bfloat16).reshape(B, B, TOK_DEV)
        out_grads = lax.dynamic_slice_in_dim(cotangent, start, TOK_DEV, 1).reshape(B, B, TOK_DEV)
        output, input_grad, grads = mixer_block(inputs, out_grads, factors)
        new_sums = tuple((total + piece for total, piece in zip(sums_carry, grads)))
        return (new_sums, (output.reshape(D, TOK_DEV), input_grad.reshape(D, TOK_DEV)))
    zero_sums = tuple((jnp.zeros((B, B, B), jnp.float32) for factor in factors))
    sums_final, (outputs, input_grads) = lax.scan(step, zero_sums, jnp.arange(N_DP, dtype=jnp.int32))
    output = jnp.moveaxis(outputs, 0, 1).reshape(D, TOKENS)
    packed_grad = jnp.moveaxis(input_grads, 0, 1).reshape(D, TOKENS)
    picked = jnp.take(packed_grad, jnp.where(live, destinations, 0).astype(jnp.int32), axis=1)
    mixed_grad = jnp.where(live[None, :], picked, jnp.zeros((), jnp.bfloat16))
    grad_scale = TOKENS ** (-0.5)
    scaled = tuple((total * grad_scale for total in sums_final))
    return (output, mixed_grad, scaled[0], scaled[1], scaled[2], scaled[3], scaled[4], scaled[5])
```

```python
import functools

import jax
import jax.numpy as jnp
from jax import lax
from jax.experimental import pallas as pl
from jax.experimental.pallas import tpu as pltpu
from jax.sharding import PartitionSpec as P

F32 = jnp.float32
BF16 = jnp.bfloat16
VMEM_LIMIT = 48 * 1024 * 1024


def params(steps=1):
    return pltpu.CompilerParams(
        vmem_limit_bytes=VMEM_LIMIT, dimension_semantics=("arbitrary",) * steps
    )


def dot(a, b, over):
    return lax.dot_general(a, b, (over, ((), ())), preferred_element_type=F32)


NN = ((1,), (0,))
NT = ((1,), (1,))
TN = ((0,), (0,))


def routing_kernel(sizes, own_ref, dest_ref, home_ref, back_ref, back_t_ref):
    groups, tok, cap, lanes = sizes
    rows, slots = dest_ref.shape
    own = own_ref[0]
    dest = dest_ref[...]
    group = lax.broadcasted_iota(jnp.int32, (rows, slots), 0)
    if groups & (groups - 1) == 0:
        relative = group ^ own
    else:
        relative = jnp.where(group >= own, group - own, group - own + groups)
    before = lax.broadcasted_iota(jnp.int32, (slots, slots), 0) < lax.broadcasted_iota(
        jnp.int32, (slots, slots), 1
    )
    before = jnp.where(before, 1.0, 0.0).astype(BF16)
    lane = lax.broadcasted_iota(jnp.int32, (lanes, slots), 0)

    def place(members):
        return dot(jnp.where(members, 1.0, 0.0).astype(BF16), before, NN).astype(jnp.int32)

    mine = jnp.sum(jnp.where(group == own, dest, 0), axis=0, keepdims=True)
    local = mine - group * tok
    leaving = (local >= 0) & (local < tok) & (group < groups) & (mine >= 0)
    index = jnp.where(leaving, relative * cap + place(leaving) + 1, 0)
    home = jnp.sum(index, axis=0, keepdims=True) - 1
    home_ref[...] = jnp.where(lane == home, 1.0, 0.0).astype(BF16)
    local = dest - own * tok
    arriving = (local >= 0) & (local < tok) & (dest >= 0)
    index = jnp.where(arriving, relative * cap + place(arriving), -1)
    total = jnp.zeros((lanes, slots), jnp.int32)
    for source in range(groups):
        total = total + jnp.where(
            lane == index[source : source + 1], local[source : source + 1] + 1, 0
        )
    row = jnp.sum(total.astype(F32), axis=1, keepdims=True).astype(jnp.int32) - 1
    taken = lax.broadcasted_iota(jnp.int32, (lanes, tok), 1) == row
    taken = jnp.where(taken, 1.0, 0.0)
    back_ref[...] = taken.astype(BF16)
    back_t_ref[...] = taken.T.astype(BF16)


def routing(destinations, own, groups, tok, cap):
    slots = destinations.shape[0] // groups
    lanes = groups * cap
    rows = -(-groups // 16) * 16
    table = destinations.reshape(groups, slots)
    table = jnp.pad(table, ((0, rows - groups), (0, 0)), constant_values=-1)
    return pl.pallas_call(
        functools.partial(routing_kernel, (groups, tok, cap, lanes)),
        in_specs=[
            pl.BlockSpec(memory_space=pltpu.SMEM),
            pl.BlockSpec(memory_space=pltpu.VMEM),
        ],
        out_specs=[pl.BlockSpec(memory_space=pltpu.VMEM)] * 3,
        out_shape=[
            jax.ShapeDtypeStruct((lanes, slots), BF16),
            jax.ShapeDtypeStruct((lanes, tok), BF16),
            jax.ShapeDtypeStruct((tok, lanes), BF16),
        ],
        compiler_params=pltpu.CompilerParams(vmem_limit_bytes=VMEM_LIMIT),
        name="routing",
    )(own, table)


def mix_kernel(weights_ref, earlier_ref, home_ref, *out_refs):
    total = weights_ref[0] * earlier_ref[0].astype(F32)
    for k in range(1, earlier_ref.shape[0]):
        total = total + weights_ref[k] * earlier_ref[k].astype(F32)
    sent = dot(home_ref[...], total.astype(BF16), NT).astype(BF16)
    cap = out_refs[0].shape[0]
    for k, ref in enumerate(out_refs):
        ref[...] = sent[k * cap : (k + 1) * cap]


def mix_and_sort(earlier, mix_weights, home, groups, width):
    depth, feats, slots = earlier.shape
    lanes = home.shape[0]
    cap = lanes // groups
    step = 2 * width
    return pl.pallas_call(
        mix_kernel,
        grid=(feats // step,),
        in_specs=[
            pl.BlockSpec(memory_space=pltpu.SMEM),
            pl.BlockSpec((depth, step, slots), lambda i: (0, i, 0)),
            pl.BlockSpec((lanes, slots), lambda i: (0, 0)),
        ],
        out_specs=[pl.BlockSpec((cap, step), lambda i: (0, i))] * groups,
        out_shape=[jax.ShapeDtypeStruct((cap, feats), BF16)] * groups,
        compiler_params=params(),
        name="mix_and_sort",
    )(mix_weights, earlier, home)


def exchange_rows(slabs, groups):
    received = [slabs[0]]
    for k in range(1, groups):
        if groups & (groups - 1) == 0:
            pairs = [(i, i ^ k) for i in range(groups)]
        else:
            pairs = [(i, (i + k) % groups) for i in range(groups)]
        received.append(lax.ppermute(slabs[k], "dp", pairs))
    return received


def unsort_kernel(home_ref, *refs):
    in_refs, out_ref = refs[:-1], refs[-1]
    rows = jnp.concatenate([ref[...] for ref in in_refs], axis=0)
    out_ref[...] = dot(rows, home_ref[...], TN).astype(BF16)


def unsort(slabs, home, width):
    lanes, slots = home.shape
    cap, feats = slabs[0].shape
    step = 2 * width
    return pl.pallas_call(
        unsort_kernel,
        grid=(feats // step,),
        in_specs=[pl.BlockSpec((lanes, slots), lambda i: (0, 0))]
        + [pl.BlockSpec((cap, step), lambda i: (0, i))] * len(slabs),
        out_specs=pl.BlockSpec((step, slots), lambda i: (i, 0)),
        out_shape=jax.ShapeDtypeStruct((feats, slots), BF16),
        compiler_params=params(),
        name="unsort",
    )(home, *slabs)


class Plan:
    def __init__(self, peers, held, width, tok):
        self.peers, self.held, self.width, self.tok = peers, held, width, tok
        self.piece = held * held
        self.direct = held % 16 == 0

    def sent_shape(self, parts):
        return jax.ShapeDtypeStruct((self.peers, parts * self.piece, self.tok), BF16)

    def sent_spec(self, parts, step):
        return pl.BlockSpec((self.peers, parts * self.piece, step), lambda t: (0, 0, t))

    def arranged(self, array):
        if self.direct:
            return array
        parts = array.shape[1] // self.piece
        array = array.reshape(self.peers, parts, self.held, self.held, self.tok)
        array = array.transpose(1, 2, 0, 3, 4)
        return array.reshape(parts * self.held, self.width, self.tok)

    def arrived_spec(self, parts, step):
        if self.direct:
            return self.sent_spec(parts, step)
        return pl.BlockSpec((parts * self.held, self.width, step), lambda t: (0, 0, t))

    def block(self, ref, part, b):
        if not self.direct:
            return ref[part * self.held + b]
        base = part * self.piece + b * self.held
        return jnp.concatenate(
            [ref[s, base : base + self.held, :] for s in range(self.peers)], axis=0
        )

    def put(self, scratch, b, value):
        for at in range(scratch.shape[0]):
            scratch[at, pl.ds(b, self.width, stride=self.held), :] = value[
                :, at * 128 : (at + 1) * 128
            ]

    def store(self, out_ref, part, scratch):
        rows = slice(part * self.piece, (part + 1) * self.piece)
        for at in range(scratch.shape[0]):
            out_ref[:, rows, at * 128 : (at + 1) * 128] = (
                scratch[at].reshape(self.peers, self.piece, 128).astype(BF16)
            )


def step_of(tok):
    return 256 if tok % 256 == 0 else 128


def scratch_for(plan, step):
    return pltpu.VMEM((step // 128, plan.width * plan.held, 128), F32)


def whole(array):
    return pl.BlockSpec(array.shape, lambda t: (0,) * array.ndim)


def sum_over_steps(ref, b, value, scale):
    step = pl.program_id(0)

    @pl.when(step == 0)
    def _():
        ref[b] = value * scale

    @pl.when(step > 0)
    def _():
        ref[b] += value * scale


def cotangent_kernel(plan, in_ref, out_ref, scratch):
    for b in range(plan.held):
        plan.put(scratch, b, in_ref[b * plan.width : (b + 1) * plan.width, :].astype(F32))
    plan.store(out_ref, 0, scratch)


def send_cotangent(plan, cotangent):
    step = step_of(plan.tok)
    return pl.pallas_call(
        functools.partial(cotangent_kernel, plan),
        grid=(plan.tok // step,),
        in_specs=[pl.BlockSpec((plan.width * plan.held, step), lambda t: (0, t))],
        out_specs=plan.sent_spec(1, step),
        out_shape=plan.sent_shape(1),
        scratch_shapes=[scratch_for(plan, step)],
        compiler_params=params(),
        name="send_cotangent",
    )(cotangent)


def product_kernel(plan, over, in_ref, factor_ref, out_ref, scratch):
    for b in range(plan.held):
        plan.put(scratch, b, dot(factor_ref[b], plan.block(in_ref, 0, b), over))
    plan.store(out_ref, 0, scratch)


def product(plan, arrived, factor, over, name):
    step = step_of(plan.tok)
    return pl.pallas_call(
        functools.partial(product_kernel, plan, over),
        grid=(plan.tok // step,),
        in_specs=[plan.arrived_spec(1, step), whole(factor)],
        out_specs=plan.sent_spec(1, step),
        out_shape=plan.sent_shape(1),
        scratch_shapes=[scratch_for(plan, step)],
        compiler_params=params(),
        name=name,
    )(arrived, factor)


def product_and_grad_kernel(
    plan, scale, values_first, in_ref, other_ref, factor_ref, out_ref, grad_ref, scratch, sums
):
    for b in range(plan.held):
        values = plan.block(in_ref, 0, b)
        others = plan.block(other_ref, 0, b)
        plan.put(scratch, b, dot(factor_ref[b], values, TN))
        sum_over_steps(sums, b, dot(values, others, NT), scale)
    plan.store(out_ref, 0, scratch)
    grad_ref[...] = sums[...].astype(BF16)


def product_and_grad(plan, arrived, other, factor, scale, name):
    step = step_of(plan.tok)
    return pl.pallas_call(
        functools.partial(product_and_grad_kernel, plan, scale, True),
        grid=(plan.tok // step,),
        in_specs=[plan.arrived_spec(1, step), plan.arrived_spec(1, step), whole(factor)],
        out_specs=[plan.sent_spec(1, step), whole(factor)],
        out_shape=[plan.sent_shape(1), jax.ShapeDtypeStruct(factor.shape, BF16)],
        scratch_shapes=[scratch_for(plan, step), pltpu.VMEM(factor.shape, F32)],
        compiler_params=params(),
        name=name,
    )(arrived, other, factor)


def first_kernel(plan, groups, *refs):
    slab_refs, (back_t_ref, gate_ref, up_ref, packed_ref, out_ref, gates, ups) = (
        refs[:groups],
        refs[groups:],
    )
    step = pl.program_id(0)
    count = gate_ref.shape[0]
    rows = jnp.concatenate([ref[...] for ref in slab_refs], axis=0)
    packed = dot(back_t_ref[...], rows, NN).astype(BF16)
    packed_ref[...] = packed
    for at in range(count):
        values = packed[:, at * plan.width : (at + 1) * plan.width]
        b = step * count + at
        plan.put(gates, b, dot(gate_ref[at], values, ((0,), (1,))))
        plan.put(ups, b, dot(up_ref[at], values, ((0,), (1,))))

    @pl.when(step == pl.num_programs(0) - 1)
    def _():
        plan.store(out_ref, 0, gates)
        plan.store(out_ref, 1, ups)


def first_products(plan, slabs, back_t, right_gate, right_up):
    count = 4
    cap, feats = slabs[0].shape
    width = plan.width
    steps = plan.held // count
    factor_spec = pl.BlockSpec((count,) + right_gate.shape[1:], lambda i: (i, 0, 0))
    return pl.pallas_call(
        functools.partial(first_kernel, plan, len(slabs)),
        grid=(steps,),
        in_specs=[pl.BlockSpec((cap, count * width), lambda i: (0, i))] * len(slabs)
        + [whole(back_t), factor_spec, factor_spec],
        out_specs=[
            pl.BlockSpec((plan.tok, count * width), lambda i: (0, i)),
            pl.BlockSpec(plan.sent_shape(2).shape, lambda i: (0, 0, 0)),
        ],
        out_shape=[jax.ShapeDtypeStruct((plan.tok, feats), BF16), plan.sent_shape(2)],
        scratch_shapes=[scratch_for(plan, plan.tok)] * 2,
        compiler_params=params(),
        name="first_products",
    )(*slabs, back_t, right_gate, right_up)


ROOT = 0.7978845608028654
CUBE = 0.044715


def gelu_and_slope(x):
    square = x * x
    wave = jnp.tanh(ROOT * (x + CUBE * (square * x)))
    half = 0.5 * (1.0 + wave)
    slope = half + 0.5 * x * (1.0 - wave * wave) * (ROOT * (1.0 + 3.0 * CUBE * square))
    return x * half, slope


def middle_kernel(
    plan,
    scale,
    spread_ref,
    hidden_grad_ref,
    gate_ref,
    up_ref,
    hidden_ref,
    out_ref,
    gate_grad_ref,
    up_grad_ref,
    hiddens,
    gates,
    ups,
    gate_sums,
    up_sums,
):
    for b in range(plan.held):
        gate_in = plan.block(spread_ref, 0, b)
        up_in = plan.block(spread_ref, 1, b)
        gate_out = dot(gate_ref[b], gate_in, TN).astype(BF16).astype(F32)
        up_out = dot(up_ref[b], up_in, TN).astype(BF16).astype(F32)
        back = plan.block(hidden_grad_ref, 0, b).astype(F32)
        active, slope = gelu_and_slope(gate_out)
        plan.put(hiddens, b, active * up_out)
        gate_back = (back * up_out * slope).astype(BF16)
        up_back = (back * active).astype(BF16)
        plan.put(gates, b, dot(gate_ref[b], gate_back, NN))
        plan.put(ups, b, dot(up_ref[b], up_back, NN))
        sum_over_steps(gate_sums, b, dot(gate_in, gate_back, NT), scale)
        sum_over_steps(up_sums, b, dot(up_in, up_back, NT), scale)
    plan.store(hidden_ref, 0, hiddens)
    plan.store(out_ref, 0, gates)
    plan.store(out_ref, 1, ups)
    gate_grad_ref[...] = gate_sums[...].astype(BF16)
    up_grad_ref[...] = up_sums[...].astype(BF16)


def middle(plan, spreads, hidden_grad, left_gate, left_up, scale):
    step = step_of(plan.tok)
    grad_shape = jax.ShapeDtypeStruct(left_gate.shape, BF16)
    return pl.pallas_call(
        functools.partial(middle_kernel, plan, scale),
        grid=(plan.tok // step,),
        in_specs=[
            plan.arrived_spec(2, step),
            plan.arrived_spec(1, step),
            whole(left_gate),
            whole(left_up),
        ],
        out_specs=[
            plan.sent_spec(1, step),
            plan.sent_spec(2, step),
            whole(left_gate),
            whole(left_up),
        ],
        out_shape=[plan.sent_shape(1), plan.sent_shape(2), grad_shape, grad_shape],
        scratch_shapes=[scratch_for(plan, step)] * 3 + [pltpu.VMEM(left_gate.shape, F32)] * 2,
        compiler_params=params(),
        name="middle",
    )(spreads, hidden_grad, left_gate, left_up)


def last_kernel(plan, scale, groups, in_ref, packed_ref, back_ref, gate_ref, up_ref, *out_refs):
    slab_refs, (gate_grad_ref, up_grad_ref) = out_refs[:groups], out_refs[groups:]
    count = gate_ref.shape[0]
    width = plan.width
    cap = slab_refs[0].shape[0]
    for at in range(count):
        if plan.direct:
            parts = [
                jnp.concatenate(
                    [
                        in_ref[s, part, at * plan.held : (at + 1) * plan.held, :]
                        for s in range(plan.peers)
                    ],
                    axis=0,
                )
                for part in range(2)
            ]
        else:
            parts = [in_ref[part, at] for part in range(2)]
        gate_back, up_back = parts
        back = dot(gate_ref[at], gate_back, NN) + dot(up_ref[at], up_back, NN)
        columns = slice(at * width, (at + 1) * width)
        sent = dot(back_ref[...], back.astype(BF16), NT).astype(BF16)
        for k, ref in enumerate(slab_refs):
            ref[:, columns] = sent[k * cap : (k + 1) * cap]
        values = packed_ref[:, columns]
        gate_grad_ref[at] = (dot(values, gate_back, ((0,), (1,))) * scale).astype(BF16)
        up_grad_ref[at] = (dot(values, up_back, ((0,), (1,))) * scale).astype(BF16)


def last_products(plan, arrived, packed, back, right_gate, right_up, groups, scale):
    count = 4
    lanes = back.shape[0]
    cap = lanes // groups
    feats = packed.shape[1]
    width = plan.width
    if plan.direct:
        arrived = arrived.reshape(plan.peers, 2, plan.piece, plan.tok)
        arrived_spec = pl.BlockSpec(
            (plan.peers, 2, count * plan.held, plan.tok), lambda i: (0, 0, i, 0)
        )
    else:
        arrived = arrived.reshape(2, plan.held, width, plan.tok)
        arrived_spec = pl.BlockSpec((2, count, width, plan.tok), lambda i: (0, i, 0, 0))
    factor_spec = pl.BlockSpec((count,) + right_gate.shape[1:], lambda i: (i, 0, 0))
    grad_shape = jax.ShapeDtypeStruct(right_gate.shape, BF16)
    outs = pl.pallas_call(
        functools.partial(last_kernel, plan, scale, groups),
        grid=(plan.held // count,),
        in_specs=[
            arrived_spec,
            pl.BlockSpec((plan.tok, count * width), lambda i: (0, i)),
            whole(back),
            factor_spec,
            factor_spec,
        ],
        out_specs=[pl.BlockSpec((cap, count * width), lambda i: (0, i))] * groups
        + [factor_spec] * 2,
        out_shape=[jax.ShapeDtypeStruct((cap, feats), BF16)] * groups + [grad_shape] * 2,
        compiler_params=params(),
        name="last_products",
    )(arrived, packed, back, right_gate, right_up)
    return outs[:groups], outs[groups], outs[groups + 1]


def body(
    earlier,
    mix_weights,
    destinations,
    cotangent,
    right_gate,
    left_gate,
    right_up,
    left_up,
    right_down,
    left_down,
):
    held, width = right_gate.shape[0], right_gate.shape[1]
    feats = earlier.shape[1]
    tok = cotangent.shape[1]
    groups = lax.axis_size("dp")
    peers = lax.axis_size("feat")
    cap = 5 * tok // (4 * groups)
    scale = (tok * groups) ** (-0.5)
    plan = Plan(peers, held, width, tok)

    def swap(array):
        return plan.arranged(
            lax.all_to_all(array, "feat", split_axis=0, concat_axis=0, tiled=True)
        )

    own = lax.axis_index("dp").reshape(1)
    home, back, back_t = routing(destinations, own, groups, tok, cap)
    slabs = exchange_rows(mix_and_sort(earlier, mix_weights, home, groups, width), groups)

    out_grads = swap(send_cotangent(plan, cotangent))
    down_spread_grad = swap(product(plan, out_grads, left_down, NN, "left_back_down"))
    hidden_grad = swap(product(plan, down_spread_grad, right_down, NN, "right_back_down"))

    packed, spreads = first_products(plan, slabs, back_t, right_gate, right_up)
    hidden, spread_grads, grad_left_gate, grad_left_up = middle(
        plan, swap(spreads), hidden_grad, left_gate, left_up, scale
    )
    slabs, grad_right_gate, grad_right_up = last_products(
        plan, swap(spread_grads), packed, back, right_gate, right_up, groups, scale
    )
    slabs = exchange_rows(slabs, groups)
    down_spread, grad_right_down = product_and_grad(
        plan, swap(hidden), down_spread_grad, right_down, scale, "right_down"
    )
    result, grad_left_down = product_and_grad(
        plan, swap(down_spread), out_grads, left_down, scale, "left_down"
    )
    result = lax.all_to_all(result, "feat", split_axis=0, concat_axis=0, tiled=True)
    output = result.reshape(peers, held, held, tok).transpose(1, 0, 2, 3).reshape(feats, tok)
    mixed_grad = unsort(slabs, home, width)

    def total(*grads):
        joined = jnp.concatenate(grads, axis=0)
        summed = lax.psum_scatter(joined, "dp", scatter_dimension=1, tiled=True).astype(F32)
        return jnp.split(summed, len(grads), axis=0)

    grad_left_gate, grad_left_up = total(grad_left_gate, grad_left_up)
    grad_right_gate, grad_right_up = total(grad_right_gate, grad_right_up)
    (grad_right_down,) = total(grad_right_down)
    (grad_left_down,) = total(grad_left_down)
    return (
        output,
        mixed_grad,
        grad_right_gate,
        grad_left_gate,
        grad_right_up,
        grad_left_up,
        grad_right_down,
        grad_left_down,
    )


def solution(mesh):
    return jax.shard_map(
        body,
        mesh=mesh,
        in_specs=(
            P(None, "feat", "dp"),
            P(),
            P(),
            P("feat", "dp"),
            P("feat", None, None),
            P("feat", None, None),
            P("feat", None, None),
            P("feat", None, None),
            P("feat", None, None),
            P("feat", None, None),
        ),
        out_specs=(
            P("feat", "dp"),
            P("feat", "dp"),
            P("feat", "dp", None),
            P("feat", "dp", None),
            P("feat", "dp", None),
            P("feat", "dp", None),
            P("feat", "dp", None),
            P("feat", "dp", None),
        ),
        check_vma=False,
    )
```

```python
import functools
import math

import jax
import jax.numpy as jnp
from jax import lax
from jax.experimental import pallas as pl
from jax.experimental.pallas import tpu as pltpu
from jax.sharding import PartitionSpec as P

F32 = jnp.float32
BF16 = jnp.bfloat16
UNROLL = 16
VMEM_LIMIT = 48 * 1024 * 1024


def params(steps=1):
    return pltpu.CompilerParams(
        vmem_limit_bytes=VMEM_LIMIT, dimension_semantics=("arbitrary",) * steps
    )


def dot(a, b, over):
    return lax.dot_general(a, b, (over, ((), ())), preferred_element_type=F32)


def in_hbm(*arrays):
    return [pltpu.with_memory_space_constraint(array, pltpu.HBM) for array in arrays]


NN = ((1,), (0,))
NT = ((1,), (1,))
TN = ((0,), (0,))


def routing_kernel(sizes, own_ref, dest_ref, home_ref, back_ref, back_t_ref):
    groups, tok, cap, lanes = sizes
    rows, slots = dest_ref.shape
    own = own_ref[0]
    dest = dest_ref[...]
    group = lax.broadcasted_iota(jnp.int32, (rows, slots), 0)
    if groups & (groups - 1) == 0:
        relative = group ^ own
    else:
        relative = jnp.where(group >= own, group - own, group - own + groups)
    before = lax.broadcasted_iota(jnp.int32, (slots, slots), 0) < lax.broadcasted_iota(
        jnp.int32, (slots, slots), 1
    )
    before = jnp.where(before, 1.0, 0.0).astype(BF16)
    lane = lax.broadcasted_iota(jnp.int32, (lanes, slots), 0)

    def place(members):
        return dot(jnp.where(members, 1.0, 0.0).astype(BF16), before, NN).astype(jnp.int32)

    mine = jnp.sum(jnp.where(group == own, dest, 0), axis=0, keepdims=True)
    local = mine - group * tok
    leaving = (local >= 0) & (local < tok) & (group < groups) & (mine >= 0)
    index = jnp.where(leaving, relative * cap + place(leaving) + 1, 0)
    home = jnp.sum(index, axis=0, keepdims=True) - 1
    home_ref[...] = jnp.where(lane == home, 1.0, 0.0).astype(BF16)
    local = dest - own * tok
    arriving = (local >= 0) & (local < tok) & (dest >= 0)
    index = jnp.where(arriving, relative * cap + place(arriving), -1)
    total = jnp.zeros((lanes, slots), jnp.int32)
    for source in range(groups):
        total = total + jnp.where(
            lane == index[source : source + 1], local[source : source + 1] + 1, 0
        )
    row = jnp.sum(total.astype(F32), axis=1, keepdims=True).astype(jnp.int32) - 1
    taken = lax.broadcasted_iota(jnp.int32, (lanes, tok), 1) == row
    taken = jnp.where(taken, 1.0, 0.0)
    back_ref[...] = taken.astype(BF16)
    back_t_ref[...] = taken.T.astype(BF16)


def routing(destinations, own, groups, tok, cap):
    slots = destinations.shape[0] // groups
    lanes = groups * cap
    rows = -(-groups // 16) * 16
    table = destinations.reshape(groups, slots)
    table = jnp.pad(table, ((0, rows - groups), (0, 0)), constant_values=-1)
    return pl.pallas_call(
        functools.partial(routing_kernel, (groups, tok, cap, lanes)),
        grid=(1,),
        in_specs=[
            pl.BlockSpec(memory_space=pltpu.SMEM),
            pl.BlockSpec(table.shape, lambda i: (0, 0)),
        ],
        out_specs=[
            pl.BlockSpec((lanes, slots), lambda i: (0, 0)),
            pl.BlockSpec((lanes, tok), lambda i: (0, 0)),
            pl.BlockSpec((tok, lanes), lambda i: (0, 0)),
        ],
        out_shape=[
            pltpu.HBM((lanes, slots), BF16),
            pltpu.HBM((lanes, tok), BF16),
            pltpu.HBM((tok, lanes), BF16),
        ],
        compiler_params=params(),
        name="routing",
    )(own, table)


def mix_kernel(weights_ref, earlier_ref, home_ref, *out_refs):
    total = weights_ref[0] * earlier_ref[0].astype(F32)
    for k in range(1, earlier_ref.shape[0]):
        total = total + weights_ref[k] * earlier_ref[k].astype(F32)
    sent = dot(home_ref[...], total.astype(BF16), NT).astype(BF16)
    cap = out_refs[0].shape[0]
    for k, ref in enumerate(out_refs):
        ref[...] = sent[k * cap : (k + 1) * cap]


def pieces_of(*sizes):
    unit = math.gcd(*sizes)
    starts = [sum(sizes[:k]) for k in range(len(sizes))]
    return [(start // unit, size // unit) for start, size in zip(starts, sizes)], unit


def mix_and_sort(earlier, mix_weights, home, groups, piece, step):
    depth, _, slots = earlier.shape
    lanes = home.shape[0]
    cap = lanes // groups
    start, count = piece
    return pl.pallas_call(
        mix_kernel,
        grid=(count,),
        in_specs=[
            pl.BlockSpec(memory_space=pltpu.SMEM),
            pl.BlockSpec((depth, step, slots), lambda i: (0, start + i, 0)),
            pl.BlockSpec((lanes, slots), lambda i: (0, 0)),
        ],
        out_specs=[pl.BlockSpec((cap, step), lambda i: (0, i))] * groups,
        out_shape=[pltpu.HBM((cap, step * count), BF16)] * groups,
        compiler_params=params(),
        name=f"mix_and_sort_{start}",
    )(mix_weights, *in_hbm(earlier, home))


def exchange_rows(slabs, groups):
    received = [slabs[0]]
    for k in range(1, groups):
        if groups & (groups - 1) == 0:
            pairs = [(i, i ^ k) for i in range(groups)]
        else:
            pairs = [(i, (i + k) % groups) for i in range(groups)]
        received.append(lax.ppermute(slabs[k], "dp", pairs))
    return received


def unsort_kernel(groups, home_ref, *refs):
    in_refs, out_ref = refs[:groups], refs[-1]
    rows = jnp.concatenate([ref[...] for ref in in_refs], axis=0)
    out_ref[...] = dot(rows, home_ref[...], TN).astype(BF16)


def unsort(slabs, home, piece, step, feats, partial):
    lanes, slots = home.shape
    cap = slabs[0].shape[0]
    groups = len(slabs)
    start, count = piece
    more = [] if partial is None else [partial]
    return pl.pallas_call(
        functools.partial(unsort_kernel, groups),
        grid=(count,),
        in_specs=[pl.BlockSpec((lanes, slots), lambda i: (0, 0))]
        + [pl.BlockSpec((cap, step), lambda i: (0, i))] * groups
        + [pl.BlockSpec(memory_space=pl.ANY)] * len(more),
        out_specs=pl.BlockSpec((step, slots), lambda i: (start + i, 0)),
        out_shape=pltpu.HBM((feats, slots), BF16),
        input_output_aliases={1 + groups: 0} if more else {},
        compiler_params=params(),
        name=f"unsort_{start}",
    )(*in_hbm(home, *slabs, *more))


class Plan:
    def __init__(self, peers, held, width, tok):
        self.peers, self.held, self.width, self.tok = peers, held, width, tok
        self.piece = held * held
        self.direct = held % 16 == 0

    def sent_shape(self, parts):
        return pltpu.HBM((self.peers, parts * self.piece, self.tok), BF16)

    def sent_spec(self, parts, step, offset=0):
        return pl.BlockSpec((self.peers, parts * self.piece, step), lambda t: (0, 0, t + offset))

    def arranged(self, array):
        if self.direct:
            return array
        parts = array.shape[1] // self.piece
        array = array.reshape(self.peers, parts, self.held, self.held, self.tok)
        array = array.transpose(1, 2, 0, 3, 4)
        return array.reshape(parts * self.held, self.width, self.tok)

    def arrived_spec(self, parts, step, offset=0):
        if self.direct:
            return self.sent_spec(parts, step, offset)
        return pl.BlockSpec((parts * self.held, self.width, step), lambda t: (0, 0, t + offset))

    def each_block(self, unroll, step):
        def some(outer, carry):
            for inner in range(unroll):
                step(outer * unroll + inner)
            return carry

        unroll = min(unroll, self.held)
        lax.fori_loop(0, self.held // unroll, some, 0)

    def block(self, ref, part, b):
        if not self.direct:
            return ref[part * self.held + b]
        rows = pl.ds(pl.multiple_of(part * self.piece + b * self.held, self.held), self.held)
        return jnp.concatenate([ref[s, rows, :] for s in range(self.peers)], axis=0)

    def put(self, scratch, b, value):
        for at in range(scratch.shape[0]):
            scratch[at, pl.ds(b, self.width, stride=self.held), :] = value[
                :, at * 128 : (at + 1) * 128
            ]

    def store_range(self, out_ref, part, scratch, which):
        size = self.piece // 2
        rows = slice(part * size, (part + 1) * size)
        for at in range(scratch.shape[0]):
            for peer in range(self.peers):
                start = peer * self.piece + which * size
                out_ref[peer, rows, at * 128 : (at + 1) * 128] = scratch[
                    at, start : start + size
                ].astype(BF16)

    def store(self, out_ref, part, scratch):
        rows = slice(part * self.piece, (part + 1) * self.piece)
        for at in range(scratch.shape[0]):
            out_ref[:, rows, at * 128 : (at + 1) * 128] = (
                scratch[at].reshape(self.peers, self.piece, 128).astype(BF16)
            )


def step_of(tok):
    return 256 if tok % 256 == 0 else 128


def scratch_for(plan, step):
    return pltpu.VMEM((step // 128, plan.width * plan.held, 128), F32)


def whole(array):
    return pl.BlockSpec(array.shape, lambda t: (0,) * len(array.shape))


def clear_at_first(*refs):
    @pl.when(pl.program_id(0) == 0)
    def _():
        for ref in refs:
            ref[...] = jnp.zeros_like(ref)


def cotangent_kernel(plan, in_ref, out_ref, scratch):
    def one(b):
        rows = pl.ds(pl.multiple_of(b * plan.width, plan.width), plan.width)
        plan.put(scratch, b, in_ref[rows, :].astype(F32))

    plan.each_block(UNROLL, one)
    plan.store(out_ref, 0, scratch)


def send_cotangent(plan, cotangent):
    step = step_of(plan.tok)
    return pl.pallas_call(
        functools.partial(cotangent_kernel, plan),
        grid=(plan.tok // step,),
        in_specs=[pl.BlockSpec((plan.width * plan.held, step), lambda t: (0, t))],
        out_specs=plan.sent_spec(1, step),
        out_shape=plan.sent_shape(1),
        scratch_shapes=[scratch_for(plan, step)],
        compiler_params=params(),
        name="send_cotangent",
    )(*in_hbm(cotangent))


def product_kernel(plan, over, in_ref, factor_ref, out_ref, scratch):
    def one(b):
        plan.put(scratch, b, dot(factor_ref[b], plan.block(in_ref, 0, b), over))

    plan.each_block(UNROLL, one)
    plan.store(out_ref, 0, scratch)


def product(plan, arrived, factor, over, name):
    step = step_of(plan.tok)
    return pl.pallas_call(
        functools.partial(product_kernel, plan, over),
        grid=(plan.tok // step,),
        in_specs=[plan.arrived_spec(1, step), whole(factor)],
        out_specs=plan.sent_spec(1, step),
        out_shape=plan.sent_shape(1),
        scratch_shapes=[scratch_for(plan, step)],
        compiler_params=params(),
        name=name,
    )(arrived, *in_hbm(factor))


def cut_rows(own, array, out_refs):
    groups = len(out_refs)
    size = array.shape[1] // groups
    for k, ref in enumerate(out_refs):
        if groups & (groups - 1) == 0:
            target = own ^ k
        else:
            target = lax.rem(own + k, groups)
        ref[...] = array[:, pl.ds(pl.multiple_of(target * size, size), size), :].astype(BF16)


def sum_rows_kernel(*refs):
    total = refs[0][...].astype(F32)
    for ref in refs[1:-1]:
        total = total + ref[...].astype(F32)
    refs[-1][...] = total


def sum_rows(pieces):
    shape = pieces[0].shape
    return pl.pallas_call(
        sum_rows_kernel,
        grid=(1,),
        in_specs=[whole(piece) for piece in pieces],
        out_specs=whole(pieces[0]),
        out_shape=pltpu.HBM(shape, F32),
        compiler_params=params(),
        name="sum_rows",
    )(*in_hbm(*pieces))


def product_and_cut_kernel(plan, scale, own_ref, in_ref, other_ref, factor_ref, out_ref, *refs):
    out_refs, (sums, scratch) = refs[:-2], refs[-2:]

    def one(b):
        values = plan.block(in_ref, 0, b)
        others = plan.block(other_ref, 0, b)
        plan.put(scratch, b, dot(factor_ref[b], values, TN))
        sums[b] = dot(values, others, NT) * scale

    plan.each_block(UNROLL, one)
    plan.store(out_ref, 0, scratch)
    cut_rows(own_ref[0], sums, out_refs)


def product_and_cut(plan, arrived, other, factor, scale, own, groups, name):
    step = plan.tok
    held, width, columns = factor.shape
    cut = pltpu.HBM((held, width // groups, columns), BF16)
    outs = pl.pallas_call(
        functools.partial(product_and_cut_kernel, plan, scale),
        grid=(1,),
        in_specs=[
            pl.BlockSpec(memory_space=pltpu.SMEM),
            plan.arrived_spec(1, step),
            plan.arrived_spec(1, step),
            whole(factor),
        ],
        out_specs=[plan.sent_spec(1, step)] + [whole(cut)] * groups,
        out_shape=[plan.sent_shape(1)] + [cut] * groups,
        scratch_shapes=[pltpu.VMEM(factor.shape, F32), scratch_for(plan, step)],
        compiler_params=params(),
        name=name,
    )(own, arrived, other, *in_hbm(factor))
    return outs[0], outs[1:]


def product_and_grad_kernel(plan, scale, first, last, in_ref, other_ref, factor_ref, *refs):
    if not first:
        before_ref, refs = refs[0], refs[2:]
    out_ref, sums_ref, scratch = refs

    def one(b):
        values = plan.block(in_ref, 0, b)
        others = plan.block(other_ref, 0, b)
        plan.put(scratch, b, dot(factor_ref[b], values, TN))
        total = dot(values, others, NT)
        if not first:
            total = total + before_ref[b]
        sums_ref[b] = (total * scale).astype(BF16) if last else total

    plan.each_block(UNROLL, one)
    plan.store(out_ref, 0, scratch)


def product_and_grad(plan, full, arrived, other, factor, scale, half, halves, before, name):
    step = plan.tok
    first, last = half == 0, half == halves - 1
    sums = pltpu.HBM(factor.shape, BF16 if last else F32)
    return pl.pallas_call(
        functools.partial(product_and_grad_kernel, plan, scale, first, last),
        grid=(1,),
        in_specs=[
            plan.arrived_spec(1, step, half if arrived.shape[2] > step else 0),
            full.arrived_spec(1, step, half),
            whole(factor),
        ]
        + ([] if first else [whole(sums), pl.BlockSpec(memory_space=pl.ANY)]),
        out_specs=[full.sent_spec(1, step, half), whole(sums)],
        out_shape=[full.sent_shape(1), sums],
        input_output_aliases={} if first else {4: 0},
        scratch_shapes=[scratch_for(plan, step)],
        compiler_params=params(),
        name=f"{name}_{half}",
    )(arrived, other, *in_hbm(factor, *before))


def first_kernel(plan, groups, count, *refs):
    slab_refs, (back_t_ref, gate_ref, up_ref, packed_ref, out_ref, gates, ups) = (
        refs[: groups * count],
        refs[groups * count :],
    )
    b = 0
    for piece in range(count):
        here = slab_refs[piece * groups : (piece + 1) * groups]
        rows = jnp.concatenate([ref[...] for ref in here], axis=0)
        packed = dot(back_t_ref[...], rows, NN).astype(BF16)
        size = packed.shape[1]
        packed_ref[:, b * plan.width : b * plan.width + size] = packed
        for at in range(size // plan.width):
            values = packed[:, at * plan.width : (at + 1) * plan.width]
            plan.put(gates, b, dot(gate_ref[b], values, ((0,), (1,))))
            plan.put(ups, b, dot(up_ref[b], values, ((0,), (1,))))
            b += 1
    plan.store(out_ref, 0, gates)
    plan.store(out_ref, 1, ups)


def first_products(plan, pieces, back_t, right_gate, right_up, half):
    groups = len(pieces[0])
    feats = plan.held * plan.width
    slabs = [slab for piece in pieces for slab in piece]
    sent = plan.sent_shape(2)
    return pl.pallas_call(
        functools.partial(first_kernel, plan, groups, len(pieces)),
        grid=(1,),
        in_specs=[whole(slab) for slab in slabs]
        + [
            pl.BlockSpec((plan.tok, back_t.shape[1]), lambda i: (half, 0)),
            whole(right_gate),
            whole(right_up),
        ],
        out_specs=[
            pl.BlockSpec((plan.tok, feats), lambda i: (0, 0)),
            plan.sent_spec(2, plan.tok),
        ],
        out_shape=[pltpu.HBM((plan.tok, feats), BF16), sent],
        scratch_shapes=[scratch_for(plan, plan.tok)] * 2,
        compiler_params=params(),
        name=f"first_products_{half}",
    )(*in_hbm(*slabs, back_t, right_gate, right_up))


ROOT = 0.7978845608028654
CUBE = 0.044715


def gelu_and_slope(x):
    square = x * x
    wave = jnp.tanh(x * (ROOT + (ROOT * CUBE) * square))
    half = 0.5 + 0.5 * wave
    slope = half + x * (1.0 - wave * wave) * (0.5 * ROOT + (1.5 * ROOT * CUBE) * square)
    return x * half, slope


def middle_kernel(plan, scale, first, last, spread_ref, hidden_grad_ref, gate_ref, up_ref, *refs):
    if not first:
        before_ref, refs = refs[0], refs[3:]
    hidden_ref, low_ref, high_ref, sums_ref, hiddens, gates, ups = refs

    def add_sum(at, value):
        if not first:
            value = value + before_ref[at]
        sums_ref[at] = (value * scale).astype(BF16) if last else value

    def one(b):
        gate_in = plan.block(spread_ref, 0, b)
        up_in = plan.block(spread_ref, 1, b)
        gate_out = dot(gate_ref[b], gate_in, TN).astype(BF16).astype(F32)
        up_out = dot(up_ref[b], up_in, TN).astype(BF16).astype(F32)
        back = plan.block(hidden_grad_ref, 0, b).astype(F32)
        active, slope = gelu_and_slope(gate_out)
        plan.put(hiddens, b, active * up_out)
        gate_back = (back * up_out * slope).astype(BF16)
        up_back = (back * active).astype(BF16)
        plan.put(gates, b, dot(gate_ref[b], gate_back, NN))
        plan.put(ups, b, dot(up_ref[b], up_back, NN))
        add_sum(b, dot(gate_in, gate_back, NT))
        add_sum(plan.held + b, dot(up_in, up_back, NT))

    plan.each_block(UNROLL, one)
    plan.store(hidden_ref, 0, hiddens)
    for part, scratch in enumerate((gates, ups)):
        plan.store_range(low_ref, part, scratch, 0)
        plan.store_range(high_ref, part, scratch, 1)


def middle(plan, full, spreads, hidden_grad, left_gate, left_up, scale, half, halves, before):
    step = plan.tok
    first, last = half == 0, half == halves - 1
    sums = pltpu.HBM((2 * plan.held,) + left_gate.shape[1:], BF16 if last else F32)
    sums_spec = whole(sums)
    kept = pl.BlockSpec(memory_space=pl.ANY)
    return pl.pallas_call(
        functools.partial(middle_kernel, plan, scale, first, last),
        grid=(1,),
        in_specs=[
            plan.arrived_spec(2, step),
            full.arrived_spec(1, step, half),
            whole(left_gate),
            whole(left_up),
        ]
        + ([] if first else [sums_spec, kept, kept]),
        out_specs=[plan.sent_spec(1, step)] + [full.sent_spec(1, step, half)] * 2 + [sums_spec],
        out_shape=[plan.sent_shape(1), full.sent_shape(1), full.sent_shape(1), sums],
        input_output_aliases={} if first else {5: 1, 6: 2},
        scratch_shapes=[scratch_for(plan, step)] * 3,
        compiler_params=params(),
        name=f"middle_{half}",
    )(spreads, hidden_grad, *in_hbm(left_gate, left_up, *before))


def spread_blocks(plan, in_ref, at):
    if not plan.direct:
        return in_ref[0, at], in_ref[1, at]
    rows = slice(at * plan.held, (at + 1) * plan.held)
    return tuple(
        jnp.concatenate([in_ref[s, part, rows, :] for s in range(plan.peers)], axis=0)
        for part in range(2)
    )


def spread_form(plan, arrived, count, offset):
    size = plan.piece // 2
    if plan.direct:
        return arrived.reshape(plan.peers, 2, size, plan.tok), pl.BlockSpec(
            (plan.peers, 2, count * plan.held, plan.tok), lambda i: (0, 0, i + offset, 0)
        )
    array = arrived.reshape(plan.peers, 2, plan.held // 2, plan.held, plan.tok)
    array = array.transpose(1, 2, 0, 3, 4).reshape(2, plan.held // 2, plan.width, plan.tok)
    return array, pl.BlockSpec(
        (2, count, plan.width, plan.tok), lambda i: (0, i + offset, 0, 0)
    )


def last_kernel(plan, in_ref, back_ref, gate_ref, up_ref, *slab_refs):
    cap = slab_refs[0].shape[0]
    for at in range(gate_ref.shape[0]):
        gate_back, up_back = spread_blocks(plan, in_ref, at)
        back = dot(gate_ref[at], gate_back, NN) + dot(up_ref[at], up_back, NN)
        columns = slice(at * plan.width, (at + 1) * plan.width)
        sent = dot(back_ref[...], back.astype(BF16), NT).astype(BF16)
        for k, ref in enumerate(slab_refs):
            ref[:, columns] = sent[k * cap : (k + 1) * cap]


def last_products(plan, arrived, back, right_gate, right_up, groups, piece, unit):
    start, count = piece
    offset = start % (plan.held // 2 // unit)
    lanes = back.shape[0]
    cap = lanes // groups
    arrived, arrived_spec = spread_form(plan, arrived, unit, offset)
    factor_spec = pl.BlockSpec((unit,) + right_gate.shape[1:], lambda i: (start + i, 0, 0))
    size = unit * plan.width
    return pl.pallas_call(
        functools.partial(last_kernel, plan),
        grid=(count,),
        in_specs=[arrived_spec, whole(back), factor_spec, factor_spec],
        out_specs=[pl.BlockSpec((cap, size), lambda i: (0, i))] * groups,
        out_shape=[pltpu.HBM((cap, size * count), BF16)] * groups,
        compiler_params=params(),
        name=f"last_products_{start}",
    )(arrived, *in_hbm(back, right_gate, right_up))


def right_grads_kernel(plan, scale, halves, in_ref, *refs):
    packed_refs, grads_ref = refs[:halves], refs[-1]
    for at in range(grads_ref.shape[1]):
        columns = slice(at * plan.width, (at + 1) * plan.width)
        values = jnp.concatenate([ref[:, columns] for ref in packed_refs], axis=0)
        for part, spread in enumerate(spread_blocks(plan, in_ref, at)):
            grads_ref[part, at] = (dot(values, spread, ((0,), (1,))) * scale).astype(BF16)


def right_grads(plan, arrived, packed, factor, scale, unit, which, before):
    arrived, arrived_spec = spread_form(plan, arrived, unit, 0)
    block = factor.shape[1:]
    count = plan.held // 2 // unit
    start = which * count
    rows = packed[0].shape[0]
    return pl.pallas_call(
        functools.partial(right_grads_kernel, plan, scale, len(packed)),
        grid=(count,),
        in_specs=[arrived_spec]
        + [pl.BlockSpec((rows, unit * plan.width), lambda i: (0, start + i))] * len(packed)
        + [pl.BlockSpec(memory_space=pl.ANY)] * len(before),
        out_specs=pl.BlockSpec((2, unit) + block, lambda i: (0, start + i, 0, 0)),
        out_shape=pltpu.HBM((2,) + factor.shape, BF16),
        input_output_aliases={1 + len(packed): 0} if before else {},
        compiler_params=params(),
        name=f"right_grads_{which}",
    )(arrived, *in_hbm(*packed, *before))


def natural_kernel(in_ref, out_ref):
    held, _, held_there, tok = out_ref.shape
    out_ref[...] = in_ref[...].reshape(held, 1, held_there, tok)


def natural_order(plan, arrived):
    shape = (plan.held, plan.peers, plan.held, plan.tok)
    if not plan.direct:
        array = arrived.reshape(plan.peers, plan.held, plan.held, plan.tok)
        return array.transpose(1, 0, 2, 3).reshape(-1, plan.tok)
    array = pl.pallas_call(
        natural_kernel,
        grid=(plan.peers,),
        in_specs=[pl.BlockSpec((1, plan.piece, plan.tok), lambda s: (s, 0, 0))],
        out_specs=pl.BlockSpec((plan.held, 1, plan.held, plan.tok), lambda s: (0, s, 0, 0)),
        out_shape=pltpu.HBM(shape, BF16),
        compiler_params=params(),
        name="natural_order",
    )(arrived)
    return array.reshape(-1, plan.tok)


def body(
    earlier,
    mix_weights,
    destinations,
    cotangent,
    right_gate,
    left_gate,
    right_up,
    left_up,
    right_down,
    left_down,
):
    held, width = right_gate.shape[0], right_gate.shape[1]
    feats = earlier.shape[1]
    tok = cotangent.shape[1]
    groups = lax.axis_size("dp")
    peers = lax.axis_size("feat")
    cap = 5 * tok // (4 * groups)
    scale = (tok * groups) ** (-0.5)
    halves = 2 if tok % 256 == 0 else 1
    halves = 2 if tok % 256 == 0 else 1
    plan = Plan(peers, held, width, tok)
    part = Plan(peers, held, width, tok // halves)
    there, unit = pieces_of(
        held // 4, (held - held // 4) // 2, held - held // 4 - (held - held // 4) // 2
    )
    step = unit * width

    def move(array):
        return lax.all_to_all(array, "feat", split_axis=0, concat_axis=0, tiled=True)

    def swap(array):
        return plan.arranged(move(array))

    def after(array, *others):
        return lax.optimization_barrier((array, *others))[0]

    def total(grads):
        return lax.psum_scatter(grads, "dp", scatter_dimension=1, tiled=True)

    def exchanged_total(pieces):
        return sum_rows(exchange_rows(pieces, groups))

    own = lax.axis_index("dp").reshape(1)
    home, back, back_t = routing(destinations, own, groups, tok, cap)
    sent = [mix_and_sort(earlier, mix_weights, home, groups, p, step) for p in there]
    rows = [exchange_rows(slabs, groups) for slabs in sent]

    out_grads = swap(send_cotangent(plan, cotangent))
    out_grads = after(out_grads, rows[0], *sent[1:])
    down_spread_grad = swap(product(plan, out_grads, left_down, NN, "left_back_down"))
    down_spread_grad = after(down_spread_grad, rows[1])
    hidden_grad = product(plan, down_spread_grad, right_down, NN, "right_back_down")
    rows[2] = after(rows[2], hidden_grad)
    hidden_grad = swap(hidden_grad)

    packed, spreads = zip(
        *[first_products(part, rows, back_t, right_gate, right_up, h) for h in range(halves)]
    )
    arrived, moved = [], hidden_grad
    for h in range(halves):
        moved = move(after(spreads[h], moved))
        arrived.append(part.arranged(moved))
    if halves > 1:
        arrived[0] = after(arrived[0], spreads[1])
    hidden, before = [], ()
    for h in range(halves):
        if h:
            arrived[h] = after(arrived[h], hidden[0])
        sent_hidden, low, high, left_sums = middle(
            part, plan, arrived[h], hidden_grad, left_gate, left_up, scale, h, halves, before
        )
        hidden.append(sent_hidden)
        before = (left_sums, low, high)
    if halves > 1:
        hidden[0] = moved = move(after(hidden[0], moved))
    low = move(after(low, moved))
    left_sums = total(left_sums)
    high = move(after(high, low, left_sums))
    half = held // 2
    back_pieces, unit = pieces_of(
        half * 3 // 4, half - half * 3 // 4, half // 2, half - half // 2
    )
    step = unit * width
    factors = (back, right_gate, right_up, groups)
    sent = [last_products(plan, low, *factors, p, unit) for p in back_pieces[:2]]
    rows = [exchange_rows(slabs, groups) for slabs in sent]
    right_sums = right_grads(
        plan, after(low, sent), packed, right_gate, scale, unit, 0, ()
    )
    hidden[-1] = move(after(hidden[-1], high, rows[0], sent[1], right_sums))
    sent = [last_products(plan, high, *factors, p, unit) for p in back_pieces[2:]]
    rows += [exchange_rows(slabs, groups) for slabs in sent]
    right_sums = right_grads(
        plan, after(high, sent), packed, right_gate, scale, unit, 1, (right_sums,)
    )
    before = ()
    for h in range(halves):
        arrived = hidden[h]
        if h == halves - 1:
            arrived = after(arrived, rows[1], right_sums, *sent)
        down_spread, down_sums = product_and_grad(
            part, plan, part.arranged(arrived), down_spread_grad, right_down, scale, h, halves,
            before, "right_down",
        )
        before = (down_sums, down_spread)
    grad_right_down = down_sums
    down_spread = after(swap(down_spread), rows[2])
    result, grad_left_down = product_and_cut(
        plan, down_spread, out_grads, left_down, scale, own, groups, "left_down"
    )
    right_sums = right_sums.reshape((2 * held,) + right_gate.shape[1:])
    right_sums = total(jnp.concatenate((right_sums, grad_right_down))).astype(F32)
    grad_right_gate, grad_right_up, grad_right_down = jnp.split(right_sums, 3)
    grad_left_gate, grad_left_up = jnp.split(left_sums.astype(F32), 2)
    grad_left_down = exchanged_total(grad_left_down)
    mixed_grad = None
    for slabs, piece in zip(rows, back_pieces):
        mixed_grad = unsort(slabs, home, piece, step, feats, mixed_grad)
    output = natural_order(plan, move(result))

    return (
        output,
        mixed_grad,
        grad_right_gate,
        grad_left_gate,
        grad_right_up,
        grad_left_up,
        grad_right_down,
        grad_left_down,
    )


def solution(mesh):
    return jax.shard_map(
        body,
        mesh=mesh,
        in_specs=(
            P(None, "feat", "dp"),
            P(),
            P(),
            P("feat", "dp"),
            P("feat", None, None),
            P("feat", None, None),
            P("feat", None, None),
            P("feat", None, None),
            P("feat", None, None),
            P("feat", None, None),
        ),
        out_specs=(
            P("feat", "dp"),
            P("feat", "dp"),
            P("feat", "dp", None),
            P("feat", "dp", None),
            P("feat", "dp", None),
            P("feat", "dp", None),
            P("feat", "dp", None),
            P("feat", "dp", None),
        ),
        check_vma=False,
    )
```

```python
import functools
import math

import jax
import jax.numpy as jnp
from jax import lax
from jax.experimental import pallas as pl
from jax.experimental.pallas import tpu as pltpu
from jax.sharding import PartitionSpec as P

F32 = jnp.float32
BF16 = jnp.bfloat16
UNROLL = 16
MIB = 1024 * 1024


def params(limit=16):
    return pltpu.CompilerParams(
        vmem_limit_bytes=limit * MIB, dimension_semantics=("arbitrary",)
    )


def dot(a, b, over):
    return lax.dot_general(a, b, (over, ((), ())), preferred_element_type=F32)


def in_hbm(*arrays):
    return [pltpu.with_memory_space_constraint(array, pltpu.HBM) for array in arrays]


NN = ((1,), (0,))
NT = ((1,), (1,))
TN = ((0,), (0,))


def routing_kernel(sizes, own_ref, dest_ref, home_ref, back_ref, back_t_ref):
    groups, tok, cap, lanes = sizes
    rows, slots = dest_ref.shape
    own = own_ref[0]
    dest = dest_ref[...]
    group = lax.broadcasted_iota(jnp.int32, (rows, slots), 0)
    if groups & (groups - 1) == 0:
        relative = group ^ own
    else:
        relative = jnp.where(group >= own, group - own, group - own + groups)
    before = lax.broadcasted_iota(jnp.int32, (slots, slots), 0) < lax.broadcasted_iota(
        jnp.int32, (slots, slots), 1
    )
    before = jnp.where(before, 1.0, 0.0).astype(BF16)
    lane = lax.broadcasted_iota(jnp.int32, (lanes, slots), 0)

    def place(members):
        return dot(jnp.where(members, 1.0, 0.0).astype(BF16), before, NN).astype(jnp.int32)

    mine = jnp.sum(jnp.where(group == own, dest, 0), axis=0, keepdims=True)
    local = mine - group * tok
    leaving = (local >= 0) & (local < tok) & (group < groups) & (mine >= 0)
    index = jnp.where(leaving, relative * cap + place(leaving) + 1, 0)
    home = jnp.sum(index, axis=0, keepdims=True) - 1
    home_ref[...] = jnp.where(lane == home, 1.0, 0.0).astype(BF16)
    local = dest - own * tok
    arriving = (local >= 0) & (local < tok) & (dest >= 0)
    index = jnp.where(arriving, relative * cap + place(arriving), -1)
    total = jnp.zeros((lanes, slots), jnp.int32)
    for source in range(groups):
        total = total + jnp.where(
            lane == index[source : source + 1], local[source : source + 1] + 1, 0
        )
    row = jnp.sum(total.astype(F32), axis=1, keepdims=True).astype(jnp.int32) - 1
    taken = lax.broadcasted_iota(jnp.int32, (lanes, tok), 1) == row
    taken = jnp.where(taken, 1.0, 0.0)
    back_ref[...] = taken.astype(BF16)
    back_t_ref[...] = taken.T.astype(BF16)


def routing(destinations, own, groups, tok, cap):
    slots = destinations.shape[0] // groups
    lanes = groups * cap
    rows = -(-groups // 16) * 16
    table = destinations.reshape(groups, slots)
    table = jnp.pad(table, ((0, rows - groups), (0, 0)), constant_values=-1)
    return pl.pallas_call(
        functools.partial(routing_kernel, (groups, tok, cap, lanes)),
        grid=(1,),
        in_specs=[
            pl.BlockSpec(memory_space=pltpu.SMEM),
            pl.BlockSpec(table.shape, lambda i: (0, 0)),
        ],
        out_specs=[
            pl.BlockSpec((lanes, slots), lambda i: (0, 0)),
            pl.BlockSpec((lanes, tok), lambda i: (0, 0)),
            pl.BlockSpec((tok, lanes), lambda i: (0, 0)),
        ],
        out_shape=[
            pltpu.HBM((lanes, slots), BF16),
            pltpu.HBM((lanes, tok), BF16),
            pltpu.HBM((tok, lanes), BF16),
        ],
        compiler_params=params(32),
        name="routing",
    )(own, table)


def mix_kernel(weights_ref, earlier_ref, home_ref, *out_refs):
    total = weights_ref[0] * earlier_ref[0].astype(F32)
    for k in range(1, earlier_ref.shape[0]):
        total = total + weights_ref[k] * earlier_ref[k].astype(F32)
    sent = dot(home_ref[...], total.astype(BF16), NT).astype(BF16)
    cap = out_refs[0].shape[0]
    for k, ref in enumerate(out_refs):
        ref[...] = sent[k * cap : (k + 1) * cap]


def pieces_of(*sizes):
    unit = math.gcd(*sizes)
    starts = [sum(sizes[:k]) for k in range(len(sizes))]
    return [(start // unit, size // unit) for start, size in zip(starts, sizes)], unit


def mix_and_sort(earlier, mix_weights, home, groups, piece, step):
    depth, _, slots = earlier.shape
    lanes = home.shape[0]
    cap = lanes // groups
    start, count = piece
    return pl.pallas_call(
        mix_kernel,
        grid=(count,),
        in_specs=[
            pl.BlockSpec(memory_space=pltpu.SMEM),
            pl.BlockSpec((depth, step, slots), lambda i: (0, start + i, 0)),
            pl.BlockSpec((lanes, slots), lambda i: (0, 0)),
        ],
        out_specs=[pl.BlockSpec((cap, step), lambda i: (0, i))] * groups,
        out_shape=[pltpu.HBM((cap, step * count), BF16)] * groups,
        compiler_params=params(),
        name=f"mix_and_sort_{start}",
    )(mix_weights, *in_hbm(earlier, home))


def partner(own, k, count):
    return own ^ k if count & (count - 1) == 0 else lax.rem(own + k, count)


def exchange(arrays, axis, count):
    received = [arrays[0]]
    for k in range(1, count):
        if count & (count - 1) == 0:
            pairs = [(i, i ^ k) for i in range(count)]
        else:
            pairs = [(i, (i + k) % count) for i in range(count)]
        received.append(lax.ppermute(arrays[k], axis, pairs))
    return received


def exchange_rows(slabs, groups):
    return exchange(slabs, "dp", groups)


def unsort_kernel(groups, home_ref, *refs):
    in_refs, out_ref = refs[:groups], refs[-1]
    rows = jnp.concatenate([ref[...] for ref in in_refs], axis=0)
    out_ref[...] = dot(rows, home_ref[...], TN).astype(BF16)


def unsort(slabs, piece, home, step, feats, partial):
    lanes, slots = home.shape
    cap = slabs[0].shape[0]
    groups = len(slabs)
    start, count = piece
    more = [] if partial is None else [partial]
    return pl.pallas_call(
        functools.partial(unsort_kernel, groups),
        grid=(count,),
        in_specs=[pl.BlockSpec((lanes, slots), lambda i: (0, 0))]
        + [pl.BlockSpec((cap, step), lambda i: (0, i))] * groups
        + [pl.BlockSpec(memory_space=pl.ANY)] * len(more),
        out_specs=pl.BlockSpec((step, slots), lambda i: (start + i, 0)),
        out_shape=pltpu.HBM((feats, slots), BF16),
        input_output_aliases={1 + groups: 0} if more else {},
        compiler_params=params(),
        name=f"unsort_{start}",
    )(*in_hbm(home, *slabs, *more))


class Plan:
    def __init__(self, peers, held, width, tok):
        self.peers, self.held, self.width, self.tok = peers, held, width, tok
        self.piece = held * held
        self.direct = held % 16 == 0

    def sent_shape(self, parts):
        return pltpu.HBM((self.peers, parts * self.piece, self.tok), BF16)

    def sent_spec(self, parts, step, offset=0):
        return pl.BlockSpec((self.peers, parts * self.piece, step), lambda t: (0, 0, t + offset))

    def arranged(self, array):
        if self.direct:
            return array
        parts = array.shape[1] // self.piece
        array = array.reshape(self.peers, parts, self.held, self.held, self.tok)
        array = array.transpose(1, 2, 0, 3, 4)
        return array.reshape(parts * self.held, self.width, self.tok)

    def arrived_spec(self, parts, step, offset=0):
        if self.direct:
            return self.sent_spec(parts, step, offset)
        return pl.BlockSpec((parts * self.held, self.width, step), lambda t: (0, 0, t + offset))

    def each_block(self, unroll, step):
        def some(outer, carry):
            for inner in range(unroll):
                step(outer * unroll + inner)
            return carry

        unroll = min(unroll, self.held)
        lax.fori_loop(0, self.held // unroll, some, 0)

    def block(self, ref, part, b):
        if not self.direct:
            return ref[part * self.held + b]
        rows = pl.ds(pl.multiple_of(part * self.piece + b * self.held, self.held), self.held)
        return jnp.concatenate([ref[s, rows, :] for s in range(self.peers)], axis=0)

    def put(self, scratch, b, value):
        for at in range(scratch.shape[0]):
            scratch[at, pl.ds(b, self.width, stride=self.held), :] = value[
                :, at * 128 : (at + 1) * 128
            ]

    def store_range(self, out_ref, part, scratch, which):
        size = self.piece // 2
        rows = slice(part * size, (part + 1) * size)
        for at in range(scratch.shape[0]):
            for peer in range(self.peers):
                start = peer * self.piece + which * size
                out_ref[peer, rows, at * 128 : (at + 1) * 128] = scratch[
                    at, start : start + size
                ].astype(BF16)

    def store(self, out_ref, part, scratch):
        rows = slice(part * self.piece, (part + 1) * self.piece)
        for at in range(scratch.shape[0]):
            out_ref[:, rows, at * 128 : (at + 1) * 128] = (
                scratch[at].reshape(self.peers, self.piece, 128).astype(BF16)
            )


def step_of(tok):
    return 256 if tok % 256 == 0 else 128


def scratch_for(plan, step):
    return pltpu.VMEM((step // 128, plan.width * plan.held, 128), F32)


def whole(array):
    return pl.BlockSpec(array.shape, lambda t: (0,) * len(array.shape))


def clear_at_first(*refs):
    @pl.when(pl.program_id(0) == 0)
    def _():
        for ref in refs:
            ref[...] = jnp.zeros_like(ref)


def cotangent_kernel(plan, in_ref, out_ref, scratch):
    def one(b):
        rows = pl.ds(pl.multiple_of(b * plan.width, plan.width), plan.width)
        plan.put(scratch, b, in_ref[rows, :].astype(F32))

    plan.each_block(UNROLL, one)
    plan.store(out_ref, 0, scratch)


def send_cotangent(plan, cotangent):
    step = step_of(plan.tok)
    return pl.pallas_call(
        functools.partial(cotangent_kernel, plan),
        grid=(plan.tok // step,),
        in_specs=[pl.BlockSpec((plan.width * plan.held, step), lambda t: (0, t))],
        out_specs=plan.sent_spec(1, step),
        out_shape=plan.sent_shape(1),
        scratch_shapes=[scratch_for(plan, step)],
        compiler_params=params(),
        name="send_cotangent",
    )(*in_hbm(cotangent))


def product_kernel(plan, over, in_ref, factor_ref, out_ref, scratch):
    def one(b):
        plan.put(scratch, b, dot(factor_ref[b], plan.block(in_ref, 0, b), over))

    plan.each_block(UNROLL, one)
    plan.store(out_ref, 0, scratch)


def product(plan, arrived, factor, over, name):
    step = step_of(plan.tok)
    return pl.pallas_call(
        functools.partial(product_kernel, plan, over),
        grid=(plan.tok // step,),
        in_specs=[plan.arrived_spec(1, step), whole(factor)],
        out_specs=plan.sent_spec(1, step),
        out_shape=plan.sent_shape(1),
        scratch_shapes=[scratch_for(plan, step)],
        compiler_params=params(),
        name=name,
    )(arrived, factor)


def cut_rows(own, array, out_refs):
    groups = len(out_refs)
    size = array.shape[1] // groups
    for k, ref in enumerate(out_refs):
        target = partner(own, k, groups)
        ref[...] = array[:, pl.ds(pl.multiple_of(target * size, size), size), :].astype(BF16)


def split_rows(own, array, keep_ref, send_ref):
    groups = 2 * keep_ref.shape[0]
    size = array.shape[1] // groups
    for k in range(groups):
        start = pl.multiple_of((own ^ k) * size, size)
        ref = send_ref if k % 2 else keep_ref
        ref[k // 2] = array[:, pl.ds(start, size), :].astype(BF16)


def split_shapes(blocks, factor, groups):
    shape = (groups // 2, blocks, factor.shape[1] // groups, factor.shape[2])
    return [pltpu.HBM(shape, BF16)] * 2


def halve_kernel(count, *refs):
    for at in range(count):
        total = refs[2 * at][...].astype(F32) + refs[2 * at + 1][...].astype(F32)
        outs = refs[2 * (count + at) : 2 * (count + at) + 2]
        for k in range(total.shape[0]):
            ref = outs[k % 2]
            ref[k // 2] = total[k].astype(ref.dtype)


def halve(pairs, name):
    shapes = []
    for keep, _ in pairs:
        shape = (keep.shape[0] // 2,) + keep.shape[1:]
        shapes += [pltpu.HBM(shape, F32), pltpu.HBM(shape, BF16)]
    arrays = [array for pair in pairs for array in pair]
    outs = pl.pallas_call(
        functools.partial(halve_kernel, len(pairs)),
        grid=(1,),
        in_specs=[whole(array) for array in arrays],
        out_specs=[whole(shape) for shape in shapes],
        out_shape=shapes,
        compiler_params=params(),
        name=name,
    )(*in_hbm(*arrays))
    return [(outs[2 * at], outs[2 * at + 1]) for at in range(len(pairs))]


def swap_rows(array, bit, groups):
    return lax.ppermute(array, "dp", [(i, i ^ bit) for i in range(groups)])


def finish(pairs, groups, name):
    bit = 2
    while bit < groups:
        split = halve(pairs, f"{name}_{bit}")
        pairs = [(keep, swap_rows(send, bit, groups)) for keep, send in split]
        bit *= 2
    return [[array[0] for array in pair] for pair in pairs]


def sum_kernel(counts, *refs):
    in_refs, out_refs = refs[: sum(counts)], refs[sum(counts) :]
    at = 0
    done = [0] * len(out_refs)
    for count in counts:
        total = in_refs[at][...].astype(F32)
        for ref in in_refs[at + 1 : at + count]:
            total = total + ref[...].astype(F32)
        at += count
        size = total.shape[0] // len(out_refs)
        for part, ref in enumerate(out_refs):
            ref[done[part] : done[part] + size] = total[part * size : (part + 1) * size]
            done[part] += size


def sums_of(sets, parts, name):
    pieces = [piece for pieces in sets for piece in pieces]
    size = sum(pieces[0].shape[0] for pieces in sets) // parts
    out = pltpu.HBM((size,) + pieces[0].shape[1:], F32)
    return pl.pallas_call(
        functools.partial(sum_kernel, [len(pieces) for pieces in sets]),
        grid=(1,),
        in_specs=[whole(piece) for piece in pieces],
        out_specs=[whole(out)] * parts,
        out_shape=[out] * parts,
        compiler_params=params(),
        name=name,
    )(*in_hbm(*pieces))


def grad_kernel(plan, scale, own_ref, in_ref, other_ref, *refs):
    *out_refs, sums = refs

    def one(b):
        sums[b] = dot(plan.block(in_ref, 0, b), plan.block(other_ref, 0, b), NT) * scale

    plan.each_block(UNROLL, one)
    split_rows(own_ref[0], sums, *out_refs)


def cut_shape(blocks, factor, groups):
    return pltpu.HBM((blocks, factor.shape[1] // groups, factor.shape[2]), BF16)


def factor_grad(plan, own, arrived, other, factor, scale, groups, name):
    outs = split_shapes(plan.held, factor, groups)
    return pl.pallas_call(
        functools.partial(grad_kernel, plan, scale),
        grid=(1,),
        in_specs=[
            pl.BlockSpec(memory_space=pltpu.SMEM),
            plan.arrived_spec(1, plan.tok),
            plan.arrived_spec(1, plan.tok),
        ],
        out_specs=[whole(out) for out in outs],
        out_shape=outs,
        scratch_shapes=[pltpu.VMEM(factor.shape, F32)],
        compiler_params=params(),
        name=name,
    )(own, arrived, other)


def first_kernel(plan, groups, count, *refs):
    slab_refs, (back_t_ref, gate_ref, up_ref, packed_ref, out_ref, gates, ups) = (
        refs[: groups * count],
        refs[groups * count :],
    )
    b = 0
    for piece in range(count):
        here = slab_refs[piece * groups : (piece + 1) * groups]
        rows = jnp.concatenate([ref[...] for ref in here], axis=0)
        packed = dot(back_t_ref[...], rows, NN).astype(BF16)
        size = packed.shape[1]
        packed_ref[:, b * plan.width : b * plan.width + size] = packed
        for at in range(size // plan.width):
            values = packed[:, at * plan.width : (at + 1) * plan.width]
            plan.put(gates, b, dot(gate_ref[b], values, ((0,), (1,))))
            plan.put(ups, b, dot(up_ref[b], values, ((0,), (1,))))
            b += 1
    plan.store(out_ref, 0, gates)
    plan.store(out_ref, 1, ups)


def first_products(plan, pieces, back_t, right_gate, right_up, half):
    groups = len(pieces[0])
    feats = plan.held * plan.width
    slabs = [slab for piece in pieces for slab in piece]
    sent = plan.sent_shape(2)
    return pl.pallas_call(
        functools.partial(first_kernel, plan, groups, len(pieces)),
        grid=(1,),
        in_specs=[whole(slab) for slab in slabs]
        + [
            pl.BlockSpec((plan.tok, back_t.shape[1]), lambda i: (half, 0)),
            whole(right_gate),
            whole(right_up),
        ],
        out_specs=[
            pl.BlockSpec((plan.tok, feats), lambda i: (0, 0)),
            plan.sent_spec(2, plan.tok),
        ],
        out_shape=[pltpu.HBM((plan.tok, feats), BF16), sent],
        scratch_shapes=[scratch_for(plan, plan.tok)] * 2,
        compiler_params=params(32),
        name=f"first_products_{half}",
    )(*in_hbm(*slabs, back_t, right_gate, right_up))


ROOT = 0.7978845608028654
CUBE = 0.044715


def gelu_and_slope(x):
    square = x * x
    wave = jnp.tanh(x * (ROOT + (ROOT * CUBE) * square))
    half = 0.5 + 0.5 * wave
    slope = half + x * (1.0 - wave * wave) * (0.5 * ROOT + (1.5 * ROOT * CUBE) * square)
    return x * half, slope


def middle_kernel(
    plan, scale, first, last, own_ref, spread_ref, hidden_grad_ref, gate_ref, up_ref, *refs
):
    if not first:
        before_ref, refs = refs[0], refs[4:]
    hidden_ref, low_ref, high_ref = refs[:3]
    out_refs, (sums, hiddens, gates, ups) = refs[3:-4], refs[-4:]

    def one(b):
        gate_in = plan.block(spread_ref, 0, b)
        up_in = plan.block(spread_ref, 1, b)
        gate_out = dot(gate_ref[b], gate_in, TN).astype(BF16).astype(F32)
        up_out = dot(up_ref[b], up_in, TN).astype(BF16).astype(F32)
        back = plan.block(hidden_grad_ref, 0, b).astype(F32)
        active, slope = gelu_and_slope(gate_out)
        plan.put(hiddens, b, active * up_out)
        gate_back = (back * up_out * slope).astype(BF16)
        up_back = (back * active).astype(BF16)
        plan.put(gates, b, dot(gate_ref[b], gate_back, NN))
        plan.put(ups, b, dot(up_ref[b], up_back, NN))
        for at, values, grads in (b, gate_in, gate_back), (plan.held + b, up_in, up_back):
            total = dot(values, grads, NT)
            if not first:
                total = total + before_ref[at]
            if last:
                sums[at] = total * scale
            else:
                out_refs[0][at] = total

    plan.each_block(UNROLL, one)
    plan.store(hidden_ref, 0, hiddens)
    for part, scratch in enumerate((gates, ups)):
        plan.store_range(low_ref, part, scratch, 0)
        plan.store_range(high_ref, part, scratch, 1)
    if last:
        cut_rows(own_ref[0], sums, out_refs)


def middle(
    plan, full, own, spreads, hidden_grad, left_gate, left_up, scale, groups, half, halves, before
):
    step = plan.tok
    first, last = half == 0, half == halves - 1
    sums_shape = (2 * plan.held,) + left_gate.shape[1:]
    if last:
        sums = [cut_shape(2 * plan.held, left_gate, groups)] * groups
    else:
        sums = [pltpu.HBM(sums_shape, F32)]
    kept = pl.BlockSpec(memory_space=pl.ANY)
    here = full.sent_spec(1, step, half)
    outs = pl.pallas_call(
        functools.partial(middle_kernel, plan, scale, first, last),
        grid=(1,),
        in_specs=[
            pl.BlockSpec(memory_space=pltpu.SMEM),
            plan.arrived_spec(2, step),
            full.arrived_spec(1, step, half),
            whole(left_gate),
            whole(left_up),
        ]
        + ([] if first else [pl.BlockSpec(sums_shape, lambda t: (0, 0, 0)), kept, kept, kept]),
        out_specs=[here] * 3 + [whole(out) for out in sums],
        out_shape=[full.sent_shape(1)] * 3 + sums,
        input_output_aliases={} if first else {6: 0, 7: 1, 8: 2},
        scratch_shapes=[pltpu.VMEM(sums_shape, F32)] + [scratch_for(plan, step)] * 3,
        compiler_params=params(40),
        name=f"middle_{half}",
    )(own, spreads, hidden_grad, *in_hbm(left_gate, left_up, *before))
    return outs[:3], outs[3:]


def spread_blocks(plan, in_ref, at):
    if not plan.direct:
        return in_ref[0, at], in_ref[1, at]
    rows = slice(at * plan.held, (at + 1) * plan.held)
    return tuple(
        jnp.concatenate([in_ref[s, part, rows, :] for s in range(plan.peers)], axis=0)
        for part in range(2)
    )


def spread_form(plan, arrived, count, offset):
    size = plan.piece // 2
    if plan.direct:
        return arrived.reshape(plan.peers, 2, size, plan.tok), pl.BlockSpec(
            (plan.peers, 2, count * plan.held, plan.tok), lambda i: (0, 0, i + offset, 0)
        )
    array = arrived.reshape(plan.peers, 2, plan.held // 2, plan.held, plan.tok)
    array = array.transpose(1, 2, 0, 3, 4).reshape(2, plan.held // 2, plan.width, plan.tok)
    return array, pl.BlockSpec(
        (2, count, plan.width, plan.tok), lambda i: (0, i + offset, 0, 0)
    )


def last_kernel(plan, in_ref, back_ref, gate_ref, up_ref, *slab_refs):
    cap = slab_refs[0].shape[0]
    for at in range(gate_ref.shape[0]):
        gate_back, up_back = spread_blocks(plan, in_ref, at)
        back = dot(gate_ref[at], gate_back, NN) + dot(up_ref[at], up_back, NN)
        columns = slice(at * plan.width, (at + 1) * plan.width)
        sent = dot(back_ref[...], back.astype(BF16), NT).astype(BF16)
        for k, ref in enumerate(slab_refs):
            ref[:, columns] = sent[k * cap : (k + 1) * cap]


def last_products(plan, arrived, back, right_gate, right_up, groups, piece, unit):
    start, count = piece
    offset = start % (plan.held // 2 // unit)
    lanes = back.shape[0]
    cap = lanes // groups
    arrived, arrived_spec = spread_form(plan, arrived, unit, offset)
    factor_spec = pl.BlockSpec((unit,) + right_gate.shape[1:], lambda i: (start + i, 0, 0))
    size = unit * plan.width
    return pl.pallas_call(
        functools.partial(last_kernel, plan),
        grid=(count,),
        in_specs=[arrived_spec, whole(back), factor_spec, factor_spec],
        out_specs=[pl.BlockSpec((cap, size), lambda i: (0, i))] * groups,
        out_shape=[pltpu.HBM((cap, size * count), BF16)] * groups,
        compiler_params=params(32),
        name=f"last_products_{start}",
    )(arrived, *in_hbm(back, right_gate, right_up))


def right_grads_kernel(plan, scale, halves, own_ref, in_ref, *refs):
    packed_refs, out_refs, sums = refs[:halves], refs[halves:-1], refs[-1]
    count = sums.shape[0] // 2
    for at in range(count):
        columns = slice(at * plan.width, (at + 1) * plan.width)
        values = jnp.concatenate([ref[:, columns] for ref in packed_refs], axis=0)
        for part, spread in enumerate(spread_blocks(plan, in_ref, at)):
            sums[part * count + at] = dot(values, spread, ((0,), (1,))) * scale
    split_rows(own_ref[0], sums, *out_refs)


def right_grads(plan, own, arrived, packed, factor, scale, groups, which):
    count = plan.held // 2
    arrived, arrived_spec = spread_form(plan, arrived, count, 0)
    rows = packed[0].shape[0]
    outs = split_shapes(2 * count, factor, groups)
    return pl.pallas_call(
        functools.partial(right_grads_kernel, plan, scale, len(packed)),
        grid=(1,),
        in_specs=[pl.BlockSpec(memory_space=pltpu.SMEM), arrived_spec]
        + [pl.BlockSpec((rows, count * plan.width), lambda i: (0, which))] * len(packed),
        out_specs=[whole(out) for out in outs],
        out_shape=outs,
        scratch_shapes=[pltpu.VMEM((2 * count,) + factor.shape[1:], F32)],
        compiler_params=params(32),
        name=f"right_grads_{which}",
    )(own, arrived, *in_hbm(*packed))


def natural_kernel(in_ref, out_ref):
    held, _, held_there, tok = out_ref.shape
    out_ref[...] = in_ref[...].reshape(held, 1, held_there, tok)


def natural_order(plan, arrived):
    shape = (plan.held, plan.peers, plan.held, plan.tok)
    if not plan.direct:
        array = arrived.reshape(plan.peers, plan.held, plan.held, plan.tok)
        return array.transpose(1, 0, 2, 3).reshape(-1, plan.tok)
    array = pl.pallas_call(
        natural_kernel,
        grid=(plan.peers,),
        in_specs=[pl.BlockSpec((1, plan.piece, plan.tok), lambda s: (s, 0, 0))],
        out_specs=pl.BlockSpec((plan.held, 1, plan.held, plan.tok), lambda s: (0, s, 0, 0)),
        out_shape=pltpu.HBM(shape, BF16),
        compiler_params=params(),
        name="natural_order",
    )(arrived)
    return array.reshape(-1, plan.tok)


def body(
    earlier,
    mix_weights,
    destinations,
    cotangent,
    right_gate,
    left_gate,
    right_up,
    left_up,
    right_down,
    left_down,
):
    held, width = right_gate.shape[0], right_gate.shape[1]
    feats = earlier.shape[1]
    tok = cotangent.shape[1]
    groups = lax.axis_size("dp")
    peers = lax.axis_size("feat")
    cap = 5 * tok // (4 * groups)
    scale = (tok * groups) ** (-0.5)
    halves = 2 if tok % 256 == 0 else 1
    halves = 2 if tok % 256 == 0 else 1
    plan = Plan(peers, held, width, tok)
    part = Plan(peers, held, width, tok // halves)
    there, unit = pieces_of(
        held // 4, (held - held // 4) // 2, held - held // 4 - (held - held // 4) // 2
    )
    step = unit * width

    def move(array):
        return lax.all_to_all(array, "feat", split_axis=0, concat_axis=0, tiled=True)

    def swap(array):
        return plan.arranged(move(array))

    def after(array, *others):
        return lax.optimization_barrier((array, *others))[0]

    own = lax.axis_index("dp").reshape(1)
    home, back, back_t = routing(destinations, own, groups, tok, cap)
    sent = [mix_and_sort(earlier, mix_weights, home, groups, p, step) for p in there]
    rows = [exchange_rows(slabs, groups) for slabs in sent]

    out_grads = swap(send_cotangent(plan, cotangent))
    out_grads = after(out_grads, rows[0], *sent[1:])
    down_spread_grad = swap(product(plan, out_grads, left_down, NN, "left_back_down"))
    down_spread_grad = after(down_spread_grad, rows[1])
    hidden_grad = product(plan, down_spread_grad, right_down, NN, "right_back_down")
    rows[2] = after(rows[2], hidden_grad)
    hidden_grad = swap(hidden_grad)

    packed, spreads = zip(
        *[first_products(part, rows, back_t, right_gate, right_up, h) for h in range(halves)]
    )
    arrived, moved = [], hidden_grad
    for h in range(halves):
        moved = move(after(spreads[h], moved))
        arrived.append(part.arranged(moved))
    if halves > 1:
        arrived[0] = after(arrived[0], spreads[1])
    before = ()
    for h in range(halves):
        if h:
            arrived[h] = after(arrived[h], before[0])
        (hidden, low, high), left_sums = middle(
            part, plan, own, arrived[h], hidden_grad, left_gate, left_up, scale, groups, h, halves,
            before,
        )
        before = (left_sums[0], hidden, low, high)
    low = move(low)
    left_sums = exchange_rows(left_sums, groups)
    high = move(after(high, low, *left_sums))
    grad_left_gate, grad_left_up = sums_of([left_sums], 2, "sum_left")
    half = held // 2
    most = max(half * 5 // 8, 1)
    back_pieces, unit = pieces_of(most, half - most, half - most, most)
    step = unit * width
    factors = (back, right_gate, right_up, groups)
    sent = [last_products(plan, low, *factors, p, unit) for p in back_pieces[:2]]
    rows = [exchange_rows(slabs, groups) for slabs in sent]
    right_low = right_grads(plan, own, after(low, sent), packed, right_gate, scale, groups, 0)
    hidden = swap(after(hidden, high, rows[0], sent[1], right_low, grad_left_gate))
    sent = [last_products(plan, high, *factors, p, unit) for p in back_pieces[2:]]
    rows += [exchange_rows(slabs, groups) for slabs in sent]
    right_high = right_grads(
        plan, own, after(high, sent), packed, right_gate, scale, groups, 1
    )
    places = (home, step, feats)
    mixed_grad = unsort(rows[0], back_pieces[0], *places, None)
    right_low = [(right_low[0], swap_rows(right_low[1], 1, groups))]
    hidden = after(hidden, rows[1], rows[2], sent[1], right_high, mixed_grad, right_low)
    down_spread = product(plan, hidden, right_down, TN, "right_down")
    down_grad = factor_grad(
        plan, own, after(hidden, down_spread), down_spread_grad, right_down, scale, groups,
        "right_down_grad",
    )
    down_spread = swap(down_spread)
    mixed_grad = unsort(rows[1], back_pieces[1], *places, mixed_grad)
    mixed_grad = unsort(rows[2], back_pieces[2], *places, mixed_grad)
    right_low = finish(right_low, groups, "halve_right_low")
    right_high = (right_high[0], swap_rows(right_high[1], 1, groups))
    down_grad = (down_grad[0], swap_rows(down_grad[1], 1, groups))
    down_spread = after(
        down_spread, rows[3], right_low, right_high[1], down_grad[1], mixed_grad
    )
    result = product(plan, down_spread, left_down, TN, "left_down")
    left_down_grad = factor_grad(
        plan, own, after(down_spread, result), out_grads, left_down, scale, groups,
        "left_down_grad",
    )
    output = natural_order(plan, move(result))
    mixed_grad = unsort(rows[3], back_pieces[3], *places, mixed_grad)
    left_down_grad = [(left_down_grad[0], swap_rows(left_down_grad[1], 1, groups))]
    right_high, down_grad = finish([right_high, down_grad], groups, "halve_right")
    left_down_grad = finish(left_down_grad, groups, "halve_left_down")[0]
    grad_right_gate, grad_right_up = sums_of([right_low[0], right_high], 2, "sum_right")
    (grad_right_down,) = sums_of([down_grad], 1, "sum_right_down")
    left_down_grad = after(left_down_grad, output, mixed_grad, grad_right_gate, grad_right_down)
    (grad_left_down,) = sums_of([left_down_grad], 1, "sum_left_down")
    return (
        output,
        mixed_grad,
        grad_right_gate,
        grad_left_gate,
        grad_right_up,
        grad_left_up,
        grad_right_down,
        grad_left_down,
    )


def solution(mesh):
    return jax.shard_map(
        body,
        mesh=mesh,
        in_specs=(
            P(None, "feat", "dp"),
            P(),
            P(),
            P("feat", "dp"),
            P("feat", None, None),
            P("feat", None, None),
            P("feat", None, None),
            P("feat", None, None),
            P("feat", None, None),
            P("feat", None, None),
        ),
        out_specs=(
            P("feat", "dp"),
            P("feat", "dp"),
            P("feat", "dp", None),
            P("feat", "dp", None),
            P("feat", "dp", None),
            P("feat", "dp", None),
            P("feat", "dp", None),
            P("feat", "dp", None),
        ),
        check_vma=False,
    )
```

```python
import functools
import math

import jax
import jax.numpy as jnp
from jax import lax
from jax.experimental import pallas as pl
from jax.experimental.pallas import tpu as pltpu
from jax.sharding import PartitionSpec as P

F32 = jnp.float32
BF16 = jnp.bfloat16
UNROLL = 16
MIB = 1024 * 1024


def params(limit=16):
    return pltpu.CompilerParams(
        vmem_limit_bytes=limit * MIB, dimension_semantics=("arbitrary",)
    )


def dot(a, b, over):
    return lax.dot_general(a, b, (over, ((), ())), preferred_element_type=F32)


def in_hbm(*arrays):
    return [pltpu.with_memory_space_constraint(array, pltpu.HBM) for array in arrays]


NN = ((1,), (0,))
NT = ((1,), (1,))
TN = ((0,), (0,))


def routing_kernel(sizes, own_ref, dest_ref, home_ref, back_ref, back_t_ref):
    groups, tok, cap, lanes = sizes
    rows, slots = dest_ref.shape
    own = own_ref[0]
    dest = dest_ref[...]
    group = lax.broadcasted_iota(jnp.int32, (rows, slots), 0)
    if groups & (groups - 1) == 0:
        relative = group ^ own
    else:
        relative = jnp.where(group >= own, group - own, group - own + groups)
    before = lax.broadcasted_iota(jnp.int32, (slots, slots), 0) < lax.broadcasted_iota(
        jnp.int32, (slots, slots), 1
    )
    before = jnp.where(before, 1.0, 0.0).astype(BF16)
    lane = lax.broadcasted_iota(jnp.int32, (lanes, slots), 0)

    def place(members):
        return dot(jnp.where(members, 1.0, 0.0).astype(BF16), before, NN).astype(jnp.int32)

    mine = jnp.sum(jnp.where(group == own, dest, 0), axis=0, keepdims=True)
    local = mine - group * tok
    leaving = (local >= 0) & (local < tok) & (group < groups) & (mine >= 0)
    index = jnp.where(leaving, relative * cap + place(leaving) + 1, 0)
    home = jnp.sum(index, axis=0, keepdims=True) - 1
    home_ref[...] = jnp.where(lane == home, 1.0, 0.0).astype(BF16)
    local = dest - own * tok
    arriving = (local >= 0) & (local < tok) & (dest >= 0)
    index = jnp.where(arriving, relative * cap + place(arriving), -1)
    total = jnp.zeros((lanes, slots), jnp.int32)
    for source in range(groups):
        total = total + jnp.where(
            lane == index[source : source + 1], local[source : source + 1] + 1, 0
        )
    row = jnp.sum(total.astype(F32), axis=1, keepdims=True).astype(jnp.int32) - 1
    taken = lax.broadcasted_iota(jnp.int32, (lanes, tok), 1) == row
    taken = jnp.where(taken, 1.0, 0.0)
    back_ref[...] = taken.astype(BF16)
    back_t_ref[...] = taken.T.astype(BF16)


def routing(destinations, own, groups, tok, cap):
    slots = destinations.shape[0] // groups
    lanes = groups * cap
    rows = -(-groups // 16) * 16
    table = destinations.reshape(groups, slots)
    table = jnp.pad(table, ((0, rows - groups), (0, 0)), constant_values=-1)
    return pl.pallas_call(
        functools.partial(routing_kernel, (groups, tok, cap, lanes)),
        grid=(1,),
        in_specs=[
            pl.BlockSpec(memory_space=pltpu.SMEM),
            pl.BlockSpec(table.shape, lambda i: (0, 0)),
        ],
        out_specs=[
            pl.BlockSpec((lanes, slots), lambda i: (0, 0)),
            pl.BlockSpec((lanes, tok), lambda i: (0, 0)),
            pl.BlockSpec((tok, lanes), lambda i: (0, 0)),
        ],
        out_shape=[
            pltpu.HBM((lanes, slots), BF16),
            pltpu.HBM((lanes, tok), BF16),
            pltpu.HBM((tok, lanes), BF16),
        ],
        compiler_params=params(32),
        name="routing",
    )(own, table)


def mix_kernel(weights_ref, earlier_ref, home_ref, *out_refs):
    total = weights_ref[0] * earlier_ref[0].astype(F32)
    for k in range(1, earlier_ref.shape[0]):
        total = total + weights_ref[k] * earlier_ref[k].astype(F32)
    sent = dot(home_ref[...], total.astype(BF16), NT).astype(BF16)
    cap = out_refs[0].shape[0]
    for k, ref in enumerate(out_refs):
        ref[...] = sent[k * cap : (k + 1) * cap]


def pieces_of(*sizes):
    unit = math.gcd(*sizes)
    starts = [sum(sizes[:k]) for k in range(len(sizes))]
    return [(start // unit, size // unit) for start, size in zip(starts, sizes)], unit


def mix_and_sort(earlier, mix_weights, home, groups, piece, step):
    depth, _, slots = earlier.shape
    lanes = home.shape[0]
    cap = lanes // groups
    start, count = piece
    return pl.pallas_call(
        mix_kernel,
        grid=(count,),
        in_specs=[
            pl.BlockSpec(memory_space=pltpu.SMEM),
            pl.BlockSpec((depth, step, slots), lambda i: (0, start + i, 0)),
            pl.BlockSpec((lanes, slots), lambda i: (0, 0)),
        ],
        out_specs=[pl.BlockSpec((cap, step), lambda i: (0, i))] * groups,
        out_shape=[pltpu.HBM((cap, step * count), BF16)] * groups,
        compiler_params=params(),
        name=f"mix_and_sort_{start}",
    )(mix_weights, *in_hbm(earlier, home))


def partner(own, k, count):
    return own ^ k if count & (count - 1) == 0 else lax.rem(own + k, count)


def exchange(arrays, axis, count):
    received = [arrays[0]]
    for k in range(1, count):
        if count & (count - 1) == 0:
            pairs = [(i, i ^ k) for i in range(count)]
        else:
            pairs = [(i, (i + k) % count) for i in range(count)]
        received.append(lax.ppermute(arrays[k], axis, pairs))
    return received


def exchange_rows(slabs, groups):
    return exchange(slabs, "dp", groups)


def unsort_kernel(groups, home_ref, *refs):
    in_refs, out_ref = refs[:groups], refs[-1]
    rows = jnp.concatenate([ref[...] for ref in in_refs], axis=0)
    out_ref[...] = dot(rows, home_ref[...], TN).astype(BF16)


def unsort(slabs, piece, home, step, feats, partial):
    lanes, slots = home.shape
    cap = slabs[0].shape[0]
    groups = len(slabs)
    start, count = piece
    more = [] if partial is None else [partial]
    return pl.pallas_call(
        functools.partial(unsort_kernel, groups),
        grid=(count,),
        in_specs=[pl.BlockSpec((lanes, slots), lambda i: (0, 0))]
        + [pl.BlockSpec((cap, step), lambda i: (0, i))] * groups
        + [pl.BlockSpec(memory_space=pl.ANY)] * len(more),
        out_specs=pl.BlockSpec((step, slots), lambda i: (start + i, 0)),
        out_shape=pltpu.HBM((feats, slots), BF16),
        input_output_aliases={1 + groups: 0} if more else {},
        compiler_params=params(),
        name=f"unsort_{start}",
    )(*in_hbm(home, *slabs, *more))


class Plan:
    def __init__(self, peers, held, width, tok):
        self.peers, self.held, self.width, self.tok = peers, held, width, tok
        self.piece = held * held
        self.direct = held % 16 == 0

    def sent_shape(self, parts):
        return pltpu.HBM((self.peers, parts * self.piece, self.tok), BF16)

    def sent_spec(self, parts, step, offset=0):
        return pl.BlockSpec((self.peers, parts * self.piece, step), lambda t: (0, 0, t + offset))

    def arranged(self, array):
        if self.direct:
            return array
        parts = array.shape[1] // self.piece
        array = array.reshape(self.peers, parts, self.held, self.held, self.tok)
        array = array.transpose(1, 2, 0, 3, 4)
        return array.reshape(parts * self.held, self.width, self.tok)

    def arrived_spec(self, parts, step, offset=0):
        if self.direct:
            return self.sent_spec(parts, step, offset)
        return pl.BlockSpec((parts * self.held, self.width, step), lambda t: (0, 0, t + offset))

    def each_block(self, unroll, step):
        def some(outer, carry):
            for inner in range(unroll):
                step(outer * unroll + inner)
            return carry

        unroll = min(unroll, self.held)
        lax.fori_loop(0, self.held // unroll, some, 0)

    def block(self, ref, part, b):
        if not self.direct:
            return ref[part * self.held + b]
        rows = pl.ds(pl.multiple_of(part * self.piece + b * self.held, self.held), self.held)
        return jnp.concatenate([ref[s, rows, :] for s in range(self.peers)], axis=0)

    def put(self, scratch, b, value):
        for at in range(scratch.shape[0]):
            scratch[at, pl.ds(b, self.width, stride=self.held), :] = value[
                :, at * 128 : (at + 1) * 128
            ]

    def store_range(self, out_ref, part, scratch, which):
        size = self.piece // 2
        rows = slice(part * size, (part + 1) * size)
        for at in range(scratch.shape[0]):
            for peer in range(self.peers):
                start = peer * self.piece + which * size
                out_ref[peer, rows, at * 128 : (at + 1) * 128] = scratch[
                    at, start : start + size
                ].astype(BF16)

    def store(self, out_ref, part, scratch):
        rows = slice(part * self.piece, (part + 1) * self.piece)
        for at in range(scratch.shape[0]):
            out_ref[:, rows, at * 128 : (at + 1) * 128] = (
                scratch[at].reshape(self.peers, self.piece, 128).astype(BF16)
            )


def step_of(tok):
    return 256 if tok % 256 == 0 else 128


def scratch_for(plan, step):
    return pltpu.VMEM((step // 128, plan.width * plan.held, 128), F32)


def whole(array):
    return pl.BlockSpec(array.shape, lambda t: (0,) * len(array.shape))


def clear_at_first(*refs):
    @pl.when(pl.program_id(0) == 0)
    def _():
        for ref in refs:
            ref[...] = jnp.zeros_like(ref)


def cotangent_kernel(plan, in_ref, out_ref, scratch):
    def one(b):
        rows = pl.ds(pl.multiple_of(b * plan.width, plan.width), plan.width)
        plan.put(scratch, b, in_ref[rows, :].astype(F32))

    plan.each_block(UNROLL, one)
    plan.store(out_ref, 0, scratch)


def send_cotangent(plan, cotangent):
    step = step_of(plan.tok)
    return pl.pallas_call(
        functools.partial(cotangent_kernel, plan),
        grid=(plan.tok // step,),
        in_specs=[pl.BlockSpec((plan.width * plan.held, step), lambda t: (0, t))],
        out_specs=plan.sent_spec(1, step),
        out_shape=plan.sent_shape(1),
        scratch_shapes=[scratch_for(plan, step)],
        compiler_params=params(),
        name="send_cotangent",
    )(*in_hbm(cotangent))


def product_kernel(plan, over, in_ref, factor_ref, out_ref, scratch):
    def one(b):
        plan.put(scratch, b, dot(factor_ref[b], plan.block(in_ref, 0, b), over))

    plan.each_block(UNROLL, one)
    plan.store(out_ref, 0, scratch)


def product(plan, arrived, factor, over, name):
    step = step_of(plan.tok)
    return pl.pallas_call(
        functools.partial(product_kernel, plan, over),
        grid=(plan.tok // step,),
        in_specs=[plan.arrived_spec(1, step), whole(factor)],
        out_specs=plan.sent_spec(1, step),
        out_shape=plan.sent_shape(1),
        scratch_shapes=[scratch_for(plan, step)],
        compiler_params=params(),
        name=name,
    )(arrived, factor)


def cut_rows(own, array, out_refs):
    groups = len(out_refs)
    size = array.shape[1] // groups
    for k, ref in enumerate(out_refs):
        target = partner(own, k, groups)
        ref[...] = array[:, pl.ds(pl.multiple_of(target * size, size), size), :].astype(BF16)


def split_rows(own, array, keep_ref, send_ref):
    groups = 2 * keep_ref.shape[0]
    size = array.shape[1] // groups
    for k in range(groups):
        start = pl.multiple_of((own ^ k) * size, size)
        ref = send_ref if k % 2 else keep_ref
        ref[k // 2] = array[:, pl.ds(start, size), :].astype(BF16)


def split_shapes(blocks, factor, groups):
    shape = (groups // 2, blocks, factor.shape[1] // groups, factor.shape[2])
    return [pltpu.HBM(shape, BF16)] * 2


def halve_kernel(count, *refs):
    for at in range(count):
        total = refs[2 * at][...].astype(F32) + refs[2 * at + 1][...].astype(F32)
        outs = refs[2 * (count + at) : 2 * (count + at) + 2]
        for k in range(total.shape[0]):
            ref = outs[k % 2]
            ref[k // 2] = total[k].astype(ref.dtype)


def halve(pairs, name):
    shapes = []
    for keep, _ in pairs:
        shape = (keep.shape[0] // 2,) + keep.shape[1:]
        shapes += [pltpu.HBM(shape, F32), pltpu.HBM(shape, BF16)]
    arrays = [array for pair in pairs for array in pair]
    outs = pl.pallas_call(
        functools.partial(halve_kernel, len(pairs)),
        grid=(1,),
        in_specs=[whole(array) for array in arrays],
        out_specs=[whole(shape) for shape in shapes],
        out_shape=shapes,
        compiler_params=params(),
        name=name,
    )(*in_hbm(*arrays))
    return [(outs[2 * at], outs[2 * at + 1]) for at in range(len(pairs))]


def swap_rows(array, bit, groups):
    return lax.ppermute(array, "dp", [(i, i ^ bit) for i in range(groups)])


def finish(pairs, groups, name):
    bit = 2
    while bit < groups:
        split = halve(pairs, f"{name}_{bit}")
        pairs = [(keep, swap_rows(send, bit, groups)) for keep, send in split]
        bit *= 2
    return [[array[0] for array in pair] for pair in pairs]


def sum_kernel(counts, *refs):
    in_refs, out_refs = refs[: sum(counts)], refs[sum(counts) :]
    at = 0
    done = [0] * len(out_refs)
    for count in counts:
        total = in_refs[at][...].astype(F32)
        for ref in in_refs[at + 1 : at + count]:
            total = total + ref[...].astype(F32)
        at += count
        size = total.shape[0] // len(out_refs)
        for part, ref in enumerate(out_refs):
            ref[done[part] : done[part] + size] = total[part * size : (part + 1) * size]
            done[part] += size


def sums_of(sets, parts, name):
    pieces = [piece for pieces in sets for piece in pieces]
    size = sum(pieces[0].shape[0] for pieces in sets) // parts
    out = pltpu.HBM((size,) + pieces[0].shape[1:], F32)
    return pl.pallas_call(
        functools.partial(sum_kernel, [len(pieces) for pieces in sets]),
        grid=(1,),
        in_specs=[whole(piece) for piece in pieces],
        out_specs=[whole(out)] * parts,
        out_shape=[out] * parts,
        compiler_params=params(),
        name=name,
    )(*in_hbm(*pieces))


def grad_kernel(plan, scale, own_ref, in_ref, other_ref, *refs):
    *out_refs, sums = refs

    def one(b):
        sums[b] = dot(plan.block(in_ref, 0, b), plan.block(other_ref, 0, b), NT) * scale

    plan.each_block(UNROLL, one)
    split_rows(own_ref[0], sums, *out_refs)


def cut_shape(blocks, factor, groups):
    return pltpu.HBM((blocks, factor.shape[1] // groups, factor.shape[2]), BF16)


def factor_grad(plan, own, arrived, other, factor, scale, groups, name):
    outs = split_shapes(plan.held, factor, groups)
    return pl.pallas_call(
        functools.partial(grad_kernel, plan, scale),
        grid=(1,),
        in_specs=[
            pl.BlockSpec(memory_space=pltpu.SMEM),
            plan.arrived_spec(1, plan.tok),
            plan.arrived_spec(1, plan.tok),
        ],
        out_specs=[whole(out) for out in outs],
        out_shape=outs,
        scratch_shapes=[pltpu.VMEM(factor.shape, F32)],
        compiler_params=params(),
        name=name,
    )(own, arrived, other)


def first_kernel(plan, groups, count, *refs):
    slab_refs, (back_t_ref, gate_ref, up_ref, packed_ref, out_ref, gates, ups) = (
        refs[: groups * count],
        refs[groups * count :],
    )
    b = 0
    for piece in range(count):
        here = slab_refs[piece * groups : (piece + 1) * groups]
        rows = jnp.concatenate([ref[...] for ref in here], axis=0)
        packed = dot(back_t_ref[...], rows, NN).astype(BF16)
        size = packed.shape[1]
        packed_ref[:, b * plan.width : b * plan.width + size] = packed
        for at in range(size // plan.width):
            values = packed[:, at * plan.width : (at + 1) * plan.width]
            plan.put(gates, b, dot(gate_ref[b], values, ((0,), (1,))))
            plan.put(ups, b, dot(up_ref[b], values, ((0,), (1,))))
            b += 1
    plan.store(out_ref, 0, gates)
    plan.store(out_ref, 1, ups)


def first_products(plan, pieces, back_t, right_gate, right_up, half):
    groups = len(pieces[0])
    feats = plan.held * plan.width
    slabs = [slab for piece in pieces for slab in piece]
    sent = plan.sent_shape(2)
    return pl.pallas_call(
        functools.partial(first_kernel, plan, groups, len(pieces)),
        grid=(1,),
        in_specs=[whole(slab) for slab in slabs]
        + [
            pl.BlockSpec((plan.tok, back_t.shape[1]), lambda i: (half, 0)),
            whole(right_gate),
            whole(right_up),
        ],
        out_specs=[
            pl.BlockSpec((plan.tok, feats), lambda i: (0, 0)),
            plan.sent_spec(2, plan.tok),
        ],
        out_shape=[pltpu.HBM((plan.tok, feats), BF16), sent],
        scratch_shapes=[scratch_for(plan, plan.tok)] * 2,
        compiler_params=params(32),
        name=f"first_products_{half}",
    )(*in_hbm(*slabs, back_t, right_gate, right_up))


ROOT = 0.7978845608028654
CUBE = 0.044715


def gelu_and_slope(x):
    square = x * x
    wave = jnp.tanh(x * (ROOT + (ROOT * CUBE) * square))
    half = 0.5 + 0.5 * wave
    slope = half + x * (1.0 - wave * wave) * (0.5 * ROOT + (1.5 * ROOT * CUBE) * square)
    return x * half, slope


def middle_kernel(
    plan, scale, first, last, own_ref, spread_ref, hidden_grad_ref, gate_ref, up_ref, *refs
):
    if not first:
        before_ref, refs = refs[0], refs[4:]
    hidden_ref, low_ref, high_ref = refs[:3]
    out_refs, (sums, hiddens, gates, ups) = refs[3:-4], refs[-4:]

    def one(b):
        gate_in = plan.block(spread_ref, 0, b)
        up_in = plan.block(spread_ref, 1, b)
        gate_out = dot(gate_ref[b], gate_in, TN).astype(BF16).astype(F32)
        up_out = dot(up_ref[b], up_in, TN).astype(BF16).astype(F32)
        back = plan.block(hidden_grad_ref, 0, b).astype(F32)
        active, slope = gelu_and_slope(gate_out)
        plan.put(hiddens, b, active * up_out)
        gate_back = (back * up_out * slope).astype(BF16)
        up_back = (back * active).astype(BF16)
        plan.put(gates, b, dot(gate_ref[b], gate_back, NN))
        plan.put(ups, b, dot(up_ref[b], up_back, NN))
        for at, values, grads in (b, gate_in, gate_back), (plan.held + b, up_in, up_back):
            total = dot(values, grads, NT)
            if not first:
                total = total + before_ref[at]
            if last:
                sums[at] = total * scale
            else:
                out_refs[0][at] = total

    plan.each_block(UNROLL, one)
    plan.store(hidden_ref, 0, hiddens)
    for part, scratch in enumerate((gates, ups)):
        plan.store_range(low_ref, part, scratch, 0)
        plan.store_range(high_ref, part, scratch, 1)
    if last:
        cut_rows(own_ref[0], sums, out_refs)


def middle(
    plan, full, own, spreads, hidden_grad, left_gate, left_up, scale, groups, half, halves, before
):
    step = plan.tok
    first, last = half == 0, half == halves - 1
    sums_shape = (2 * plan.held,) + left_gate.shape[1:]
    if last:
        sums = [cut_shape(2 * plan.held, left_gate, groups)] * groups
    else:
        sums = [pltpu.HBM(sums_shape, F32)]
    kept = pl.BlockSpec(memory_space=pl.ANY)
    here = full.sent_spec(1, step, half)
    outs = pl.pallas_call(
        functools.partial(middle_kernel, plan, scale, first, last),
        grid=(1,),
        in_specs=[
            pl.BlockSpec(memory_space=pltpu.SMEM),
            plan.arrived_spec(2, step),
            full.arrived_spec(1, step, half),
            whole(left_gate),
            whole(left_up),
        ]
        + ([] if first else [pl.BlockSpec(sums_shape, lambda t: (0, 0, 0)), kept, kept, kept]),
        out_specs=[here] * 3 + [whole(out) for out in sums],
        out_shape=[full.sent_shape(1)] * 3 + sums,
        input_output_aliases={} if first else {6: 0, 7: 1, 8: 2},
        scratch_shapes=[pltpu.VMEM(sums_shape, F32)] + [scratch_for(plan, step)] * 3,
        compiler_params=params(40),
        name=f"middle_{half}",
    )(own, spreads, hidden_grad, *in_hbm(left_gate, left_up, *before))
    return outs[:3], outs[3:]


def spread_blocks(plan, in_ref, at):
    if not plan.direct:
        return in_ref[0, at], in_ref[1, at]
    rows = slice(at * plan.held, (at + 1) * plan.held)
    return tuple(
        jnp.concatenate([in_ref[s, part, rows, :] for s in range(plan.peers)], axis=0)
        for part in range(2)
    )


def spread_form(plan, arrived, count, offset):
    size = plan.piece // 2
    if plan.direct:
        return arrived.reshape(plan.peers, 2, size, plan.tok), pl.BlockSpec(
            (plan.peers, 2, count * plan.held, plan.tok), lambda i: (0, 0, i + offset, 0)
        )
    array = arrived.reshape(plan.peers, 2, plan.held // 2, plan.held, plan.tok)
    array = array.transpose(1, 2, 0, 3, 4).reshape(2, plan.held // 2, plan.width, plan.tok)
    return array, pl.BlockSpec(
        (2, count, plan.width, plan.tok), lambda i: (0, i + offset, 0, 0)
    )


def last_kernel(plan, in_ref, back_ref, gate_ref, up_ref, *slab_refs):
    cap = slab_refs[0].shape[0]
    for at in range(gate_ref.shape[0]):
        gate_back, up_back = spread_blocks(plan, in_ref, at)
        back = dot(gate_ref[at], gate_back, NN) + dot(up_ref[at], up_back, NN)
        columns = slice(at * plan.width, (at + 1) * plan.width)
        sent = dot(back_ref[...], back.astype(BF16), NT).astype(BF16)
        for k, ref in enumerate(slab_refs):
            ref[:, columns] = sent[k * cap : (k + 1) * cap]


def last_products(plan, arrived, back, right_gate, right_up, groups, piece, unit):
    start, count = piece
    offset = start % (plan.held // 2 // unit)
    lanes = back.shape[0]
    cap = lanes // groups
    arrived, arrived_spec = spread_form(plan, arrived, unit, offset)
    factor_spec = pl.BlockSpec((unit,) + right_gate.shape[1:], lambda i: (start + i, 0, 0))
    size = unit * plan.width
    return pl.pallas_call(
        functools.partial(last_kernel, plan),
        grid=(count,),
        in_specs=[arrived_spec, whole(back), factor_spec, factor_spec],
        out_specs=[pl.BlockSpec((cap, size), lambda i: (0, i))] * groups,
        out_shape=[pltpu.HBM((cap, size * count), BF16)] * groups,
        compiler_params=params(32),
        name=f"last_products_{start}",
    )(*in_hbm(arrived, back, right_gate, right_up))


def right_grads_kernel(plan, scale, halves, own_ref, in_ref, *refs):
    packed_refs, out_refs, sums = refs[:halves], refs[halves:-1], refs[-1]
    count = sums.shape[0] // 2
    for at in range(count):
        columns = slice(at * plan.width, (at + 1) * plan.width)
        values = jnp.concatenate([ref[:, columns] for ref in packed_refs], axis=0)
        for part, spread in enumerate(spread_blocks(plan, in_ref, at)):
            sums[part * count + at] = dot(values, spread, ((0,), (1,))) * scale
    split_rows(own_ref[0], sums, *out_refs)


def right_grads(plan, own, arrived, packed, factor, scale, groups, which):
    count = plan.held // 2
    arrived, arrived_spec = spread_form(plan, arrived, count, 0)
    rows = packed[0].shape[0]
    outs = split_shapes(2 * count, factor, groups)
    return pl.pallas_call(
        functools.partial(right_grads_kernel, plan, scale, len(packed)),
        grid=(1,),
        in_specs=[pl.BlockSpec(memory_space=pltpu.SMEM), arrived_spec]
        + [pl.BlockSpec((rows, count * plan.width), lambda i: (0, which))] * len(packed),
        out_specs=[whole(out) for out in outs],
        out_shape=outs,
        scratch_shapes=[pltpu.VMEM((2 * count,) + factor.shape[1:], F32)],
        compiler_params=params(32),
        name=f"right_grads_{which}",
    )(own, *in_hbm(arrived, *packed))


def natural_kernel(in_ref, out_ref):
    held, _, held_there, tok = out_ref.shape
    for peer in range(in_ref.shape[0]):
        out_ref[:, peer] = in_ref[peer].reshape(held, held_there, tok)


def natural_order(plan, arrived):
    shape = (plan.held, plan.peers, plan.held, plan.tok)
    if not plan.direct:
        array = arrived.reshape(plan.peers, plan.held, plan.held, plan.tok)
        return array.transpose(1, 0, 2, 3).reshape(-1, plan.tok)
    step = plan.peers // 2
    array = pl.pallas_call(
        natural_kernel,
        grid=(plan.peers // step,),
        in_specs=[pl.BlockSpec((step, plan.piece, plan.tok), lambda s: (s, 0, 0))],
        out_specs=pl.BlockSpec((plan.held, step, plan.held, plan.tok), lambda s: (0, s, 0, 0)),
        out_shape=pltpu.HBM(shape, BF16),
        compiler_params=params(),
        name="natural_order",
    )(arrived)
    return array.reshape(-1, plan.tok)


def body(
    earlier,
    mix_weights,
    destinations,
    cotangent,
    right_gate,
    left_gate,
    right_up,
    left_up,
    right_down,
    left_down,
):
    held, width = right_gate.shape[0], right_gate.shape[1]
    feats = earlier.shape[1]
    tok = cotangent.shape[1]
    groups = lax.axis_size("dp")
    peers = lax.axis_size("feat")
    cap = 5 * tok // (4 * groups)
    scale = (tok * groups) ** (-0.5)
    halves = 2 if tok % 256 == 0 else 1
    halves = 2 if tok % 256 == 0 else 1
    plan = Plan(peers, held, width, tok)
    part = Plan(peers, held, width, tok // halves)
    there, unit = pieces_of(
        held // 4, (held - held // 4) // 2, held - held // 4 - (held - held // 4) // 2
    )
    step = unit * width

    def move(array):
        return lax.all_to_all(array, "feat", split_axis=0, concat_axis=0, tiled=True)

    def swap(array):
        return plan.arranged(move(array))

    def after(array, *others):
        return lax.optimization_barrier((array, *others))[0]

    own = lax.axis_index("dp").reshape(1)
    home, back, back_t = routing(destinations, own, groups, tok, cap)
    sent = [mix_and_sort(earlier, mix_weights, home, groups, p, step) for p in there]
    rows = [exchange_rows(slabs, groups) for slabs in sent]

    out_grads = swap(send_cotangent(plan, cotangent))
    out_grads = after(out_grads, rows[0], *sent[1:])
    down_spread_grad = swap(product(plan, out_grads, left_down, NN, "left_back_down"))
    down_spread_grad = after(down_spread_grad, rows[1])
    hidden_grad = product(plan, down_spread_grad, right_down, NN, "right_back_down")
    rows[2] = after(rows[2], hidden_grad)
    hidden_grad = swap(hidden_grad)

    packed, spreads = zip(
        *[first_products(part, rows, back_t, right_gate, right_up, h) for h in range(halves)]
    )
    arrived, moved = [], hidden_grad
    for h in range(halves):
        moved = move(after(spreads[h], moved))
        arrived.append(part.arranged(moved))
    if halves > 1:
        arrived[0] = after(arrived[0], spreads[1])
    before = ()
    for h in range(halves):
        if h:
            arrived[h] = after(arrived[h], before[0])
        (hidden, low, high), left_sums = middle(
            part, plan, own, arrived[h], hidden_grad, left_gate, left_up, scale, groups, h, halves,
            before,
        )
        before = (left_sums[0], hidden, low, high)
    low = move(low)
    left_sums = exchange_rows(left_sums, groups)
    high = move(after(high, low, *left_sums))
    grad_left_gate, grad_left_up = sums_of([left_sums], 2, "sum_left")
    half = held // 2
    most = max(half * 5 // 8, 1)
    back_pieces, unit = pieces_of(most, half - most, half - most, most)
    step = unit * width
    factors = (back, right_gate, right_up, groups)
    sent = [last_products(plan, low, *factors, p, unit) for p in back_pieces[:2]]
    rows = [exchange_rows(slabs, groups) for slabs in sent]
    right_low = right_grads(plan, own, after(low, sent), packed, right_gate, scale, groups, 0)
    hidden = swap(after(hidden, high, rows[0], sent[1], right_low, grad_left_gate))
    sent = [last_products(plan, high, *factors, p, unit) for p in back_pieces[2:]]
    rows += [exchange_rows(slabs, groups) for slabs in sent]
    places = (home, step, feats)
    right_low = (right_low[0], swap_rows(right_low[1], 1, groups))
    hidden = after(hidden, rows[1], rows[2], sent[1])
    down_spread = product(plan, hidden, right_down, TN, "right_down")
    down_grad = factor_grad(
        plan, own, after(hidden, down_spread), down_spread_grad, right_down, scale, groups,
        "right_down_grad",
    )
    mixed_grad = unsort(rows[0], back_pieces[0], *places, None)
    mixed_grad = unsort(rows[1], back_pieces[1], *places, mixed_grad)
    right_high = right_grads(
        plan, own, after(high, rows[3], mixed_grad, down_grad), packed, right_gate, scale, groups, 1
    )
    down_spread = swap(down_spread)
    right_high = (right_high[0], swap_rows(right_high[1], 1, groups))
    down_grad = (down_grad[0], swap_rows(down_grad[1], 1, groups))
    down_spread = after(down_spread, right_low[1], right_high[1], down_grad[1])
    result = product(plan, down_spread, left_down, TN, "left_down")
    left_down_grad = factor_grad(
        plan, own, after(down_spread, result), out_grads, left_down, scale, groups,
        "left_down_grad",
    )
    output = natural_order(plan, move(result))
    left_down_grad = [(left_down_grad[0], swap_rows(left_down_grad[1], 1, groups))]
    mixed_grad = unsort(rows[2], back_pieces[2], *places, mixed_grad)
    mixed_grad = unsort(rows[3], back_pieces[3], *places, mixed_grad)
    left_down_grad = after(left_down_grad, mixed_grad)
    right_low, right_high, down_grad = finish(
        [right_low, right_high, down_grad], groups, "halve_right"
    )
    left_down_grad = finish(left_down_grad, groups, "halve_left_down")[0]
    (grad_right_down,) = sums_of([down_grad], 1, "sum_right_down")
    right_low = after(right_low, output, grad_right_down)
    grad_right_gate, grad_right_up = sums_of([right_low, right_high], 2, "sum_right")
    left_down_grad = after(left_down_grad, grad_right_gate)
    (grad_left_down,) = sums_of([left_down_grad], 1, "sum_left_down")
    return (
        output,
        mixed_grad,
        grad_right_gate,
        grad_left_gate,
        grad_right_up,
        grad_left_up,
        grad_right_down,
        grad_left_down,
    )


def solution(mesh):
    return jax.shard_map(
        body,
        mesh=mesh,
        in_specs=(
            P(None, "feat", "dp"),
            P(),
            P(),
            P("feat", "dp"),
            P("feat", None, None),
            P("feat", None, None),
            P("feat", None, None),
            P("feat", None, None),
            P("feat", None, None),
            P("feat", None, None),
        ),
        out_specs=(
            P("feat", "dp"),
            P("feat", "dp"),
            P("feat", "dp", None),
            P("feat", "dp", None),
            P("feat", "dp", None),
            P("feat", "dp", None),
            P("feat", "dp", None),
            P("feat", "dp", None),
        ),
        check_vma=False,
    )
```

```python
import functools
import math

import jax
import jax.numpy as jnp
from jax import lax
from jax.experimental import pallas as pl
from jax.experimental.pallas import tpu as pltpu
from jax.sharding import PartitionSpec as P

F32 = jnp.float32
BF16 = jnp.bfloat16
UNROLL = 16
MIB = 1024 * 1024


def params(limit=16):
    return pltpu.CompilerParams(
        vmem_limit_bytes=limit * MIB, dimension_semantics=("arbitrary",)
    )


def dot(a, b, over):
    return lax.dot_general(a, b, (over, ((), ())), preferred_element_type=F32)


def in_hbm(*arrays):
    return [pltpu.with_memory_space_constraint(array, pltpu.HBM) for array in arrays]


NN = ((1,), (0,))
NT = ((1,), (1,))
TN = ((0,), (0,))


def routing_kernel(sizes, own_ref, dest_ref, home_ref, back_ref, back_t_ref):
    groups, tok, cap, lanes = sizes
    rows, slots = dest_ref.shape
    own = own_ref[0]
    dest = dest_ref[...]
    group = lax.broadcasted_iota(jnp.int32, (rows, slots), 0)
    if groups & (groups - 1) == 0:
        relative = group ^ own
    else:
        relative = jnp.where(group >= own, group - own, group - own + groups)
    before = lax.broadcasted_iota(jnp.int32, (slots, slots), 0) < lax.broadcasted_iota(
        jnp.int32, (slots, slots), 1
    )
    before = jnp.where(before, 1.0, 0.0).astype(BF16)
    lane = lax.broadcasted_iota(jnp.int32, (lanes, slots), 0)

    def place(members):
        return dot(jnp.where(members, 1.0, 0.0).astype(BF16), before, NN).astype(jnp.int32)

    mine = jnp.sum(jnp.where(group == own, dest, 0), axis=0, keepdims=True)
    local = mine - group * tok
    leaving = (local >= 0) & (local < tok) & (group < groups) & (mine >= 0)
    index = jnp.where(leaving, relative * cap + place(leaving) + 1, 0)
    home = jnp.sum(index, axis=0, keepdims=True) - 1
    home_ref[...] = jnp.where(lane == home, 1.0, 0.0).astype(BF16)
    local = dest - own * tok
    arriving = (local >= 0) & (local < tok) & (dest >= 0)
    index = jnp.where(arriving, relative * cap + place(arriving), -1)
    total = jnp.zeros((lanes, slots), jnp.int32)
    for source in range(groups):
        total = total + jnp.where(
            lane == index[source : source + 1], local[source : source + 1] + 1, 0
        )
    row = jnp.sum(total.astype(F32), axis=1, keepdims=True).astype(jnp.int32) - 1
    taken = lax.broadcasted_iota(jnp.int32, (lanes, tok), 1) == row
    taken = jnp.where(taken, 1.0, 0.0)
    back_ref[...] = taken.astype(BF16)
    back_t_ref[...] = taken.T.astype(BF16)


def routing(destinations, own, groups, tok, cap):
    slots = destinations.shape[0] // groups
    lanes = groups * cap
    rows = -(-groups // 16) * 16
    table = destinations.reshape(groups, slots)
    table = jnp.pad(table, ((0, rows - groups), (0, 0)), constant_values=-1)
    return pl.pallas_call(
        functools.partial(routing_kernel, (groups, tok, cap, lanes)),
        grid=(1,),
        in_specs=[
            pl.BlockSpec(memory_space=pltpu.SMEM),
            pl.BlockSpec(table.shape, lambda i: (0, 0)),
        ],
        out_specs=[
            pl.BlockSpec((lanes, slots), lambda i: (0, 0)),
            pl.BlockSpec((lanes, tok), lambda i: (0, 0)),
            pl.BlockSpec((tok, lanes), lambda i: (0, 0)),
        ],
        out_shape=[
            pltpu.HBM((lanes, slots), BF16),
            pltpu.HBM((lanes, tok), BF16),
            pltpu.HBM((tok, lanes), BF16),
        ],
        compiler_params=params(32),
        name="routing",
    )(own, table)


def mix_kernel(weights_ref, earlier_ref, home_ref, *out_refs):
    total = weights_ref[0] * earlier_ref[0].astype(F32)
    for k in range(1, earlier_ref.shape[0]):
        total = total + weights_ref[k] * earlier_ref[k].astype(F32)
    sent = dot(home_ref[...], total.astype(BF16), NT).astype(BF16)
    cap = out_refs[0].shape[0]
    for k, ref in enumerate(out_refs):
        ref[...] = sent[k * cap : (k + 1) * cap]


def pieces_of(*sizes):
    unit = math.gcd(*sizes)
    starts = [sum(sizes[:k]) for k in range(len(sizes))]
    return [(start // unit, size // unit) for start, size in zip(starts, sizes)], unit


def mix_and_sort(earlier, mix_weights, home, groups, piece, step):
    depth, _, slots = earlier.shape
    lanes = home.shape[0]
    cap = lanes // groups
    start, count = piece
    return pl.pallas_call(
        mix_kernel,
        grid=(count,),
        in_specs=[
            pl.BlockSpec(memory_space=pltpu.SMEM),
            pl.BlockSpec((depth, step, slots), lambda i: (0, start + i, 0)),
            pl.BlockSpec((lanes, slots), lambda i: (0, 0)),
        ],
        out_specs=[pl.BlockSpec((cap, step), lambda i: (0, i))] * groups,
        out_shape=[pltpu.HBM((cap, step * count), BF16)] * groups,
        compiler_params=params(),
        name=f"mix_and_sort_{start}",
    )(mix_weights, *in_hbm(earlier, home))


def partner(own, k, count):
    return own ^ k if count & (count - 1) == 0 else lax.rem(own + k, count)


def exchange(arrays, axis, count):
    received = [arrays[0]]
    for k in range(1, count):
        if count & (count - 1) == 0:
            pairs = [(i, i ^ k) for i in range(count)]
        else:
            pairs = [(i, (i + k) % count) for i in range(count)]
        received.append(lax.ppermute(arrays[k], axis, pairs))
    return received


def exchange_rows(slabs, groups):
    return exchange(slabs, "dp", groups)


def unsort_kernel(groups, home_ref, *refs):
    in_refs, out_ref = refs[:groups], refs[-1]
    rows = jnp.concatenate([ref[...] for ref in in_refs], axis=0)
    out_ref[...] = dot(rows, home_ref[...], TN).astype(BF16)


def unsort(slabs, piece, home, step, feats, partial):
    lanes, slots = home.shape
    cap = slabs[0].shape[0]
    groups = len(slabs)
    start, count = piece
    more = [] if partial is None else [partial]
    return pl.pallas_call(
        functools.partial(unsort_kernel, groups),
        grid=(count,),
        in_specs=[pl.BlockSpec((lanes, slots), lambda i: (0, 0))]
        + [pl.BlockSpec((cap, step), lambda i: (0, i))] * groups
        + [pl.BlockSpec(memory_space=pl.ANY)] * len(more),
        out_specs=pl.BlockSpec((step, slots), lambda i: (start + i, 0)),
        out_shape=pltpu.HBM((feats, slots), BF16),
        input_output_aliases={1 + groups: 0} if more else {},
        compiler_params=params(),
        name=f"unsort_{start}",
    )(*in_hbm(home, *slabs, *more))


class Plan:
    def __init__(self, peers, held, width, tok):
        self.peers, self.held, self.width, self.tok = peers, held, width, tok
        self.piece = held * held
        self.direct = held % 16 == 0

    def sent_shape(self, parts):
        return pltpu.HBM((self.peers, parts * self.piece, self.tok), BF16)

    def sent_spec(self, parts, step, offset=0):
        return pl.BlockSpec((self.peers, parts * self.piece, step), lambda t: (0, 0, t + offset))

    def arranged(self, array):
        if self.direct:
            return array
        parts = array.shape[1] // self.piece
        array = array.reshape(self.peers, parts, self.held, self.held, self.tok)
        array = array.transpose(1, 2, 0, 3, 4)
        return array.reshape(parts * self.held, self.width, self.tok)

    def arrived_spec(self, parts, step, offset=0):
        if self.direct:
            return self.sent_spec(parts, step, offset)
        return pl.BlockSpec((parts * self.held, self.width, step), lambda t: (0, 0, t + offset))

    def each_block(self, unroll, step):
        def some(outer, carry):
            for inner in range(unroll):
                step(outer * unroll + inner)
            return carry

        unroll = min(unroll, self.held)
        lax.fori_loop(0, self.held // unroll, some, 0)

    def block(self, ref, part, b):
        if not self.direct:
            return ref[part * self.held + b]
        rows = pl.ds(pl.multiple_of(part * self.piece + b * self.held, self.held), self.held)
        return jnp.concatenate([ref[s, rows, :] for s in range(self.peers)], axis=0)

    def put(self, scratch, b, value):
        for at in range(scratch.shape[0]):
            scratch[at, pl.ds(b, self.width, stride=self.held), :] = value[
                :, at * 128 : (at + 1) * 128
            ]

    def store_range(self, out_ref, part, scratch, which):
        size = self.piece // 2
        rows = slice(part * size, (part + 1) * size)
        for at in range(scratch.shape[0]):
            for peer in range(self.peers):
                start = peer * self.piece + which * size
                out_ref[peer, rows, at * 128 : (at + 1) * 128] = scratch[
                    at, start : start + size
                ].astype(BF16)

    def store(self, out_ref, part, scratch):
        rows = slice(part * self.piece, (part + 1) * self.piece)
        for at in range(scratch.shape[0]):
            out_ref[:, rows, at * 128 : (at + 1) * 128] = (
                scratch[at].reshape(self.peers, self.piece, 128).astype(BF16)
            )


def step_of(tok):
    return 256 if tok % 256 == 0 else 128


def scratch_for(plan, step):
    return pltpu.VMEM((step // 128, plan.width * plan.held, 128), F32)


def whole(array):
    return pl.BlockSpec(array.shape, lambda t: (0,) * len(array.shape))


def clear_at_first(*refs):
    @pl.when(pl.program_id(0) == 0)
    def _():
        for ref in refs:
            ref[...] = jnp.zeros_like(ref)


def cotangent_kernel(plan, in_ref, out_ref, scratch):
    def one(b):
        rows = pl.ds(pl.multiple_of(b * plan.width, plan.width), plan.width)
        plan.put(scratch, b, in_ref[rows, :].astype(F32))

    plan.each_block(UNROLL, one)
    plan.store(out_ref, 0, scratch)


def send_cotangent(plan, cotangent):
    step = 128
    return pl.pallas_call(
        functools.partial(cotangent_kernel, plan),
        grid=(plan.tok // step,),
        in_specs=[pl.BlockSpec((plan.width * plan.held, step), lambda t: (0, t))],
        out_specs=plan.sent_spec(1, step),
        out_shape=plan.sent_shape(1),
        scratch_shapes=[scratch_for(plan, step)],
        compiler_params=params(),
        name="send_cotangent",
    )(*in_hbm(cotangent))


def product_kernel(plan, over, in_ref, factor_ref, out_ref, scratch):
    def one(b):
        plan.put(scratch, b, dot(factor_ref[b], plan.block(in_ref, 0, b), over))

    plan.each_block(UNROLL, one)
    plan.store(out_ref, 0, scratch)


def product(plan, arrived, factor, over, name):
    step = step_of(plan.tok)
    return pl.pallas_call(
        functools.partial(product_kernel, plan, over),
        grid=(plan.tok // step,),
        in_specs=[plan.arrived_spec(1, step), whole(factor)],
        out_specs=plan.sent_spec(1, step),
        out_shape=plan.sent_shape(1),
        scratch_shapes=[scratch_for(plan, step)],
        compiler_params=params(),
        name=name,
    )(arrived, factor)


def cut_rows(own, array, out_refs):
    groups = len(out_refs)
    size = array.shape[1] // groups
    for k, ref in enumerate(out_refs):
        target = partner(own, k, groups)
        ref[...] = array[:, pl.ds(pl.multiple_of(target * size, size), size), :].astype(BF16)


def split_rows(own, array, keep_ref, send_ref):
    groups = 2 * keep_ref.shape[0]
    size = array.shape[1] // groups
    for k in range(groups):
        start = pl.multiple_of((own ^ k) * size, size)
        ref = send_ref if k % 2 else keep_ref
        ref[k // 2] = array[:, pl.ds(start, size), :].astype(BF16)


def split_shapes(blocks, factor, groups):
    shape = (groups // 2, blocks, factor.shape[1] // groups, factor.shape[2])
    return [pltpu.HBM(shape, BF16)] * 2


def halve_kernel(count, *refs):
    for at in range(count):
        total = refs[2 * at][...].astype(F32) + refs[2 * at + 1][...].astype(F32)
        outs = refs[2 * (count + at) : 2 * (count + at) + 2]
        for k in range(total.shape[0]):
            ref = outs[k % 2]
            ref[k // 2] = total[k].astype(ref.dtype)


def halve(pairs, name):
    shapes = []
    for keep, _ in pairs:
        shape = (keep.shape[0] // 2,) + keep.shape[1:]
        shapes += [pltpu.HBM(shape, F32), pltpu.HBM(shape, BF16)]
    arrays = [array for pair in pairs for array in pair]
    outs = pl.pallas_call(
        functools.partial(halve_kernel, len(pairs)),
        grid=(1,),
        in_specs=[whole(array) for array in arrays],
        out_specs=[whole(shape) for shape in shapes],
        out_shape=shapes,
        compiler_params=params(),
        name=name,
    )(*in_hbm(*arrays))
    return [(outs[2 * at], outs[2 * at + 1]) for at in range(len(pairs))]


def swap_rows(array, bit, groups):
    return lax.ppermute(array, "dp", [(i, i ^ bit) for i in range(groups)])


def finish(pairs, groups, name):
    bit = 2
    while bit < groups:
        split = halve(pairs, f"{name}_{bit}")
        pairs = [(keep, swap_rows(send, bit, groups)) for keep, send in split]
        bit *= 2
    return [[array[0] for array in pair] for pair in pairs]


def sum_kernel(counts, *refs):
    in_refs, out_refs = refs[: sum(counts)], refs[sum(counts) :]
    at = 0
    done = [0] * len(out_refs)
    for count in counts:
        total = in_refs[at][...].astype(F32)
        for ref in in_refs[at + 1 : at + count]:
            total = total + ref[...].astype(F32)
        at += count
        size = total.shape[0] // len(out_refs)
        for part, ref in enumerate(out_refs):
            ref[done[part] : done[part] + size] = total[part * size : (part + 1) * size]
            done[part] += size


def sums_of(sets, parts, name):
    pieces = [piece for pieces in sets for piece in pieces]
    size = sum(pieces[0].shape[0] for pieces in sets) // parts
    out = pltpu.HBM((size,) + pieces[0].shape[1:], F32)
    return pl.pallas_call(
        functools.partial(sum_kernel, [len(pieces) for pieces in sets]),
        grid=(1,),
        in_specs=[whole(piece) for piece in pieces],
        out_specs=[whole(out)] * parts,
        out_shape=[out] * parts,
        compiler_params=params(),
        name=name,
    )(*in_hbm(*pieces))


def grad_kernel(plan, scale, own_ref, in_ref, other_ref, *refs):
    *out_refs, sums = refs

    def one(b):
        sums[b] = dot(plan.block(in_ref, 0, b), plan.block(other_ref, 0, b), NT) * scale

    plan.each_block(UNROLL, one)
    split_rows(own_ref[0], sums, *out_refs)


def cut_shape(blocks, factor, groups):
    return pltpu.HBM((blocks, factor.shape[1] // groups, factor.shape[2]), BF16)


def factor_grad(plan, own, arrived, other, factor, scale, groups, name):
    outs = split_shapes(plan.held, factor, groups)
    return pl.pallas_call(
        functools.partial(grad_kernel, plan, scale),
        grid=(1,),
        in_specs=[
            pl.BlockSpec(memory_space=pltpu.SMEM),
            plan.arrived_spec(1, plan.tok),
            plan.arrived_spec(1, plan.tok),
        ],
        out_specs=[whole(out) for out in outs],
        out_shape=outs,
        scratch_shapes=[pltpu.VMEM(factor.shape, F32)],
        compiler_params=params(),
        name=name,
    )(own, arrived, other)


def first_kernel(plan, groups, count, *refs):
    slab_refs, (back_t_ref, gate_ref, up_ref, packed_ref, out_ref, gates, ups) = (
        refs[: groups * count],
        refs[groups * count :],
    )
    b = 0
    for piece in range(count):
        here = slab_refs[piece * groups : (piece + 1) * groups]
        rows = jnp.concatenate([ref[...] for ref in here], axis=0)
        packed = dot(back_t_ref[...], rows, NN).astype(BF16)
        size = packed.shape[1]
        packed_ref[:, b * plan.width : b * plan.width + size] = packed
        for at in range(size // plan.width):
            values = packed[:, at * plan.width : (at + 1) * plan.width]
            plan.put(gates, b, dot(gate_ref[b], values, ((0,), (1,))))
            plan.put(ups, b, dot(up_ref[b], values, ((0,), (1,))))
            b += 1
    plan.store(out_ref, 0, gates)
    plan.store(out_ref, 1, ups)


def first_products(plan, pieces, back_t, right_gate, right_up, half, offset):
    groups = len(pieces[0])
    feats = plan.held * plan.width
    slabs = [slab for piece in pieces for slab in piece]
    sent = plan.sent_shape(2)
    return pl.pallas_call(
        functools.partial(first_kernel, plan, groups, len(pieces)),
        grid=(1,),
        in_specs=[whole(slab) for slab in slabs]
        + [
            pl.BlockSpec((plan.tok, back_t.shape[1]), lambda i: (offset, 0)),
            whole(right_gate),
            whole(right_up),
        ],
        out_specs=[
            pl.BlockSpec((plan.tok, feats), lambda i: (0, 0)),
            plan.sent_spec(2, plan.tok),
        ],
        out_shape=[pltpu.HBM((plan.tok, feats), BF16), sent],
        scratch_shapes=[scratch_for(plan, plan.tok)] * 2,
        compiler_params=params(32),
        name=f"first_products_{half}",
    )(*in_hbm(*slabs, back_t, right_gate, right_up))


ROOT = 0.7978845608028654
CUBE = 0.044715


def gelu_and_slope(x):
    square = x * x
    wave = jnp.tanh(x * (ROOT + (ROOT * CUBE) * square))
    half = 0.5 + 0.5 * wave
    slope = half + x * (1.0 - wave * wave) * (0.5 * ROOT + (1.5 * ROOT * CUBE) * square)
    return x * half, slope


def middle_kernel(
    plan, scale, first, last, own_ref, spread_ref, hidden_grad_ref, gate_ref, up_ref, *refs
):
    if not first:
        before_ref, refs = refs[0], refs[4:]
    hidden_ref, low_ref, high_ref = refs[:3]
    out_refs, (sums, hiddens, gates, ups) = refs[3:-4], refs[-4:]

    def one(b):
        gate_in = plan.block(spread_ref, 0, b)
        up_in = plan.block(spread_ref, 1, b)
        gate_out = dot(gate_ref[b], gate_in, TN).astype(BF16).astype(F32)
        up_out = dot(up_ref[b], up_in, TN).astype(BF16).astype(F32)
        back = plan.block(hidden_grad_ref, 0, b).astype(F32)
        active, slope = gelu_and_slope(gate_out)
        plan.put(hiddens, b, active * up_out)
        gate_back = (back * up_out * slope).astype(BF16)
        up_back = (back * active).astype(BF16)
        plan.put(gates, b, dot(gate_ref[b], gate_back, NN))
        plan.put(ups, b, dot(up_ref[b], up_back, NN))
        for at, values, grads in (b, gate_in, gate_back), (plan.held + b, up_in, up_back):
            total = dot(values, grads, NT)
            if not first:
                total = total + before_ref[at]
            if last:
                sums[at] = total * scale
            else:
                out_refs[0][at] = total

    plan.each_block(UNROLL, one)
    plan.store(hidden_ref, 0, hiddens)
    for part, scratch in enumerate((gates, ups)):
        plan.store_range(low_ref, part, scratch, 0)
        plan.store_range(high_ref, part, scratch, 1)
    if last:
        cut_rows(own_ref[0], sums, out_refs)


def middle(
    plan, full, own, spreads, hidden_grad, left_gate, left_up, scale, groups, half, offset, last,
    before,
):
    step = plan.tok
    first = half == 0
    sums_shape = (2 * plan.held,) + left_gate.shape[1:]
    if last:
        sums = [cut_shape(2 * plan.held, left_gate, groups)] * groups
    else:
        sums = [pltpu.HBM(sums_shape, F32)]
    kept = pl.BlockSpec(memory_space=pl.ANY)
    here = full.sent_spec(1, step, offset)
    outs = pl.pallas_call(
        functools.partial(middle_kernel, plan, scale, first, last),
        grid=(1,),
        in_specs=[
            pl.BlockSpec(memory_space=pltpu.SMEM),
            plan.arrived_spec(2, step),
            full.arrived_spec(1, step, offset),
            whole(left_gate),
            whole(left_up),
        ]
        + ([] if first else [pl.BlockSpec(sums_shape, lambda t: (0, 0, 0)), kept, kept, kept]),
        out_specs=[here] * 3 + [whole(out) for out in sums],
        out_shape=[full.sent_shape(1)] * 3 + sums,
        input_output_aliases={} if first else {6: 0, 7: 1, 8: 2},
        scratch_shapes=[pltpu.VMEM(sums_shape, F32)] + [scratch_for(plan, step)] * 3,
        compiler_params=params(48),
        name=f"middle_{half}",
    )(own, spreads, hidden_grad, *in_hbm(left_gate, left_up, *before))
    return outs[:3], outs[3:]


def spread_blocks(plan, in_ref, at):
    if not plan.direct:
        return in_ref[0, at], in_ref[1, at]
    rows = slice(at * plan.held, (at + 1) * plan.held)
    return tuple(
        jnp.concatenate([in_ref[s, part, rows, :] for s in range(plan.peers)], axis=0)
        for part in range(2)
    )


def spread_form(plan, arrived):
    size = plan.piece // 2
    if plan.direct:
        return in_hbm(arrived.reshape(plan.peers, 2, size, plan.tok))[0]
    array = arrived.reshape(plan.peers, 2, plan.held // 2, plan.held, plan.tok)
    array = array.transpose(1, 2, 0, 3, 4).reshape(2, plan.held // 2, plan.width, plan.tok)
    return in_hbm(array)[0]


def spread_spec(plan, count, offset):
    if plan.direct:
        return pl.BlockSpec(
            (plan.peers, 2, count * plan.held, plan.tok), lambda i: (0, 0, i + offset, 0)
        )
    return pl.BlockSpec((2, count, plan.width, plan.tok), lambda i: (0, i + offset, 0, 0))


def last_kernel(plan, in_ref, back_ref, gate_ref, up_ref, *slab_refs):
    cap = slab_refs[0].shape[0]
    for at in range(gate_ref.shape[0]):
        gate_back, up_back = spread_blocks(plan, in_ref, at)
        back = dot(gate_ref[at], gate_back, NN) + dot(up_ref[at], up_back, NN)
        columns = slice(at * plan.width, (at + 1) * plan.width)
        sent = dot(back_ref[...], back.astype(BF16), NT).astype(BF16)
        for k, ref in enumerate(slab_refs):
            ref[:, columns] = sent[k * cap : (k + 1) * cap]


def last_products(plan, arrived, back, right_gate, right_up, groups, piece, unit):
    start, count = piece
    offset = start % (plan.held // 2 // unit)
    lanes = back.shape[0]
    cap = lanes // groups
    arrived_spec = spread_spec(plan, unit, offset)
    factor_spec = pl.BlockSpec((unit,) + right_gate.shape[1:], lambda i: (start + i, 0, 0))
    size = unit * plan.width
    return pl.pallas_call(
        functools.partial(last_kernel, plan),
        grid=(count,),
        in_specs=[arrived_spec, whole(back), factor_spec, factor_spec],
        out_specs=[pl.BlockSpec((cap, size), lambda i: (0, i))] * groups,
        out_shape=[pltpu.HBM((cap, size * count), BF16)] * groups,
        compiler_params=params(32),
        name=f"last_products_{start}",
    )(*in_hbm(arrived, back, right_gate, right_up))


def right_grads_kernel(plan, scale, halves, own_ref, in_ref, *refs):
    packed_refs, out_refs, sums = refs[:halves], refs[halves:-1], refs[-1]
    count = sums.shape[0] // 2
    for at in range(count):
        columns = slice(at * plan.width, (at + 1) * plan.width)
        values = jnp.concatenate([ref[:, columns] for ref in packed_refs], axis=0)
        for part, spread in enumerate(spread_blocks(plan, in_ref, at)):
            sums[part * count + at] = dot(values, spread, ((0,), (1,))) * scale
    split_rows(own_ref[0], sums, *out_refs)


def right_grads(plan, own, arrived, packed, factor, scale, groups, which):
    count = plan.held // 2
    arrived_spec = spread_spec(plan, count, 0)
    outs = split_shapes(2 * count, factor, groups)
    return pl.pallas_call(
        functools.partial(right_grads_kernel, plan, scale, len(packed)),
        grid=(1,),
        in_specs=[pl.BlockSpec(memory_space=pltpu.SMEM), arrived_spec]
        + [
            pl.BlockSpec((array.shape[0], count * plan.width), lambda i: (0, which))
            for array in packed
        ],
        out_specs=[whole(out) for out in outs],
        out_shape=outs,
        scratch_shapes=[pltpu.VMEM((2 * count,) + factor.shape[1:], F32)],
        compiler_params=params(32),
        name=f"right_grads_{which}",
    )(own, *in_hbm(arrived, *packed))


def natural_kernel(in_ref, out_ref):
    held, _, held_there, tok = out_ref.shape
    for peer in range(in_ref.shape[0]):
        out_ref[:, peer] = in_ref[peer].reshape(held, held_there, tok)


def natural_order(plan, arrived):
    shape = (plan.held, plan.peers, plan.held, plan.tok)
    if not plan.direct:
        array = arrived.reshape(plan.peers, plan.held, plan.held, plan.tok)
        return array.transpose(1, 0, 2, 3).reshape(-1, plan.tok)
    step = plan.peers // 2
    array = pl.pallas_call(
        natural_kernel,
        grid=(plan.peers // step,),
        in_specs=[pl.BlockSpec((step, plan.piece, plan.tok), lambda s: (s, 0, 0))],
        out_specs=pl.BlockSpec((plan.held, step, plan.held, plan.tok), lambda s: (0, s, 0, 0)),
        out_shape=pltpu.HBM(shape, BF16),
        compiler_params=params(),
        name="natural_order",
    )(arrived)
    return array.reshape(-1, plan.tok)


def body(
    earlier,
    mix_weights,
    destinations,
    cotangent,
    right_gate,
    left_gate,
    right_up,
    left_up,
    right_down,
    left_down,
):
    held, width = right_gate.shape[0], right_gate.shape[1]
    feats = earlier.shape[1]
    tok = cotangent.shape[1]
    groups = lax.axis_size("dp")
    peers = lax.axis_size("feat")
    cap = 5 * tok // (4 * groups)
    scale = (tok * groups) ** (-0.5)
    sizes = [3 * tok // 4, tok // 4] if tok % 512 == 0 else [tok]
    offsets = [0, 3][: len(sizes)]
    halves = len(sizes)
    plan = Plan(peers, held, width, tok)
    parts = [Plan(peers, held, width, size) for size in sizes]
    there, unit = pieces_of(
        held // 4, (held - held // 4) // 2, held - held // 4 - (held - held // 4) // 2
    )
    step = unit * width

    def move(array):
        return lax.all_to_all(array, "feat", split_axis=0, concat_axis=0, tiled=True)

    def swap(array):
        return plan.arranged(move(array))

    def after(array, *others):
        return lax.optimization_barrier((array, *others))[0]

    own = lax.axis_index("dp").reshape(1)
    home, back, back_t = routing(destinations, own, groups, tok, cap)
    sent = [mix_and_sort(earlier, mix_weights, home, groups, p, step) for p in there]
    rows = [exchange_rows(slabs, groups) for slabs in sent]

    out_grads = swap(send_cotangent(plan, cotangent))
    out_grads = after(out_grads, rows[0], *sent[1:])
    down_spread_grad = swap(product(plan, out_grads, left_down, NN, "left_back_down"))
    down_spread_grad = after(down_spread_grad, rows[1])
    hidden_grad = product(plan, down_spread_grad, right_down, NN, "right_back_down")
    rows[2] = after(rows[2], hidden_grad)
    hidden_grad = swap(hidden_grad)

    packed, spreads = zip(
        *[
            first_products(parts[h], rows, back_t, right_gate, right_up, h, offsets[h])
            for h in range(halves)
        ]
    )
    arrived, moved = [], hidden_grad
    for h in range(halves):
        moved = move(after(spreads[h], moved))
        arrived.append(parts[h].arranged(moved))
    if halves > 1:
        arrived[0] = after(arrived[0], spreads[1])
    before = ()
    for h in range(halves):
        if h:
            arrived[h] = after(arrived[h], before[0])
        (hidden, low, high), left_sums = middle(
            parts[h], plan, own, arrived[h], hidden_grad, left_gate, left_up, scale, groups, h,
            offsets[h], h == halves - 1, before,
        )
        before = (left_sums[0], hidden, low, high)
    low = spread_form(plan, move(low))
    left_sums = exchange_rows(left_sums, groups)
    high = spread_form(plan, move(after(high, low, *left_sums)))
    grad_left_gate, grad_left_up = sums_of([left_sums], 2, "sum_left")
    half = held // 2
    most = max(half * 5 // 8, 1)
    back_pieces, unit = pieces_of(most, half - most, half - most, most)
    step = unit * width
    factors = (back, right_gate, right_up, groups)
    sent = [last_products(plan, low, *factors, p, unit) for p in back_pieces[:2]]
    rows = [exchange_rows(slabs, groups) for slabs in sent]
    right_low = right_grads(plan, own, after(low, sent), packed, right_gate, scale, groups, 0)
    hidden = swap(after(hidden, high, rows[0], sent[1], right_low, grad_left_gate))
    sent = [last_products(plan, high, *factors, p, unit) for p in back_pieces[2:]]
    rows += [exchange_rows(slabs, groups) for slabs in sent]
    places = (home, step, feats)
    right_low = (right_low[0], swap_rows(right_low[1], 1, groups))
    hidden = after(hidden, rows[1], rows[2], sent[1])
    down_spread = product(plan, hidden, right_down, TN, "right_down")
    down_grad = factor_grad(
        plan, own, after(hidden, down_spread), down_spread_grad, right_down, scale, groups,
        "right_down_grad",
    )
    mixed_grad = unsort(rows[0], back_pieces[0], *places, None)
    mixed_grad = unsort(rows[1], back_pieces[1], *places, mixed_grad)
    right_high = right_grads(
        plan, own, after(high, rows[3], mixed_grad, down_grad), packed, right_gate, scale, groups, 1
    )
    down_spread = swap(down_spread)
    right_high = (right_high[0], swap_rows(right_high[1], 1, groups))
    down_grad = (down_grad[0], swap_rows(down_grad[1], 1, groups))
    down_spread = after(down_spread, right_low[1], right_high[0], down_grad[1])
    result = product(plan, down_spread, left_down, TN, "left_down")
    left_down_grad = factor_grad(
        plan, own, after(down_spread, result), out_grads, left_down, scale, groups,
        "left_down_grad",
    )
    output = natural_order(plan, move(result))
    left_down_grad = [(left_down_grad[0], swap_rows(left_down_grad[1], 1, groups))]
    mixed_grad = unsort(rows[2], back_pieces[2], *places, mixed_grad)
    mixed_grad = unsort(rows[3], back_pieces[3], *places, mixed_grad)
    left_down_grad = after(left_down_grad, mixed_grad)
    right_low, right_high, down_grad = finish(
        [right_low, right_high, down_grad], groups, "halve_right"
    )
    left_down_grad = finish(left_down_grad, groups, "halve_left_down")[0]
    (grad_right_down,) = sums_of([down_grad], 1, "sum_right_down")
    right_low = after(right_low, output, grad_right_down)
    grad_right_gate, grad_right_up = sums_of([right_low, right_high], 2, "sum_right")
    left_down_grad = after(left_down_grad, grad_right_gate)
    (grad_left_down,) = sums_of([left_down_grad], 1, "sum_left_down")
    return (
        output,
        mixed_grad,
        grad_right_gate,
        grad_left_gate,
        grad_right_up,
        grad_left_up,
        grad_right_down,
        grad_left_down,
    )


def solution(mesh):
    return jax.shard_map(
        body,
        mesh=mesh,
        in_specs=(
            P(None, "feat", "dp"),
            P(),
            P(),
            P("feat", "dp"),
            P("feat", None, None),
            P("feat", None, None),
            P("feat", None, None),
            P("feat", None, None),
            P("feat", None, None),
            P("feat", None, None),
        ),
        out_specs=(
            P("feat", "dp"),
            P("feat", "dp"),
            P("feat", "dp", None),
            P("feat", "dp", None),
            P("feat", "dp", None),
            P("feat", "dp", None),
            P("feat", "dp", None),
            P("feat", "dp", None),
        ),
        check_vma=False,
    )
```

```python
import functools
import math

import jax
import jax.numpy as jnp
from jax import lax
from jax.experimental import pallas as pl
from jax.experimental.pallas import tpu as pltpu
from jax.sharding import PartitionSpec as P

F32 = jnp.float32
BF16 = jnp.bfloat16
UNROLL = 16
MIB = 1024 * 1024


def params(limit=16):
    return pltpu.CompilerParams(
        vmem_limit_bytes=limit * MIB, dimension_semantics=("arbitrary",)
    )


def dot(a, b, over):
    return lax.dot_general(a, b, (over, ((), ())), preferred_element_type=F32)


def in_hbm(*arrays):
    return [pltpu.with_memory_space_constraint(array, pltpu.HBM) for array in arrays]


NN = ((1,), (0,))
NT = ((1,), (1,))
TN = ((0,), (0,))


def routing_kernel(sizes, own_ref, dest_ref, home_ref, back_ref, back_t_ref):
    groups, tok, cap, lanes = sizes
    rows, slots = dest_ref.shape
    own = own_ref[0]
    dest = dest_ref[...]
    group = lax.broadcasted_iota(jnp.int32, (rows, slots), 0)
    if groups & (groups - 1) == 0:
        relative = group ^ own
    else:
        relative = jnp.where(group >= own, group - own, group - own + groups)
    before = lax.broadcasted_iota(jnp.int32, (slots, slots), 0) < lax.broadcasted_iota(
        jnp.int32, (slots, slots), 1
    )
    before = jnp.where(before, 1.0, 0.0).astype(BF16)
    lane = lax.broadcasted_iota(jnp.int32, (lanes, slots), 0)

    def place(members):
        return dot(jnp.where(members, 1.0, 0.0).astype(BF16), before, NN).astype(jnp.int32)

    mine = jnp.sum(jnp.where(group == own, dest, 0), axis=0, keepdims=True)
    local = mine - group * tok
    leaving = (local >= 0) & (local < tok) & (group < groups) & (mine >= 0)
    index = jnp.where(leaving, relative * cap + place(leaving) + 1, 0)
    home = jnp.sum(index, axis=0, keepdims=True) - 1
    home_ref[...] = jnp.where(lane == home, 1.0, 0.0).astype(BF16)
    local = dest - own * tok
    arriving = (local >= 0) & (local < tok) & (dest >= 0)
    index = jnp.where(arriving, relative * cap + place(arriving), -1)
    total = jnp.zeros((lanes, slots), jnp.int32)
    for source in range(groups):
        total = total + jnp.where(
            lane == index[source : source + 1], local[source : source + 1] + 1, 0
        )
    row = jnp.sum(total.astype(F32), axis=1, keepdims=True).astype(jnp.int32) - 1
    taken = lax.broadcasted_iota(jnp.int32, (lanes, tok), 1) == row
    taken = jnp.where(taken, 1.0, 0.0)
    back_ref[...] = taken.astype(BF16)
    back_t_ref[...] = taken.T.astype(BF16)


def routing(destinations, own, groups, tok, cap):
    slots = destinations.shape[0] // groups
    lanes = groups * cap
    rows = -(-groups // 16) * 16
    table = destinations.reshape(groups, slots)
    table = jnp.pad(table, ((0, rows - groups), (0, 0)), constant_values=-1)
    return pl.pallas_call(
        functools.partial(routing_kernel, (groups, tok, cap, lanes)),
        grid=(1,),
        in_specs=[
            pl.BlockSpec(memory_space=pltpu.SMEM),
            pl.BlockSpec(table.shape, lambda i: (0, 0)),
        ],
        out_specs=[
            pl.BlockSpec((lanes, slots), lambda i: (0, 0)),
            pl.BlockSpec((lanes, tok), lambda i: (0, 0)),
            pl.BlockSpec((tok, lanes), lambda i: (0, 0)),
        ],
        out_shape=[
            pltpu.HBM((lanes, slots), BF16),
            pltpu.HBM((lanes, tok), BF16),
            pltpu.HBM((tok, lanes), BF16),
        ],
        compiler_params=params(32),
        name="routing",
    )(own, table)


def mix_kernel(weights_ref, earlier_ref, home_ref, *out_refs):
    total = weights_ref[0] * earlier_ref[0].astype(F32)
    for k in range(1, earlier_ref.shape[0]):
        total = total + weights_ref[k] * earlier_ref[k].astype(F32)
    sent = dot(home_ref[...], total.astype(BF16), NT).astype(BF16)
    cap = out_refs[0].shape[0]
    for k, ref in enumerate(out_refs):
        ref[...] = sent[k * cap : (k + 1) * cap]


def pieces_of(*sizes):
    unit = math.gcd(*sizes)
    starts = [sum(sizes[:k]) for k in range(len(sizes))]
    return [(start // unit, size // unit) for start, size in zip(starts, sizes)], unit


def mix_and_sort(earlier, mix_weights, home, groups, piece, step):
    depth, _, slots = earlier.shape
    lanes = home.shape[0]
    cap = lanes // groups
    start, count = piece
    return pl.pallas_call(
        mix_kernel,
        grid=(count,),
        in_specs=[
            pl.BlockSpec(memory_space=pltpu.SMEM),
            pl.BlockSpec((depth, step, slots), lambda i: (0, start + i, 0)),
            pl.BlockSpec((lanes, slots), lambda i: (0, 0)),
        ],
        out_specs=[pl.BlockSpec((cap, step), lambda i: (0, i))] * groups,
        out_shape=[pltpu.HBM((cap, step * count), BF16)] * groups,
        compiler_params=params(),
        name=f"mix_and_sort_{start}",
    )(mix_weights, *in_hbm(earlier, home))


def partner(own, k, count):
    return own ^ k if count & (count - 1) == 0 else lax.rem(own + k, count)


def exchange(arrays, axis, count):
    received = [arrays[0]]
    for k in range(1, count):
        if count & (count - 1) == 0:
            pairs = [(i, i ^ k) for i in range(count)]
        else:
            pairs = [(i, (i + k) % count) for i in range(count)]
        received.append(lax.ppermute(arrays[k], axis, pairs))
    return received


def exchange_rows(slabs, groups):
    return exchange(slabs, "dp", groups)


def unsort_kernel(groups, home_ref, *refs):
    in_refs, out_ref = refs[:groups], refs[-1]
    rows = jnp.concatenate([ref[...] for ref in in_refs], axis=0)
    out_ref[...] = dot(rows, home_ref[...], TN).astype(BF16)


def unsort(slabs, piece, home, step, feats, partial):
    lanes, slots = home.shape
    cap = slabs[0].shape[0]
    groups = len(slabs)
    start, count = piece
    more = [] if partial is None else [partial]
    return pl.pallas_call(
        functools.partial(unsort_kernel, groups),
        grid=(count,),
        in_specs=[pl.BlockSpec((lanes, slots), lambda i: (0, 0))]
        + [pl.BlockSpec((cap, step), lambda i: (0, i))] * groups
        + [pl.BlockSpec(memory_space=pl.ANY)] * len(more),
        out_specs=pl.BlockSpec((step, slots), lambda i: (start + i, 0)),
        out_shape=pltpu.HBM((feats, slots), BF16),
        input_output_aliases={1 + groups: 0} if more else {},
        compiler_params=params(),
        name=f"unsort_{start}",
    )(*in_hbm(home, *slabs, *more))


class Plan:
    def __init__(self, peers, held, width, tok):
        self.peers, self.held, self.width, self.tok = peers, held, width, tok
        self.piece = held * held
        self.direct = held % 16 == 0

    def sent_shape(self, parts):
        return pltpu.HBM((self.peers, parts * self.piece, self.tok), BF16)

    def sent_spec(self, parts, step, offset=0):
        return pl.BlockSpec((self.peers, parts * self.piece, step), lambda t: (0, 0, t + offset))

    def arranged(self, array):
        if self.direct:
            return array
        parts = array.shape[1] // self.piece
        array = array.reshape(self.peers, parts, self.held, self.held, self.tok)
        array = array.transpose(1, 2, 0, 3, 4)
        return array.reshape(parts * self.held, self.width, self.tok)

    def arrived_spec(self, parts, step, offset=0):
        if self.direct:
            return self.sent_spec(parts, step, offset)
        return pl.BlockSpec((parts * self.held, self.width, step), lambda t: (0, 0, t + offset))

    def each_block(self, unroll, step):
        def some(outer, carry):
            for inner in range(unroll):
                step(outer * unroll + inner)
            return carry

        unroll = min(unroll, self.held)
        lax.fori_loop(0, self.held // unroll, some, 0)

    def block(self, ref, part, b):
        if not self.direct:
            return ref[part * self.held + b]
        rows = pl.ds(pl.multiple_of(part * self.piece + b * self.held, self.held), self.held)
        return jnp.concatenate([ref[s, rows, :] for s in range(self.peers)], axis=0)

    def put(self, scratch, b, value):
        for at in range(scratch.shape[0]):
            scratch[at, pl.ds(b, self.width, stride=self.held), :] = value[
                :, at * 128 : (at + 1) * 128
            ]

    def store_range(self, out_ref, part, scratch, which):
        size = self.piece // 2
        rows = slice(part * size, (part + 1) * size)
        for at in range(scratch.shape[0]):
            for peer in range(self.peers):
                start = peer * self.piece + which * size
                out_ref[peer, rows, at * 128 : (at + 1) * 128] = scratch[
                    at, start : start + size
                ].astype(BF16)

    def store(self, out_ref, part, scratch):
        rows = slice(part * self.piece, (part + 1) * self.piece)
        for at in range(scratch.shape[0]):
            out_ref[:, rows, at * 128 : (at + 1) * 128] = (
                scratch[at].reshape(self.peers, self.piece, 128).astype(BF16)
            )


def step_of(tok):
    return 256 if tok % 256 == 0 else 128


def scratch_for(plan, step):
    return pltpu.VMEM((step // 128, plan.width * plan.held, 128), F32)


def whole(array):
    return pl.BlockSpec(array.shape, lambda t: (0,) * len(array.shape))


def clear_at_first(*refs):
    @pl.when(pl.program_id(0) == 0)
    def _():
        for ref in refs:
            ref[...] = jnp.zeros_like(ref)


def cotangent_kernel(plan, in_ref, out_ref, scratch):
    def one(b):
        rows = pl.ds(pl.multiple_of(b * plan.width, plan.width), plan.width)
        plan.put(scratch, b, in_ref[rows, :].astype(F32))

    plan.each_block(UNROLL, one)
    plan.store(out_ref, 0, scratch)


def send_cotangent(plan, cotangent):
    step = 128
    return pl.pallas_call(
        functools.partial(cotangent_kernel, plan),
        grid=(plan.tok // step,),
        in_specs=[pl.BlockSpec((plan.width * plan.held, step), lambda t: (0, t))],
        out_specs=plan.sent_spec(1, step),
        out_shape=plan.sent_shape(1),
        scratch_shapes=[scratch_for(plan, step)],
        compiler_params=params(),
        name="send_cotangent",
    )(*in_hbm(cotangent))


def product_kernel(plan, over, in_ref, factor_ref, out_ref, scratch):
    def one(b):
        plan.put(scratch, b, dot(factor_ref[b], plan.block(in_ref, 0, b), over))

    plan.each_block(UNROLL, one)
    plan.store(out_ref, 0, scratch)


def product(plan, arrived, factor, over, name):
    step = step_of(plan.tok)
    return pl.pallas_call(
        functools.partial(product_kernel, plan, over),
        grid=(plan.tok // step,),
        in_specs=[plan.arrived_spec(1, step), whole(factor)],
        out_specs=plan.sent_spec(1, step),
        out_shape=plan.sent_shape(1),
        scratch_shapes=[scratch_for(plan, step)],
        compiler_params=params(),
        name=name,
    )(arrived, factor)


def cut_rows(own, array, out_refs):
    groups = len(out_refs)
    size = array.shape[1] // groups
    for k, ref in enumerate(out_refs):
        target = partner(own, k, groups)
        ref[...] = array[:, pl.ds(pl.multiple_of(target * size, size), size), :].astype(BF16)


def split_rows(own, array, keep_ref, send_ref):
    groups = 2 * keep_ref.shape[0]
    size = array.shape[1] // groups
    for k in range(groups):
        start = pl.multiple_of((own ^ k) * size, size)
        ref = send_ref if k % 2 else keep_ref
        ref[k // 2] = array[:, pl.ds(start, size), :].astype(BF16)


def split_shapes(blocks, factor, groups):
    shape = (groups // 2, blocks, factor.shape[1] // groups, factor.shape[2])
    return [pltpu.HBM(shape, BF16)] * 2


def halve_kernel(count, *refs):
    for at in range(count):
        total = refs[2 * at][...].astype(F32) + refs[2 * at + 1][...].astype(F32)
        outs = refs[2 * (count + at) : 2 * (count + at) + 2]
        for k in range(total.shape[0]):
            ref = outs[k % 2]
            ref[k // 2] = total[k].astype(ref.dtype)


def halve(pairs, name):
    shapes = []
    for keep, _ in pairs:
        shape = (keep.shape[0] // 2,) + keep.shape[1:]
        shapes += [pltpu.HBM(shape, F32), pltpu.HBM(shape, BF16)]
    arrays = [array for pair in pairs for array in pair]
    outs = pl.pallas_call(
        functools.partial(halve_kernel, len(pairs)),
        grid=(1,),
        in_specs=[whole(array) for array in arrays],
        out_specs=[whole(shape) for shape in shapes],
        out_shape=shapes,
        compiler_params=params(),
        name=name,
    )(*in_hbm(*arrays))
    return [(outs[2 * at], outs[2 * at + 1]) for at in range(len(pairs))]


def swap_rows(array, bit, groups):
    return lax.ppermute(array, "dp", [(i, i ^ bit) for i in range(groups)])


def finish(pairs, groups, name):
    bit = 2
    while bit < groups:
        split = halve(pairs, f"{name}_{bit}")
        pairs = [(keep, swap_rows(send, bit, groups)) for keep, send in split]
        bit *= 2
    return [[array[0] for array in pair] for pair in pairs]


def sum_kernel(counts, *refs):
    in_refs, out_refs = refs[: sum(counts)], refs[sum(counts) :]
    at = 0
    done = [0] * len(out_refs)
    for count in counts:
        total = in_refs[at][...].astype(F32)
        for ref in in_refs[at + 1 : at + count]:
            total = total + ref[...].astype(F32)
        at += count
        size = total.shape[0] // len(out_refs)
        for part, ref in enumerate(out_refs):
            ref[done[part] : done[part] + size] = total[part * size : (part + 1) * size]
            done[part] += size


def sums_of(sets, parts, name):
    pieces = [piece for pieces in sets for piece in pieces]
    size = sum(pieces[0].shape[0] for pieces in sets) // parts
    out = pltpu.HBM((size,) + pieces[0].shape[1:], F32)
    return pl.pallas_call(
        functools.partial(sum_kernel, [len(pieces) for pieces in sets]),
        grid=(1,),
        in_specs=[whole(piece) for piece in pieces],
        out_specs=[whole(out)] * parts,
        out_shape=[out] * parts,
        compiler_params=params(),
        name=name,
    )(*in_hbm(*pieces))


def grad_kernel(plan, scale, own_ref, in_ref, other_ref, *refs):
    *out_refs, sums = refs

    def one(b):
        sums[b] = dot(plan.block(in_ref, 0, b), plan.block(other_ref, 0, b), NT) * scale

    plan.each_block(UNROLL, one)
    split_rows(own_ref[0], sums, *out_refs)


def cut_shape(blocks, factor, groups):
    return pltpu.HBM((blocks, factor.shape[1] // groups, factor.shape[2]), BF16)


def factor_grad(plan, own, arrived, other, factor, scale, groups, name):
    outs = split_shapes(plan.held, factor, groups)
    return pl.pallas_call(
        functools.partial(grad_kernel, plan, scale),
        grid=(1,),
        in_specs=[
            pl.BlockSpec(memory_space=pltpu.SMEM),
            plan.arrived_spec(1, plan.tok),
            plan.arrived_spec(1, plan.tok),
        ],
        out_specs=[whole(out) for out in outs],
        out_shape=outs,
        scratch_shapes=[pltpu.VMEM(factor.shape, F32)],
        compiler_params=params(),
        name=name,
    )(own, arrived, other)


def first_kernel(plan, groups, count, *refs):
    slab_refs, (back_t_ref, gate_ref, up_ref, packed_ref, out_ref, gates, ups) = (
        refs[: groups * count],
        refs[groups * count :],
    )
    b = 0
    for piece in range(count):
        here = slab_refs[piece * groups : (piece + 1) * groups]
        rows = jnp.concatenate([ref[...] for ref in here], axis=0)
        packed = dot(back_t_ref[...], rows, NN).astype(BF16)
        size = packed.shape[1]
        packed_ref[:, b * plan.width : b * plan.width + size] = packed
        for at in range(size // plan.width):
            values = packed[:, at * plan.width : (at + 1) * plan.width]
            plan.put(gates, b, dot(gate_ref[b], values, ((0,), (1,))))
            plan.put(ups, b, dot(up_ref[b], values, ((0,), (1,))))
            b += 1
    plan.store(out_ref, 0, gates)
    plan.store(out_ref, 1, ups)


def first_products(plan, pieces, back_t, right_gate, right_up, half, offset):
    groups = len(pieces[0])
    feats = plan.held * plan.width
    slabs = [slab for piece in pieces for slab in piece]
    sent = plan.sent_shape(2)
    return pl.pallas_call(
        functools.partial(first_kernel, plan, groups, len(pieces)),
        grid=(1,),
        in_specs=[whole(slab) for slab in slabs]
        + [
            pl.BlockSpec((plan.tok, back_t.shape[1]), lambda i: (offset, 0)),
            whole(right_gate),
            whole(right_up),
        ],
        out_specs=[
            pl.BlockSpec((plan.tok, feats), lambda i: (0, 0)),
            plan.sent_spec(2, plan.tok),
        ],
        out_shape=[pltpu.HBM((plan.tok, feats), BF16), sent],
        scratch_shapes=[scratch_for(plan, plan.tok)] * 2,
        compiler_params=params(32),
        name=f"first_products_{half}",
    )(*in_hbm(*slabs, back_t, right_gate, right_up))


ROOT = 0.7978845608028654
CUBE = 0.044715


def gelu_and_slope(x):
    square = x * x
    wave = jnp.tanh(x * (ROOT + (ROOT * CUBE) * square))
    half = 0.5 + 0.5 * wave
    slope = half + x * (1.0 - wave * wave) * (0.5 * ROOT + (1.5 * ROOT * CUBE) * square)
    return x * half, slope


def middle_kernel(
    plan, scale, first, last, own_ref, spread_ref, hidden_grad_ref, gate_ref, up_ref, *refs
):
    if not first:
        before_ref, refs = refs[0], refs[4:]
    hidden_ref, low_ref, high_ref = refs[:3]
    out_refs, (sums, hiddens, gates, ups) = refs[3:-4], refs[-4:]

    def one(b):
        gate_in = plan.block(spread_ref, 0, b)
        up_in = plan.block(spread_ref, 1, b)
        gate_out = dot(gate_ref[b], gate_in, TN).astype(BF16).astype(F32)
        up_out = dot(up_ref[b], up_in, TN).astype(BF16).astype(F32)
        back = plan.block(hidden_grad_ref, 0, b).astype(F32)
        active, slope = gelu_and_slope(gate_out)
        plan.put(hiddens, b, active * up_out)
        gate_back = (back * up_out * slope).astype(BF16)
        up_back = (back * active).astype(BF16)
        plan.put(gates, b, dot(gate_ref[b], gate_back, NN))
        plan.put(ups, b, dot(up_ref[b], up_back, NN))
        for at, values, grads in (b, gate_in, gate_back), (plan.held + b, up_in, up_back):
            total = dot(values, grads, NT)
            if not first:
                total = total + before_ref[at]
            if last:
                sums[at] = total * scale
            else:
                out_refs[0][at] = total

    plan.each_block(UNROLL, one)
    plan.store(hidden_ref, 0, hiddens)
    for part, scratch in enumerate((gates, ups)):
        plan.store_range(low_ref, part, scratch, 0)
        plan.store_range(high_ref, part, scratch, 1)
    if last:
        cut_rows(own_ref[0], sums, out_refs)


def middle(
    plan, full, own, spreads, hidden_grad, left_gate, left_up, scale, groups, half, offset, last,
    before,
):
    step = plan.tok
    first = half == 0
    sums_shape = (2 * plan.held,) + left_gate.shape[1:]
    if last:
        sums = [cut_shape(2 * plan.held, left_gate, groups)] * groups
    else:
        sums = [pltpu.HBM(sums_shape, F32)]
    kept = pl.BlockSpec(memory_space=pl.ANY)
    here = full.sent_spec(1, step, offset)
    outs = pl.pallas_call(
        functools.partial(middle_kernel, plan, scale, first, last),
        grid=(1,),
        in_specs=[
            pl.BlockSpec(memory_space=pltpu.SMEM),
            plan.arrived_spec(2, step),
            full.arrived_spec(1, step, offset),
            whole(left_gate),
            whole(left_up),
        ]
        + ([] if first else [pl.BlockSpec(sums_shape, lambda t: (0, 0, 0)), kept, kept, kept]),
        out_specs=[here] * 3 + [whole(out) for out in sums],
        out_shape=[full.sent_shape(1)] * 3 + sums,
        input_output_aliases={} if first else {6: 0, 7: 1, 8: 2},
        scratch_shapes=[pltpu.VMEM(sums_shape, F32)] + [scratch_for(plan, step)] * 3,
        compiler_params=params(48),
        name=f"middle_{half}",
    )(own, spreads, hidden_grad, *in_hbm(left_gate, left_up, *before))
    return outs[:3], outs[3:]


def spread_blocks(plan, in_ref, at):
    if not plan.direct:
        return in_ref[0, at], in_ref[1, at]
    rows = slice(at * plan.held, (at + 1) * plan.held)
    return tuple(
        jnp.concatenate([in_ref[s, part, rows, :] for s in range(plan.peers)], axis=0)
        for part in range(2)
    )


def spread_form(plan, arrived):
    size = plan.piece // 2
    if plan.direct:
        return in_hbm(arrived.reshape(plan.peers, 2, size, plan.tok))[0]
    array = arrived.reshape(plan.peers, 2, plan.held // 2, plan.held, plan.tok)
    array = array.transpose(1, 2, 0, 3, 4).reshape(2, plan.held // 2, plan.width, plan.tok)
    return in_hbm(array)[0]


def spread_spec(plan, count, offset):
    if plan.direct:
        return pl.BlockSpec(
            (plan.peers, 2, count * plan.held, plan.tok), lambda i: (0, 0, i + offset, 0)
        )
    return pl.BlockSpec((2, count, plan.width, plan.tok), lambda i: (0, i + offset, 0, 0))


def last_kernel(plan, in_ref, back_ref, gate_ref, up_ref, *slab_refs):
    cap = slab_refs[0].shape[0]
    for at in range(gate_ref.shape[0]):
        gate_back, up_back = spread_blocks(plan, in_ref, at)
        back = dot(gate_ref[at], gate_back, NN) + dot(up_ref[at], up_back, NN)
        columns = slice(at * plan.width, (at + 1) * plan.width)
        sent = dot(back_ref[...], back.astype(BF16), NT).astype(BF16)
        for k, ref in enumerate(slab_refs):
            ref[:, columns] = sent[k * cap : (k + 1) * cap]


def last_products(plan, arrived, back, right_gate, right_up, groups, piece, unit):
    start, count = piece
    offset = start % (plan.held // 2 // unit)
    lanes = back.shape[0]
    cap = lanes // groups
    arrived_spec = spread_spec(plan, unit, offset)
    factor_spec = pl.BlockSpec((unit,) + right_gate.shape[1:], lambda i: (start + i, 0, 0))
    size = unit * plan.width
    return pl.pallas_call(
        functools.partial(last_kernel, plan),
        grid=(count,),
        in_specs=[arrived_spec, whole(back), factor_spec, factor_spec],
        out_specs=[pl.BlockSpec((cap, size), lambda i: (0, i))] * groups,
        out_shape=[pltpu.HBM((cap, size * count), BF16)] * groups,
        compiler_params=params(32),
        name=f"last_products_{start}",
    )(*in_hbm(arrived, back, right_gate, right_up))


def right_grads_kernel(plan, scale, halves, own_ref, in_ref, *refs):
    packed_refs, out_refs, sums = refs[:halves], refs[halves:-1], refs[-1]
    count = sums.shape[0] // 2
    for at in range(count):
        columns = slice(at * plan.width, (at + 1) * plan.width)
        values = jnp.concatenate([ref[:, columns] for ref in packed_refs], axis=0)
        for part, spread in enumerate(spread_blocks(plan, in_ref, at)):
            sums[part * count + at] = dot(values, spread, ((0,), (1,))) * scale
    split_rows(own_ref[0], sums, *out_refs)


def right_grads(plan, own, arrived, packed, factor, scale, groups, which):
    count = plan.held // 2
    arrived_spec = spread_spec(plan, count, 0)
    outs = split_shapes(2 * count, factor, groups)
    return pl.pallas_call(
        functools.partial(right_grads_kernel, plan, scale, len(packed)),
        grid=(1,),
        in_specs=[pl.BlockSpec(memory_space=pltpu.SMEM), arrived_spec]
        + [
            pl.BlockSpec((array.shape[0], count * plan.width), lambda i: (0, which))
            for array in packed
        ],
        out_specs=[whole(out) for out in outs],
        out_shape=outs,
        scratch_shapes=[pltpu.VMEM((2 * count,) + factor.shape[1:], F32)],
        compiler_params=params(32),
        name=f"right_grads_{which}",
    )(own, *in_hbm(arrived, *packed))


def natural_kernel(in_ref, out_ref):
    held, _, held_there, tok = out_ref.shape
    for peer in range(in_ref.shape[0]):
        out_ref[:, peer] = in_ref[peer].reshape(held, held_there, tok)


def natural_order(plan, arrived):
    shape = (plan.held, plan.peers, plan.held, plan.tok)
    if not plan.direct:
        array = arrived.reshape(plan.peers, plan.held, plan.held, plan.tok)
        return array.transpose(1, 0, 2, 3).reshape(-1, plan.tok)
    step = plan.peers // 2
    array = pl.pallas_call(
        natural_kernel,
        grid=(plan.peers // step,),
        in_specs=[pl.BlockSpec((step, plan.piece, plan.tok), lambda s: (s, 0, 0))],
        out_specs=pl.BlockSpec((plan.held, step, plan.held, plan.tok), lambda s: (0, s, 0, 0)),
        out_shape=pltpu.HBM(shape, BF16),
        compiler_params=params(),
        name="natural_order",
    )(arrived)
    return array.reshape(-1, plan.tok)


def body(
    earlier,
    mix_weights,
    destinations,
    cotangent,
    right_gate,
    left_gate,
    right_up,
    left_up,
    right_down,
    left_down,
):
    held, width = right_gate.shape[0], right_gate.shape[1]
    feats = earlier.shape[1]
    tok = cotangent.shape[1]
    groups = lax.axis_size("dp")
    peers = lax.axis_size("feat")
    cap = 5 * tok // (4 * groups)
    scale = (tok * groups) ** (-0.5)
    sizes = [3 * tok // 4, tok // 4] if tok % 512 == 0 else [tok]
    offsets = [0, 3][: len(sizes)]
    halves = len(sizes)
    plan = Plan(peers, held, width, tok)
    parts = [Plan(peers, held, width, size) for size in sizes]
    there, unit = pieces_of(
        held // 4, (held - held // 4) // 2, held - held // 4 - (held - held // 4) // 2
    )
    step = unit * width

    def move(array):
        return lax.all_to_all(array, "feat", split_axis=0, concat_axis=0, tiled=True)

    def swap(array):
        return plan.arranged(move(array))

    def after(array, *others):
        return lax.optimization_barrier((array, *others))[0]

    own = lax.axis_index("dp").reshape(1)
    home, back, back_t = routing(destinations, own, groups, tok, cap)
    sent = [mix_and_sort(earlier, mix_weights, home, groups, p, step) for p in there]
    rows = [exchange_rows(slabs, groups) for slabs in sent]

    out_grads = swap(send_cotangent(plan, cotangent))
    out_grads = after(out_grads, rows[0], *sent[1:])
    down_spread_grad = swap(product(plan, out_grads, left_down, NN, "left_back_down"))
    down_spread_grad = after(down_spread_grad, rows[1])
    hidden_grad = product(plan, down_spread_grad, right_down, NN, "right_back_down")
    rows[2] = after(rows[2], hidden_grad)
    hidden_grad = swap(hidden_grad)

    packed, spreads = zip(
        *[
            first_products(parts[h], rows, back_t, right_gate, right_up, h, offsets[h])
            for h in range(halves)
        ]
    )
    arrived, moved = [], hidden_grad
    for h in range(halves):
        moved = move(after(spreads[h], moved))
        arrived.append(parts[h].arranged(moved))
    if halves > 1:
        arrived[0] = after(arrived[0], spreads[1])
    before = ()
    for h in range(halves):
        if h:
            arrived[h] = after(arrived[h], before[0])
        (hidden, low, high), left_sums = middle(
            parts[h], plan, own, arrived[h], hidden_grad, left_gate, left_up, scale, groups, h,
            offsets[h], h == halves - 1, before,
        )
        before = (left_sums[0], hidden, low, high)
    low = spread_form(plan, move(low))
    left_sums = exchange_rows(left_sums, groups)
    high = spread_form(plan, move(after(high, low, *left_sums)))
    grad_left_gate, grad_left_up = sums_of([left_sums], 2, "sum_left")
    half = held // 2
    most = max(half * 5 // 8, 1)
    back_pieces, unit = pieces_of(most, half - most, half - most, most)
    step = unit * width
    factors = (back, right_gate, right_up, groups)
    sent = [last_products(plan, low, *factors, p, unit) for p in back_pieces[:2]]
    rows = [exchange_rows(slabs, groups) for slabs in sent]
    right_low = right_grads(plan, own, after(low, sent), packed, right_gate, scale, groups, 0)
    hidden = swap(after(hidden, high, rows[0], sent[1], right_low, grad_left_gate))
    sent = [last_products(plan, high, *factors, p, unit) for p in back_pieces[2:]]
    rows += [exchange_rows(slabs, groups) for slabs in sent]
    places = (home, step, feats)
    right_low = (right_low[0], swap_rows(right_low[1], 1, groups))
    hidden = after(hidden, rows[1], rows[2], sent[1])
    down_spread = product(plan, hidden, right_down, TN, "right_down")
    down_grad = factor_grad(
        plan, own, after(hidden, down_spread), down_spread_grad, right_down, scale, groups,
        "right_down_grad",
    )
    mixed_grad = unsort(rows[0], back_pieces[0], *places, None)
    mixed_grad = unsort(rows[1], back_pieces[1], *places, mixed_grad)
    right_high = right_grads(
        plan, own, after(high, rows[3], mixed_grad, down_grad), packed, right_gate, scale, groups, 1
    )
    down_spread = swap(down_spread)
    right_high = (right_high[0], swap_rows(right_high[1], 1, groups))
    down_grad = (down_grad[0], swap_rows(down_grad[1], 1, groups))
    down_spread = after(down_spread, right_low[1], right_high[1], down_grad[1])
    result = product(plan, down_spread, left_down, TN, "left_down")
    left_down_grad = factor_grad(
        plan, own, after(down_spread, result), out_grads, left_down, scale, groups,
        "left_down_grad",
    )
    output = natural_order(plan, move(result))
    left_down_grad = [(left_down_grad[0], swap_rows(left_down_grad[1], 1, groups))]
    mixed_grad = unsort(rows[2], back_pieces[2], *places, mixed_grad)
    mixed_grad = unsort(rows[3], back_pieces[3], *places, mixed_grad)
    left_down_grad = after(left_down_grad, mixed_grad)
    right_low, right_high, down_grad = finish(
        [right_low, right_high, down_grad], groups, "halve_right"
    )
    left_down_grad = finish(left_down_grad, groups, "halve_left_down")[0]
    (grad_right_down,) = sums_of([down_grad], 1, "sum_right_down")
    right_low = after(right_low, output, grad_right_down)
    grad_right_gate, grad_right_up = sums_of([right_low, right_high], 2, "sum_right")
    left_down_grad = after(left_down_grad, grad_right_gate)
    (grad_left_down,) = sums_of([left_down_grad], 1, "sum_left_down")
    return (
        output,
        mixed_grad,
        grad_right_gate,
        grad_left_gate,
        grad_right_up,
        grad_left_up,
        grad_right_down,
        grad_left_down,
    )


def solution(mesh):
    return jax.shard_map(
        body,
        mesh=mesh,
        in_specs=(
            P(None, "feat", "dp"),
            P(),
            P(),
            P("feat", "dp"),
            P("feat", None, None),
            P("feat", None, None),
            P("feat", None, None),
            P("feat", None, None),
            P("feat", None, None),
            P("feat", None, None),
        ),
        out_specs=(
            P("feat", "dp"),
            P("feat", "dp"),
            P("feat", "dp", None),
            P("feat", "dp", None),
            P("feat", "dp", None),
            P("feat", "dp", None),
            P("feat", "dp", None),
            P("feat", "dp", None),
        ),
        check_vma=False,
    )
```

```python
import functools
import math

import jax
import jax.numpy as jnp
from jax import lax
from jax.experimental import pallas as pl
from jax.experimental.pallas import tpu as pltpu
from jax.sharding import PartitionSpec as P

F32 = jnp.float32
BF16 = jnp.bfloat16
UNROLL = 16
MIB = 1024 * 1024


def params(limit=16):
    return pltpu.CompilerParams(
        vmem_limit_bytes=limit * MIB, dimension_semantics=("arbitrary",)
    )


def dot(a, b, over):
    return lax.dot_general(a, b, (over, ((), ())), preferred_element_type=F32)


def in_hbm(*arrays):
    return [pltpu.with_memory_space_constraint(array, pltpu.HBM) for array in arrays]


NN = ((1,), (0,))
NT = ((1,), (1,))
TN = ((0,), (0,))


def routing_kernel(sizes, own_ref, dest_ref, home_ref, back_ref, back_t_ref):
    groups, tok, cap, lanes = sizes
    rows, slots = dest_ref.shape
    own = own_ref[0]
    dest = dest_ref[...]
    group = lax.broadcasted_iota(jnp.int32, (rows, slots), 0)
    if groups & (groups - 1) == 0:
        relative = group ^ own
    else:
        relative = jnp.where(group >= own, group - own, group - own + groups)
    before = lax.broadcasted_iota(jnp.int32, (slots, slots), 0) < lax.broadcasted_iota(
        jnp.int32, (slots, slots), 1
    )
    before = jnp.where(before, 1.0, 0.0).astype(BF16)
    lane = lax.broadcasted_iota(jnp.int32, (lanes, slots), 0)

    def place(members):
        return dot(jnp.where(members, 1.0, 0.0).astype(BF16), before, NN).astype(jnp.int32)

    mine = jnp.sum(jnp.where(group == own, dest, 0), axis=0, keepdims=True)
    local = mine - group * tok
    leaving = (local >= 0) & (local < tok) & (group < groups) & (mine >= 0)
    index = jnp.where(leaving, relative * cap + place(leaving) + 1, 0)
    home = jnp.sum(index, axis=0, keepdims=True) - 1
    home_ref[...] = jnp.where(lane == home, 1.0, 0.0).astype(BF16)
    local = dest - own * tok
    arriving = (local >= 0) & (local < tok) & (dest >= 0)
    index = jnp.where(arriving, relative * cap + place(arriving), -1)
    total = jnp.zeros((lanes, slots), jnp.int32)
    for source in range(groups):
        total = total + jnp.where(
            lane == index[source : source + 1], local[source : source + 1] + 1, 0
        )
    row = jnp.sum(total.astype(F32), axis=1, keepdims=True).astype(jnp.int32) - 1
    taken = lax.broadcasted_iota(jnp.int32, (lanes, tok), 1) == row
    taken = jnp.where(taken, 1.0, 0.0)
    back_ref[...] = taken.astype(BF16)
    back_t_ref[...] = taken.T.astype(BF16)


def routing(destinations, own, groups, tok, cap):
    slots = destinations.shape[0] // groups
    lanes = groups * cap
    rows = -(-groups // 16) * 16
    table = destinations.reshape(groups, slots)
    table = jnp.pad(table, ((0, rows - groups), (0, 0)), constant_values=-1)
    return pl.pallas_call(
        functools.partial(routing_kernel, (groups, tok, cap, lanes)),
        grid=(1,),
        in_specs=[
            pl.BlockSpec(memory_space=pltpu.SMEM),
            pl.BlockSpec(table.shape, lambda i: (0, 0)),
        ],
        out_specs=[
            pl.BlockSpec((lanes, slots), lambda i: (0, 0)),
            pl.BlockSpec((lanes, tok), lambda i: (0, 0)),
            pl.BlockSpec((tok, lanes), lambda i: (0, 0)),
        ],
        out_shape=[
            pltpu.HBM((lanes, slots), BF16),
            pltpu.HBM((lanes, tok), BF16),
            pltpu.HBM((tok, lanes), BF16),
        ],
        compiler_params=params(32),
        name="routing",
    )(own, table)


def mix_kernel(weights_ref, earlier_ref, home_ref, *out_refs):
    total = weights_ref[0] * earlier_ref[0].astype(F32)
    for k in range(1, earlier_ref.shape[0]):
        total = total + weights_ref[k] * earlier_ref[k].astype(F32)
    sent = dot(home_ref[...], total.astype(BF16), NT).astype(BF16)
    cap = out_refs[0].shape[0]
    for k, ref in enumerate(out_refs):
        ref[...] = sent[k * cap : (k + 1) * cap]


def pieces_of(*sizes):
    unit = math.gcd(*sizes)
    starts = [sum(sizes[:k]) for k in range(len(sizes))]
    return [(start // unit, size // unit) for start, size in zip(starts, sizes)], unit


def mix_and_sort(earlier, mix_weights, home, groups, piece, step):
    depth, _, slots = earlier.shape
    lanes = home.shape[0]
    cap = lanes // groups
    start, count = piece
    return pl.pallas_call(
        mix_kernel,
        grid=(count,),
        in_specs=[
            pl.BlockSpec(memory_space=pltpu.SMEM),
            pl.BlockSpec((depth, step, slots), lambda i: (0, start + i, 0)),
            pl.BlockSpec((lanes, slots), lambda i: (0, 0)),
        ],
        out_specs=[pl.BlockSpec((cap, step), lambda i: (0, i))] * groups,
        out_shape=[pltpu.HBM((cap, step * count), BF16)] * groups,
        compiler_params=params(),
        name=f"mix_and_sort_{start}",
    )(mix_weights, *in_hbm(earlier, home))


def partner(own, k, count):
    return own ^ k if count & (count - 1) == 0 else lax.rem(own + k, count)


def exchange(arrays, axis, count):
    received = [arrays[0]]
    for k in range(1, count):
        if count & (count - 1) == 0:
            pairs = [(i, i ^ k) for i in range(count)]
        else:
            pairs = [(i, (i + k) % count) for i in range(count)]
        received.append(lax.ppermute(arrays[k], axis, pairs))
    return received


def exchange_rows(slabs, groups):
    return exchange(slabs, "dp", groups)


def unsort_kernel(groups, home_ref, *refs):
    in_refs, out_ref = refs[:groups], refs[-1]
    rows = jnp.concatenate([ref[...] for ref in in_refs], axis=0)
    out_ref[...] = dot(rows, home_ref[...], TN).astype(BF16)


def unsort(slabs, piece, home, step, feats, partial):
    lanes, slots = home.shape
    cap = slabs[0].shape[0]
    groups = len(slabs)
    start, count = piece
    more = [] if partial is None else [partial]
    return pl.pallas_call(
        functools.partial(unsort_kernel, groups),
        grid=(count,),
        in_specs=[pl.BlockSpec((lanes, slots), lambda i: (0, 0))]
        + [pl.BlockSpec((cap, step), lambda i: (0, i))] * groups
        + [pl.BlockSpec(memory_space=pl.ANY)] * len(more),
        out_specs=pl.BlockSpec((step, slots), lambda i: (start + i, 0)),
        out_shape=pltpu.HBM((feats, slots), BF16),
        input_output_aliases={1 + groups: 0} if more else {},
        compiler_params=params(),
        name=f"unsort_{start}",
    )(*in_hbm(home, *slabs, *more))


class Plan:
    def __init__(self, peers, held, width, tok):
        self.peers, self.held, self.width, self.tok = peers, held, width, tok
        self.piece = held * held
        self.direct = held % 16 == 0

    def sent_shape(self, parts):
        return pltpu.HBM((self.peers, parts * self.piece, self.tok), BF16)

    def sent_spec(self, parts, step, offset=0):
        return pl.BlockSpec((self.peers, parts * self.piece, step), lambda t: (0, 0, t + offset))

    def arranged(self, array):
        if self.direct:
            return array
        parts = array.shape[1] // self.piece
        array = array.reshape(self.peers, parts, self.held, self.held, self.tok)
        array = array.transpose(1, 2, 0, 3, 4)
        return array.reshape(parts * self.held, self.width, self.tok)

    def arrived_spec(self, parts, step, offset=0):
        if self.direct:
            return self.sent_spec(parts, step, offset)
        return pl.BlockSpec((parts * self.held, self.width, step), lambda t: (0, 0, t + offset))

    def each_block(self, unroll, step):
        def some(outer, carry):
            for inner in range(unroll):
                step(outer * unroll + inner)
            return carry

        unroll = min(unroll, self.held)
        lax.fori_loop(0, self.held // unroll, some, 0)

    def block(self, ref, part, b):
        if not self.direct:
            return ref[part * self.held + b]
        rows = pl.ds(pl.multiple_of(part * self.piece + b * self.held, self.held), self.held)
        return jnp.concatenate([ref[s, rows, :] for s in range(self.peers)], axis=0)

    def put(self, scratch, b, value):
        for at in range(scratch.shape[0]):
            scratch[at, pl.ds(b, self.width, stride=self.held), :] = value[
                :, at * 128 : (at + 1) * 128
            ]

    def store_range(self, out_ref, part, scratch, which):
        size = self.piece // 2
        rows = slice(part * size, (part + 1) * size)
        for at in range(scratch.shape[0]):
            for peer in range(self.peers):
                start = peer * self.piece + which * size
                out_ref[peer, rows, at * 128 : (at + 1) * 128] = scratch[
                    at, start : start + size
                ].astype(BF16)

    def store(self, out_ref, part, scratch):
        rows = slice(part * self.piece, (part + 1) * self.piece)
        for at in range(scratch.shape[0]):
            out_ref[:, rows, at * 128 : (at + 1) * 128] = (
                scratch[at].reshape(self.peers, self.piece, 128).astype(BF16)
            )


def step_of(tok):
    return 256 if tok % 256 == 0 else 128


def scratch_for(plan, step):
    return pltpu.VMEM((step // 128, plan.width * plan.held, 128), F32)


def whole(array):
    return pl.BlockSpec(array.shape, lambda t: (0,) * len(array.shape))


def clear_at_first(*refs):
    @pl.when(pl.program_id(0) == 0)
    def _():
        for ref in refs:
            ref[...] = jnp.zeros_like(ref)


def cotangent_kernel(plan, in_ref, out_ref, scratch):
    def one(b):
        rows = pl.ds(pl.multiple_of(b * plan.width, plan.width), plan.width)
        plan.put(scratch, b, in_ref[rows, :].astype(F32))

    plan.each_block(UNROLL, one)
    plan.store(out_ref, 0, scratch)


def send_cotangent(plan, cotangent):
    step = step_of(plan.tok)
    return pl.pallas_call(
        functools.partial(cotangent_kernel, plan),
        grid=(plan.tok // step,),
        in_specs=[pl.BlockSpec((plan.width * plan.held, step), lambda t: (0, t))],
        out_specs=plan.sent_spec(1, step),
        out_shape=plan.sent_shape(1),
        scratch_shapes=[scratch_for(plan, step)],
        compiler_params=params(),
        name="send_cotangent",
    )(*in_hbm(cotangent))


def product_kernel(plan, over, in_ref, factor_ref, out_ref, scratch):
    def one(b):
        plan.put(scratch, b, dot(factor_ref[b], plan.block(in_ref, 0, b), over))

    plan.each_block(UNROLL, one)
    plan.store(out_ref, 0, scratch)


def product(plan, arrived, factor, over, name):
    step = step_of(plan.tok)
    return pl.pallas_call(
        functools.partial(product_kernel, plan, over),
        grid=(plan.tok // step,),
        in_specs=[plan.arrived_spec(1, step), whole(factor)],
        out_specs=plan.sent_spec(1, step),
        out_shape=plan.sent_shape(1),
        scratch_shapes=[scratch_for(plan, step)],
        compiler_params=params(),
        name=name,
    )(arrived, factor)


def cut_rows(own, array, out_refs):
    groups = len(out_refs)
    size = array.shape[1] // groups
    for k, ref in enumerate(out_refs):
        target = partner(own, k, groups)
        ref[...] = array[:, pl.ds(pl.multiple_of(target * size, size), size), :].astype(BF16)


def split_rows(own, array, keep_ref, send_ref):
    groups = 2 * keep_ref.shape[0]
    size = array.shape[1] // groups
    for k in range(groups):
        start = pl.multiple_of((own ^ k) * size, size)
        ref = send_ref if k % 2 else keep_ref
        ref[k // 2] = array[:, pl.ds(start, size), :].astype(BF16)


def split_shapes(blocks, factor, groups):
    shape = (groups // 2, blocks, factor.shape[1] // groups, factor.shape[2])
    return [pltpu.HBM(shape, BF16)] * 2


def halve_kernel(count, *refs):
    for at in range(count):
        total = refs[2 * at][...].astype(F32) + refs[2 * at + 1][...].astype(F32)
        outs = refs[2 * (count + at) : 2 * (count + at) + 2]
        for k in range(total.shape[0]):
            ref = outs[k % 2]
            ref[k // 2] = total[k].astype(ref.dtype)


def halve(pairs, name):
    shapes = []
    for keep, _ in pairs:
        shape = (keep.shape[0] // 2,) + keep.shape[1:]
        shapes += [pltpu.HBM(shape, F32), pltpu.HBM(shape, BF16)]
    arrays = [array for pair in pairs for array in pair]
    outs = pl.pallas_call(
        functools.partial(halve_kernel, len(pairs)),
        grid=(1,),
        in_specs=[whole(array) for array in arrays],
        out_specs=[whole(shape) for shape in shapes],
        out_shape=shapes,
        compiler_params=params(),
        name=name,
    )(*in_hbm(*arrays))
    return [(outs[2 * at], outs[2 * at + 1]) for at in range(len(pairs))]


def swap_rows(array, bit, groups):
    return lax.ppermute(array, "dp", [(i, i ^ bit) for i in range(groups)])


def finish(pairs, groups, name):
    bit = 2
    while bit < groups:
        split = halve(pairs, f"{name}_{bit}")
        pairs = [(keep, swap_rows(send, bit, groups)) for keep, send in split]
        bit *= 2
    return [[array[0] for array in pair] for pair in pairs]


def sum_kernel(counts, *refs):
    in_refs, out_refs = refs[: sum(counts)], refs[sum(counts) :]
    at = 0
    done = [0] * len(out_refs)
    for count in counts:
        total = in_refs[at][...].astype(F32)
        for ref in in_refs[at + 1 : at + count]:
            total = total + ref[...].astype(F32)
        at += count
        size = total.shape[0] // len(out_refs)
        for part, ref in enumerate(out_refs):
            ref[done[part] : done[part] + size] = total[part * size : (part + 1) * size]
            done[part] += size


def sums_of(sets, parts, name):
    pieces = [piece for pieces in sets for piece in pieces]
    size = sum(pieces[0].shape[0] for pieces in sets) // parts
    out = pltpu.HBM((size,) + pieces[0].shape[1:], F32)
    return pl.pallas_call(
        functools.partial(sum_kernel, [len(pieces) for pieces in sets]),
        grid=(1,),
        in_specs=[whole(piece) for piece in pieces],
        out_specs=[whole(out)] * parts,
        out_shape=[out] * parts,
        compiler_params=params(),
        name=name,
    )(*in_hbm(*pieces))


def grad_kernel(plan, scale, own_ref, in_ref, other_ref, *refs):
    *out_refs, sums = refs

    def one(b):
        sums[b] = dot(plan.block(in_ref, 0, b), plan.block(other_ref, 0, b), NT) * scale

    plan.each_block(UNROLL, one)
    split_rows(own_ref[0], sums, *out_refs)


def cut_shape(blocks, factor, groups):
    return pltpu.HBM((blocks, factor.shape[1] // groups, factor.shape[2]), BF16)


def factor_grad(plan, own, arrived, other, factor, scale, groups, name):
    outs = split_shapes(plan.held, factor, groups)
    return pl.pallas_call(
        functools.partial(grad_kernel, plan, scale),
        grid=(1,),
        in_specs=[
            pl.BlockSpec(memory_space=pltpu.SMEM),
            plan.arrived_spec(1, plan.tok),
            plan.arrived_spec(1, plan.tok),
        ],
        out_specs=[whole(out) for out in outs],
        out_shape=outs,
        scratch_shapes=[pltpu.VMEM(factor.shape, F32)],
        compiler_params=params(),
        name=name,
    )(own, arrived, other)


def first_kernel(plan, groups, count, *refs):
    slab_refs, (back_t_ref, gate_ref, up_ref, packed_ref, out_ref, gates, ups) = (
        refs[: groups * count],
        refs[groups * count :],
    )
    b = 0
    for piece in range(count):
        here = slab_refs[piece * groups : (piece + 1) * groups]
        rows = jnp.concatenate([ref[...] for ref in here], axis=0)
        packed = dot(back_t_ref[...], rows, NN).astype(BF16)
        size = packed.shape[1]
        packed_ref[:, b * plan.width : b * plan.width + size] = packed
        for at in range(size // plan.width):
            values = packed[:, at * plan.width : (at + 1) * plan.width]
            plan.put(gates, b, dot(gate_ref[b], values, ((0,), (1,))))
            plan.put(ups, b, dot(up_ref[b], values, ((0,), (1,))))
            b += 1
    plan.store(out_ref, 0, gates)
    plan.store(out_ref, 1, ups)


def first_products(plan, pieces, back_t, right_gate, right_up, half, offset):
    groups = len(pieces[0])
    feats = plan.held * plan.width
    slabs = [slab for piece in pieces for slab in piece]
    sent = plan.sent_shape(2)
    return pl.pallas_call(
        functools.partial(first_kernel, plan, groups, len(pieces)),
        grid=(1,),
        in_specs=[whole(slab) for slab in slabs]
        + [
            pl.BlockSpec((plan.tok, back_t.shape[1]), lambda i: (offset, 0)),
            whole(right_gate),
            whole(right_up),
        ],
        out_specs=[
            pl.BlockSpec((plan.tok, feats), lambda i: (0, 0)),
            plan.sent_spec(2, plan.tok),
        ],
        out_shape=[pltpu.HBM((plan.tok, feats), BF16), sent],
        scratch_shapes=[scratch_for(plan, plan.tok)] * 2,
        compiler_params=params(32),
        name=f"first_products_{half}",
    )(*in_hbm(*slabs, back_t, right_gate, right_up))


ROOT = 0.7978845608028654
CUBE = 0.044715


def gelu_and_slope(x):
    square = x * x
    wave = jnp.tanh(x * (ROOT + (ROOT * CUBE) * square))
    half = 0.5 + 0.5 * wave
    slope = half + x * (1.0 - wave * wave) * (0.5 * ROOT + (1.5 * ROOT * CUBE) * square)
    return x * half, slope


def middle_kernel(
    plan, scale, first, last, own_ref, spread_ref, hidden_grad_ref, gate_ref, up_ref, *refs
):
    if not first:
        before_ref, refs = refs[0], refs[4:]
    hidden_ref, low_ref, high_ref = refs[:3]
    out_refs, (sums, hiddens, gates, ups) = refs[3:-4], refs[-4:]

    def one(b):
        gate_in = plan.block(spread_ref, 0, b)
        up_in = plan.block(spread_ref, 1, b)
        gate_out = dot(gate_ref[b], gate_in, TN).astype(BF16).astype(F32)
        up_out = dot(up_ref[b], up_in, TN).astype(BF16).astype(F32)
        back = plan.block(hidden_grad_ref, 0, b).astype(F32)
        active, slope = gelu_and_slope(gate_out)
        plan.put(hiddens, b, active * up_out)
        gate_back = (back * up_out * slope).astype(BF16)
        up_back = (back * active).astype(BF16)
        plan.put(gates, b, dot(gate_ref[b], gate_back, NN))
        plan.put(ups, b, dot(up_ref[b], up_back, NN))
        for at, values, grads in (b, gate_in, gate_back), (plan.held + b, up_in, up_back):
            total = dot(values, grads, NT)
            if not first:
                total = total + before_ref[at]
            if last:
                sums[at] = total * scale
            else:
                out_refs[0][at] = total

    plan.each_block(UNROLL, one)
    plan.store(hidden_ref, 0, hiddens)
    for part, scratch in enumerate((gates, ups)):
        plan.store_range(low_ref, part, scratch, 0)
        plan.store_range(high_ref, part, scratch, 1)
    if last:
        cut_rows(own_ref[0], sums, out_refs)


def middle(
    plan, full, own, spreads, hidden_grad, left_gate, left_up, scale, groups, half, offset, last,
    before,
):
    step = plan.tok
    first = half == 0
    sums_shape = (2 * plan.held,) + left_gate.shape[1:]
    if last:
        sums = [cut_shape(2 * plan.held, left_gate, groups)] * groups
    else:
        sums = [pltpu.HBM(sums_shape, F32)]
    kept = pl.BlockSpec(memory_space=pl.ANY)
    here = full.sent_spec(1, step, offset)
    outs = pl.pallas_call(
        functools.partial(middle_kernel, plan, scale, first, last),
        grid=(1,),
        in_specs=[
            pl.BlockSpec(memory_space=pltpu.SMEM),
            plan.arrived_spec(2, step),
            full.arrived_spec(1, step, offset),
            whole(left_gate),
            whole(left_up),
        ]
        + ([] if first else [pl.BlockSpec(sums_shape, lambda t: (0, 0, 0)), kept, kept, kept]),
        out_specs=[here] * 3 + [whole(out) for out in sums],
        out_shape=[full.sent_shape(1)] * 3 + sums,
        input_output_aliases={} if first else {6: 0, 7: 1, 8: 2},
        scratch_shapes=[pltpu.VMEM(sums_shape, F32)] + [scratch_for(plan, step)] * 3,
        compiler_params=params(48),
        name=f"middle_{half}",
    )(own, spreads, hidden_grad, *in_hbm(left_gate, left_up, *before))
    return outs[:3], outs[3:]


def spread_blocks(plan, in_ref, at):
    if not plan.direct:
        return in_ref[0, at], in_ref[1, at]
    rows = slice(at * plan.held, (at + 1) * plan.held)
    return tuple(
        jnp.concatenate([in_ref[s, part, rows, :] for s in range(plan.peers)], axis=0)
        for part in range(2)
    )


def spread_form(plan, arrived):
    size = plan.piece // 2
    if plan.direct:
        return in_hbm(arrived.reshape(plan.peers, 2, size, plan.tok))[0]
    array = arrived.reshape(plan.peers, 2, plan.held // 2, plan.held, plan.tok)
    array = array.transpose(1, 2, 0, 3, 4).reshape(2, plan.held // 2, plan.width, plan.tok)
    return in_hbm(array)[0]


def spread_spec(plan, count, offset):
    if plan.direct:
        return pl.BlockSpec(
            (plan.peers, 2, count * plan.held, plan.tok), lambda i: (0, 0, i + offset, 0)
        )
    return pl.BlockSpec((2, count, plan.width, plan.tok), lambda i: (0, i + offset, 0, 0))


def last_kernel(plan, in_ref, back_ref, gate_ref, up_ref, *slab_refs):
    cap = slab_refs[0].shape[0]
    for at in range(gate_ref.shape[0]):
        gate_back, up_back = spread_blocks(plan, in_ref, at)
        back = dot(gate_ref[at], gate_back, NN) + dot(up_ref[at], up_back, NN)
        columns = slice(at * plan.width, (at + 1) * plan.width)
        sent = dot(back_ref[...], back.astype(BF16), NT).astype(BF16)
        for k, ref in enumerate(slab_refs):
            ref[:, columns] = sent[k * cap : (k + 1) * cap]


def last_products(plan, arrived, back, right_gate, right_up, groups, piece, unit):
    start, count = piece
    offset = start % (plan.held // 2 // unit)
    lanes = back.shape[0]
    cap = lanes // groups
    arrived_spec = spread_spec(plan, unit, offset)
    factor_spec = pl.BlockSpec((unit,) + right_gate.shape[1:], lambda i: (start + i, 0, 0))
    size = unit * plan.width
    return pl.pallas_call(
        functools.partial(last_kernel, plan),
        grid=(count,),
        in_specs=[arrived_spec, whole(back), factor_spec, factor_spec],
        out_specs=[pl.BlockSpec((cap, size), lambda i: (0, i))] * groups,
        out_shape=[pltpu.HBM((cap, size * count), BF16)] * groups,
        compiler_params=params(32),
        name=f"last_products_{start}",
    )(*in_hbm(arrived, back, right_gate, right_up))


def right_grads_kernel(plan, scale, halves, own_ref, in_ref, *refs):
    packed_refs, out_refs, sums = refs[:halves], refs[halves:-1], refs[-1]
    count = sums.shape[0] // 2
    for at in range(count):
        columns = slice(at * plan.width, (at + 1) * plan.width)
        values = jnp.concatenate([ref[:, columns] for ref in packed_refs], axis=0)
        for part, spread in enumerate(spread_blocks(plan, in_ref, at)):
            sums[part * count + at] = dot(values, spread, ((0,), (1,))) * scale
    split_rows(own_ref[0], sums, *out_refs)


def right_grads(plan, own, arrived, packed, factor, scale, groups, which):
    count = plan.held // 2
    arrived_spec = spread_spec(plan, count, 0)
    outs = split_shapes(2 * count, factor, groups)
    return pl.pallas_call(
        functools.partial(right_grads_kernel, plan, scale, len(packed)),
        grid=(1,),
        in_specs=[pl.BlockSpec(memory_space=pltpu.SMEM), arrived_spec]
        + [
            pl.BlockSpec((array.shape[0], count * plan.width), lambda i: (0, which))
            for array in packed
        ],
        out_specs=[whole(out) for out in outs],
        out_shape=outs,
        scratch_shapes=[pltpu.VMEM((2 * count,) + factor.shape[1:], F32)],
        compiler_params=params(32),
        name=f"right_grads_{which}",
    )(own, *in_hbm(arrived, *packed))


def natural_kernel(in_ref, out_ref):
    held, _, held_there, tok = out_ref.shape
    for peer in range(in_ref.shape[0]):
        out_ref[:, peer] = in_ref[peer].reshape(held, held_there, tok)


def natural_order(plan, arrived):
    shape = (plan.held, plan.peers, plan.held, plan.tok)
    if not plan.direct:
        array = arrived.reshape(plan.peers, plan.held, plan.held, plan.tok)
        return array.transpose(1, 0, 2, 3).reshape(-1, plan.tok)
    step = plan.peers // 2
    array = pl.pallas_call(
        natural_kernel,
        grid=(plan.peers // step,),
        in_specs=[pl.BlockSpec((step, plan.piece, plan.tok), lambda s: (s, 0, 0))],
        out_specs=pl.BlockSpec((plan.held, step, plan.held, plan.tok), lambda s: (0, s, 0, 0)),
        out_shape=pltpu.HBM(shape, BF16),
        compiler_params=params(),
        name="natural_order",
    )(arrived)
    return array.reshape(-1, plan.tok)


def body(
    earlier,
    mix_weights,
    destinations,
    cotangent,
    right_gate,
    left_gate,
    right_up,
    left_up,
    right_down,
    left_down,
):
    held, width = right_gate.shape[0], right_gate.shape[1]
    feats = earlier.shape[1]
    tok = cotangent.shape[1]
    groups = lax.axis_size("dp")
    peers = lax.axis_size("feat")
    cap = 5 * tok // (4 * groups)
    scale = (tok * groups) ** (-0.5)
    sizes = [3 * tok // 4, tok // 4] if tok % 512 == 0 else [tok]
    offsets = [0, 3][: len(sizes)]
    halves = len(sizes)
    plan = Plan(peers, held, width, tok)
    parts = [Plan(peers, held, width, size) for size in sizes]
    there, unit = pieces_of(
        held // 4, (held - held // 4) // 2, held - held // 4 - (held - held // 4) // 2
    )
    step = unit * width

    def move(array):
        return lax.all_to_all(array, "feat", split_axis=0, concat_axis=0, tiled=True)

    def swap(array):
        return plan.arranged(move(array))

    def after(array, *others):
        return lax.optimization_barrier((array, *others))[0]

    own = lax.axis_index("dp").reshape(1)
    home, back, back_t = routing(destinations, own, groups, tok, cap)
    sent = [mix_and_sort(earlier, mix_weights, home, groups, p, step) for p in there]
    rows = [exchange_rows(slabs, groups) for slabs in sent]

    out_grads = swap(send_cotangent(plan, cotangent))
    out_grads = after(out_grads, rows[0], *sent[1:])
    down_spread_grad = swap(product(plan, out_grads, left_down, NN, "left_back_down"))
    down_spread_grad = after(down_spread_grad, rows[1])
    hidden_grad = product(plan, down_spread_grad, right_down, NN, "right_back_down")
    rows[2] = after(rows[2], hidden_grad)
    hidden_grad = swap(hidden_grad)

    packed, spreads = zip(
        *[
            first_products(parts[h], rows, back_t, right_gate, right_up, h, offsets[h])
            for h in range(halves)
        ]
    )
    arrived, moved = [], hidden_grad
    for h in range(halves):
        moved = move(after(spreads[h], moved))
        arrived.append(parts[h].arranged(moved))
    if halves > 1:
        arrived[0] = after(arrived[0], spreads[1])
    before = ()
    for h in range(halves):
        if h:
            arrived[h] = after(arrived[h], before[0])
        (hidden, low, high), left_sums = middle(
            parts[h], plan, own, arrived[h], hidden_grad, left_gate, left_up, scale, groups, h,
            offsets[h], h == halves - 1, before,
        )
        before = (left_sums[0], hidden, low, high)
    low = spread_form(plan, move(low))
    left_sums = exchange_rows(left_sums, groups)
    high = spread_form(plan, move(after(high, low, *left_sums)))
    grad_left_gate, grad_left_up = sums_of([left_sums], 2, "sum_left")
    half = held // 2
    most = max(half * 5 // 8, 1)
    back_pieces, unit = pieces_of(most, half - most, half - most, most)
    step = unit * width
    factors = (back, right_gate, right_up, groups)
    sent = [last_products(plan, low, *factors, p, unit) for p in back_pieces[:2]]
    rows = [exchange_rows(slabs, groups) for slabs in sent]
    right_low = right_grads(plan, own, after(low, sent), packed, right_gate, scale, groups, 0)
    hidden = swap(after(hidden, high, rows[0], sent[1], right_low, grad_left_gate))
    sent = [last_products(plan, high, *factors, p, unit) for p in back_pieces[2:]]
    rows += [exchange_rows(slabs, groups) for slabs in sent]
    places = (home, step, feats)
    right_low = (right_low[0], swap_rows(right_low[1], 1, groups))
    hidden = after(hidden, rows[1], rows[2], sent[1])
    down_spread = product(plan, hidden, right_down, TN, "right_down")
    down_grad = factor_grad(
        plan, own, after(hidden, down_spread), down_spread_grad, right_down, scale, groups,
        "right_down_grad",
    )
    mixed_grad = unsort(rows[0], back_pieces[0], *places, None)
    mixed_grad = unsort(rows[1], back_pieces[1], *places, mixed_grad)
    right_high = right_grads(
        plan, own, after(high, rows[3], mixed_grad, down_grad), packed, right_gate, scale, groups, 1
    )
    down_spread = swap(down_spread)
    right_high = (right_high[0], swap_rows(right_high[1], 1, groups))
    down_grad = (down_grad[0], swap_rows(down_grad[1], 1, groups))
    mixed_grad = unsort(rows[2], back_pieces[2], *places, mixed_grad)
    down_spread = after(down_spread, right_low[1], right_high[1], down_grad[1], mixed_grad)
    result = product(plan, down_spread, left_down, TN, "left_down")
    left_down_grad = factor_grad(
        plan, own, after(down_spread, result), out_grads, left_down, scale, groups,
        "left_down_grad",
    )
    output = natural_order(plan, move(result))
    left_down_grad = [(left_down_grad[0], swap_rows(left_down_grad[1], 1, groups))]
    mixed_grad = unsort(rows[3], back_pieces[3], *places, mixed_grad)
    left_down_grad = after(left_down_grad, mixed_grad)
    right_low, right_high, down_grad = finish(
        [right_low, right_high, down_grad], groups, "halve_right"
    )
    left_down_grad = finish(left_down_grad, groups, "halve_left_down")[0]
    (grad_right_down,) = sums_of([down_grad], 1, "sum_right_down")
    right_low = after(right_low, output, grad_right_down)
    grad_right_gate, grad_right_up = sums_of([right_low, right_high], 2, "sum_right")
    left_down_grad = after(left_down_grad, grad_right_gate)
    (grad_left_down,) = sums_of([left_down_grad], 1, "sum_left_down")
    return (
        output,
        mixed_grad,
        grad_right_gate,
        grad_left_gate,
        grad_right_up,
        grad_left_up,
        grad_right_down,
        grad_left_down,
    )


def solution(mesh):
    return jax.shard_map(
        body,
        mesh=mesh,
        in_specs=(
            P(None, "feat", "dp"),
            P(),
            P(),
            P("feat", "dp"),
            P("feat", None, None),
            P("feat", None, None),
            P("feat", None, None),
            P("feat", None, None),
            P("feat", None, None),
            P("feat", None, None),
        ),
        out_specs=(
            P("feat", "dp"),
            P("feat", "dp"),
            P("feat", "dp", None),
            P("feat", "dp", None),
            P("feat", "dp", None),
            P("feat", "dp", None),
            P("feat", "dp", None),
            P("feat", "dp", None),
        ),
        check_vma=False,
    )
```
